32 devices in a mesh: group: 2 (over y), space: 16 (over z, x, core).
Axes of the slice: x: 2, y: 2, z: 4, core: 2. Of those that a mesh axis runs over, the one named last changes fastest.
Arguments:
- flow_field: float32 [64, 32, 128, 128], P(('group', 'space')), parts along dimension 0, may hold values from -6 to 6
- cotangent: float32 [64, 32, 128, 128], P(('group', 'space')), parts along dimension 0, may hold values from -6 to 6
- spec_weight: float32 [512, 2, 32, 1024], P('space'), may hold values from -0.75 to 0.75
- point_weight: float32 [32, 32], replicated, may hold values from -1 to 1
- pointwise_bias: float32 [32], replicated, may hold values from -3 to 3
Outputs:
- output: float32 [64, 32, 128, 128], P(('group', 'space')), parts along dimension 0
- grad_field: float32 [64, 32, 128, 128], P(('group', 'space')), parts along dimension 0
- grad_spec: float32 [1024, 2, 32, 1024], P(('group', 'space')), parts along dimension 0
- grad_point: float32 [64, 32], P('group'), parts along dimension 0
- grad_bias: float32 [64], P('group'), parts along dimension 0
The draws below stay inside these ranges and needn't reach their ends.
There are 2 independent parts, one for each index of `group`. The reference program is written for one: setup_inputs(seed, part) draws one part's arguments, and reference() takes and returns one part's arrays. A program takes and returns all parts, laid end to end along the dimension named above; an argument that names none is the same for every part. Nothing has to cross between parts.
All inputs are finite; a program needn't handle non-finite values.
Results may differ from the reference program's by a relative error of at most 0.00012.
Values sent between devices are 32-bit elements; how exact they have to be, the bound alone decides.
No kernel may reach another device: no remote copies, remote signals or barrier semaphores. Data moves between devices by JAX's collectives and lax.ppermute only.
A program may use at most 256 MiB of HBM per device.

```python
import math
import jax
import jax.numpy as jnp
from jax import lax

C = 32
MODES = 16
NY = 128
NZ = 128
NX = 32
PAIRS = 512


def steps_of(rng, extent, pieces, smallest, top_value):
    def one(position, blocks):
        steps = jax.random.uniform(jax.random.fold_in(jax.random.fold_in(rng, 6), position), (blocks,), jnp.float32, smallest / len(pieces), top_value / len(pieces))
        return jnp.repeat(jnp.exp(steps), extent[position] // blocks).reshape((-1,) + (1,) * (len(extent) - position - 1))

    loudness = one(*pieces[0])
    for cut in pieces[1:]:
        loudness = loudness * one(*cut)
    return loudness


def noise(rng, extent, scale, reach, split=(), kind=jnp.bfloat16):
    factor_of = steps_of(rng, extent, split, -0.22, 0.18) if split else 1.0
    drawn = jax.random.normal(rng, extent, jnp.float32) * scale * factor_of
    return jnp.minimum(jnp.maximum(drawn, -reach), reach).astype(kind)


def setup_inputs(seed: int = 0, part: int = 0) -> dict:
    keys = jax.random.split(jax.random.key(seed), 6)
    own_keys = jax.random.split(jax.random.fold_in(keys[5], part), 6)
    flow_field = noise(own_keys[0], (NX, C, NY, NZ), 1.0, 6.0, ((0, 16),), jnp.float32)
    cotangent = noise(own_keys[1], (NX, C, NY, NZ), 1.0, 6.0, ((0, 16),), jnp.float32)
    spec_weight = noise(keys[2], (PAIRS, 2, C, 2 * MODES * C), (2 * C) ** -0.5, 0.75, ((0, 16),), jnp.float32)
    point_weight = noise(keys[3], (C, C), C ** -0.5, 1.0, (), jnp.float32)
    pointwise_bias = noise(keys[4], (C,), 0.5, 3.0, (), jnp.float32)
    return {"flow_field": flow_field, "cotangent": cotangent, "spec_weight": spec_weight, "point_weight": point_weight, "pointwise_bias": pointwise_bias}


highest = lax.Precision.HIGHEST

def contract(form, left, right):
    return jnp.einsum(form, left, right, precision=highest)

def phase_table(positions, wavenums, length):
    phases = positions[:, None] * wavenums[None, :] % length
    angles = phases.astype(jnp.float32) * (2.0 * math.pi / length)
    return (jnp.cos(angles), jnp.sin(angles))

def signed_modes(mode_count):
    indices = jnp.arange(mode_count, dtype=jnp.int32)
    return jnp.where(indices < mode_count // 2, indices, indices - mode_count)

def yz_forward(values, z_cos, z_sin, y_cos, y_sin):
    cosine_part = contract('xcyz,zk->xcyk', values, z_cos)
    sine_part = -contract('xcyz,zk->xcyk', values, z_sin)
    real_part = contract('xcyk,yj->xjkc', cosine_part, y_cos) + contract('xcyk,yj->xjkc', sine_part, y_sin)
    imag_part = contract('xcyk,yj->xjkc', sine_part, y_cos) - contract('xcyk,yj->xjkc', cosine_part, y_sin)
    row_count, ky_count, kz_count, channels = real_part.shape
    shaped = (row_count, ky_count * kz_count, channels)
    return jnp.stack([real_part.reshape(shaped), imag_part.reshape(shaped)], axis=2)

def yz_inverse(spectrum, z_cos, z_sin, y_cos, y_sin, kz_weights):
    row_count, pair_count, _, channels = spectrum.shape
    kz_count = z_cos.shape[1]
    ky_count = pair_count // kz_count
    part_real = spectrum[:, :, 0].reshape(row_count, ky_count, kz_count, channels)
    part_imag = spectrum[:, :, 1].reshape(row_count, ky_count, kz_count, channels)
    back_real = contract('xjkc,yj->xcyk', part_real, y_cos) - contract('xjkc,yj->xcyk', part_imag, y_sin)
    back_imag = contract('xjkc,yj->xcyk', part_real, y_sin) + contract('xjkc,yj->xcyk', part_imag, y_cos)
    return contract('xcyk,zk->xcyz', back_real, z_cos * kz_weights[None, :]) - contract('xcyk,zk->xcyz', back_imag, z_sin * kz_weights[None, :])

def x_forward(spectrum, x_cos, x_sin):
    part_real = spectrum[:, :, 0]
    part_imag = spectrum[:, :, 1]
    mode_real = contract('xpc,xq->pqc', part_real, x_cos) + contract('xpc,xq->pqc', part_imag, x_sin)
    mode_imag = contract('xpc,xq->pqc', part_imag, x_cos) - contract('xpc,xq->pqc', part_real, x_sin)
    return jnp.stack([mode_real, mode_imag], axis=2)

def x_inverse(mode_data, x_cos, x_sin):
    mode_real = mode_data[:, :, 0]
    mode_imag = mode_data[:, :, 1]
    part_real = contract('pqc,xq->xpc', mode_real, x_cos) - contract('pqc,xq->xpc', mode_imag, x_sin)
    part_imag = contract('pqc,xq->xpc', mode_real, x_sin) + contract('pqc,xq->xpc', mode_imag, x_cos)
    return jnp.stack([part_real, part_imag], axis=2)

def mode_mix(mode_data, weights):
    pair_total, kx_total, _, channels = mode_data.shape
    shaped = weights.reshape(pair_total, 2, channels, kx_total, channels)
    in_real = mode_data[:, :, 0]
    in_imag = mode_data[:, :, 1]
    out_real = contract('pqi,piqo->pqo', in_real, shaped[:, 0]) - contract('pqi,piqo->pqo', in_imag, shaped[:, 1])
    out_imag = contract('pqi,piqo->pqo', in_imag, shaped[:, 0]) + contract('pqi,piqo->pqo', in_real, shaped[:, 1])
    return jnp.stack([out_real, out_imag], axis=2)

def reference(flow_field, cotangent, spec_weight, point_weight, pointwise_bias):
    kz_modes = jnp.arange(MODES, dtype=jnp.int32)
    z_cos, z_sin = phase_table(jnp.arange(NZ, dtype=jnp.int32), kz_modes, NZ)
    y_cos, y_sin = phase_table(jnp.arange(NY, dtype=jnp.int32), signed_modes(2 * MODES), NY)
    x_cos, x_sin = phase_table(jnp.arange(NX, dtype=jnp.int32), signed_modes(2 * MODES), NX)
    fwd_scale = float(NX * NY * NZ) ** (-0.5)
    inv_scale = float(4 * MODES ** 3) ** (-0.5)
    z_factor = jnp.where(kz_modes == 0, 1.0, 2.0).astype(jnp.float32)

    def fourier_layer(values, weights, point_mix, offsets):
        spec_in = x_forward(yz_forward(values, z_cos, z_sin, y_cos, y_sin), x_cos, x_sin) * fwd_scale
        spec_out = mode_mix(spec_in, weights)
        spectral = yz_inverse(x_inverse(spec_out, x_cos, x_sin), z_cos, z_sin, y_cos, y_sin, inv_scale * z_factor)
        pre_act = spectral + contract('xiyz,io->xoyz', values, point_mix) + offsets[None, :, None, None]
        return jax.nn.gelu(pre_act)
    output, pullback = jax.vjp(fourier_layer, flow_field, spec_weight, point_weight, pointwise_bias)
    grad_field, grad_spec, grad_point, grad_bias = pullback(cotangent)
    return (output, grad_field, grad_spec, grad_point * fwd_scale, grad_bias * fwd_scale)
```

```python
import functools
import math

import jax
import jax.numpy as jnp
import ml_dtypes
import numpy as np
from jax import lax
from jax.experimental import pallas as pl
from jax.experimental.pallas import tpu as pltpu
from jax.sharding import PartitionSpec as P

MODES = 16
KY = 2 * MODES
KX = 2 * MODES
MIB = 1024 * 1024
NT = (((1,), (1,)), ((), ()))
TN = (((0,), (0,)), ((), ()))
f32 = jnp.float32
bf16 = jnp.bfloat16


def signed(n):
    j = np.arange(n)
    return np.where(j < n // 2, j, j - n)


def phases(positions, waves, length):
    angle = ((positions[:, None] * waves[None, :]) % length) * (2.0 * math.pi / length)
    return np.cos(angle), np.sin(angle)


def halves(table):
    table = np.asarray(table, np.float32)
    high = table.astype(ml_dtypes.bfloat16)
    low = (table - high.astype(np.float32)).astype(ml_dtypes.bfloat16)
    return high, low


def stack3(table, axis):
    high, low = halves(table)
    return np.concatenate([high, high, low], axis=axis)


def y_table(ny):
    cos, sin = phases(np.arange(ny), signed(KY), ny)
    return np.concatenate([cos.T, -sin.T], axis=0)


def z_table(nz, scale, factor):
    cos, sin = phases(np.arange(nz), np.arange(MODES), nz)
    weight = scale * np.where(np.arange(MODES) == 0, 1.0, factor)
    cos, sin = cos.T * weight[:, None], sin.T * weight[:, None]
    real = np.concatenate([cos, sin], axis=1)
    imag = np.concatenate([-sin, cos], axis=1)
    both = np.stack([real, imag], axis=1).reshape(4, 4, 2, 2 * nz)
    return both.transpose(1, 0, 2, 3).reshape(2 * MODES, 2 * nz)


def x_forward_table(nx, scale):
    cos, sin = phases(np.arange(nx), signed(KX), nx)
    top = np.concatenate([cos, -sin], axis=1)
    bottom = np.concatenate([sin, cos], axis=1)
    return scale * np.concatenate([top, bottom], axis=0)


def x_inverse_table(nx):
    cos, sin = phases(np.arange(nx), signed(KX), nx)
    top = np.concatenate([cos, -sin], axis=1)
    bottom = np.concatenate([sin, cos], axis=1)
    return np.concatenate([top, bottom], axis=0)


def by_low(table, axis):
    order = np.arange(2 * KX).reshape(2, KX // 4, 4).transpose(0, 2, 1).reshape(-1)
    return np.take(table, order, axis=axis)


def split(values):
    high = values.astype(bf16)
    low = (values - high.astype(f32)).astype(bf16)
    return high, low


def data3(values):
    high, low = split(values)
    return jnp.concatenate([high, low, high], axis=0)


def dot(left, right, dims=(((1,), (0,)), ((), ()))):
    return lax.dot_general(left, right, dims, preferred_element_type=f32)


def group_transpose(tiles):
    group = lax.broadcasted_iota(jnp.int32, tiles[0].shape, 1) // 32
    result = []
    for m in range(4):
        moved = [pltpu.roll(tiles[n], ((n - m) * 32) % 128, 1) if n != m else tiles[n] for n in range(4)]
        low = jnp.where(group == 0, moved[0], moved[1])
        high = jnp.where(group == 2, moved[2], moved[3])
        result.append(jnp.where(group < 2, low, high))
    return result


def block_row(ky, plane, slab, ky_own):
    return (((ky // ky_own) * slab + plane) * ky_own + ky % ky_own) * 8


def forward_plane(load_channel, channels, fy_ref, tz_ref, scratch, out_ref, row_of):
    nz = scratch.shape[1]
    size = KY * channels
    for c in range(0, channels, 2):
        pair = jnp.concatenate([load_channel(c), load_channel(c + 1)], axis=1)
        high, low = split(pair)
        both = dot(fy_ref[...], jnp.concatenate([high, low], axis=0))
        half = both[: 2 * KY] + both[2 * KY :]
        for e in range(2):
            for part in range(2):
                scratch[pl.ds(part * size + c + e, KY, stride=channels), :] = half[
                    part * KY : (part + 1) * KY, e * nz : (e + 1) * nz
                ]
    high, low = split(jnp.concatenate([scratch[:size], scratch[size:]], axis=1))
    first = dot(tz_ref[...], high, NT)
    rows = first[: 2 * MODES] + first[2 * MODES :] + dot(tz_ref[: 2 * MODES, :], low, NT)
    for q in range(KY // 4):
        tiles = [rows[8 * j : 8 * j + 8, q * 128 : (q + 1) * 128] for j in range(4)]
        for e, tile in enumerate(group_transpose(tiles)):
            out_ref[pl.ds(row_of(4 * q + e), 8), :] = tile


def inverse_plane(in_ref, row_of, tz_ref, ty_ref, scratch, channels, emit):
    nz = scratch.shape[1]
    size = KY * channels
    columns = [[] for _ in range(4)]
    for q in range(KY // 4):
        tiles = [in_ref[pl.ds(row_of(4 * q + e), 8), :] for e in range(4)]
        for j, tile in enumerate(group_transpose(tiles)):
            columns[j].append(tile)
    rows = jnp.concatenate([jnp.concatenate(c, axis=1) for c in columns], axis=0)
    modes = dot(data3(rows), tz_ref[...], TN)
    for part in range(2):
        scratch[part * size : (part + 1) * size, :] = modes[:, part * nz : (part + 1) * nz]
    for c in range(0, channels, 2):
        sides = []
        for e in range(2):
            parts = [
                scratch[pl.ds(part * size + c + e, KY, stride=channels), :] for part in range(2)
            ]
            sides.append(jnp.concatenate(parts, axis=0))
        pair = dot(ty_ref[...], data3(jnp.concatenate(sides, axis=1)))
        for e in range(2):
            emit(c + e, pair[:, e * nz : (e + 1) * nz])


def spread_weight(weight, high_ref, low_ref):
    size = weight.shape[0]
    row = lax.broadcasted_iota(jnp.int32, (8 * size, size), 0) // 8
    column = lax.broadcasted_iota(jnp.int32, (8 * size, size), 1)
    expand = (row == column).astype(f32)
    tall = lax.dot_general(
        expand, weight, (((1,), (0,)), ((), ())), precision=lax.Precision.HIGHEST, preferred_element_type=f32
    )
    wide = lax.dot_general(tall, expand, NT, precision=lax.Precision.HIGHEST, preferred_element_type=f32)
    row = lax.broadcasted_iota(jnp.int32, wide.shape, 0) % 8
    column = lax.broadcasted_iota(jnp.int32, wide.shape, 1) % 8
    high, low = split(jnp.where(row == column, wide, 0.0))
    high_ref[...] = high
    low_ref[...] = low


def cell_tile(ref, start):
    sides = []
    for e in range(2):
        piece = ref[0, :, pl.ds(start + 8 * e, 8), :]
        sides.append(piece.reshape(piece.shape[0] * 8, piece.shape[2]))
    return jnp.concatenate(sides, axis=1)


def put_tile(ref, start, tile):
    channels, nz = ref.shape[1], ref.shape[3]
    for e in range(2):
        ref[0, :, pl.ds(start + 8 * e, 8), :] = tile[:, e * nz : (e + 1) * nz].reshape(channels, 8, nz)


def mix_cells(high_ref, low_ref, high, low):
    return dot(high_ref[...], high) + dot(low_ref[...], high) + dot(high_ref[...], low)


def first_kernel(slab, ky_own, field_ref, fy_ref, tz_ref, out_ref, scratch):
    plane = pl.program_id(0)
    forward_plane(
        lambda c: field_ref[0, c],
        field_ref.shape[1],
        fy_ref,
        tz_ref,
        scratch,
        out_ref,
        lambda ky: pl.multiple_of(block_row(ky, plane, slab, ky_own), 8),
    )


def quad_rows(ref, nx, lines, u):
    return jnp.concatenate([ref[pl.ds(2 * u + part, nx, stride=lines), :] for part in range(2)], axis=0)


def mix_kernel(nx, lines, in_ref, weight_ref, fx_ref, inv_ref, out_ref, sums):
    u = pl.program_id(0)
    wide = KX * 32
    modes = dot(data3(quad_rows(in_ref, nx, lines, u)), fx_ref[...], TN)
    tiles = [[], []]
    for j in range(4):
        real = modes[32 * j : 32 * j + 32, :wide]
        imag = modes[32 * j : 32 * j + 32, wide:]
        w_real, w_imag = weight_ref[j, 0], weight_ref[j, 1]
        products = (real * w_real - imag * w_imag, imag * w_real + real * w_imag)
        for part in range(2):
            total = jnp.sum(products[part].reshape(4, 8, wide), axis=0)
            base = (2 * j + part) * 64
            for a in range(8):
                sums[base + 8 * a : base + 8 * a + 8, :] = total[:, 128 * a : 128 * a + 128]
            tile = sums[pl.ds(base, 8, stride=8), :]
            for s in range(1, 8):
                tile = tile + sums[pl.ds(base + s, 8, stride=8), :]
            tiles[part].append(tile)
    mixed = jnp.concatenate(group_transpose(tiles[0]) + group_transpose(tiles[1]), axis=0)
    planes = dot(inv_ref[...], data3(mixed))
    for part in range(2):
        out_ref[pl.ds(2 * u + part, nx, stride=lines), :] = planes[part * nx : (part + 1) * nx]


def adjoint_kernel(
    nx, lines, in_ref, grad_ref, weight_ref, fx_ref, gx_ref, inv_ref, out_ref, dweight_ref, high_ref, low_ref
):
    u = pl.program_id(0)
    wide = KX * 32
    modes = dot(data3(quad_rows(in_ref, nx, lines, u)), fx_ref[...], TN)
    grads = dot(gx_ref[...], data3(quad_rows(grad_ref, nx, lines, u)))
    tiles = []
    for part in range(2):
        tiles.append(group_transpose([grads[part * 32 + 8 * b : part * 32 + 8 * b + 8, :] for b in range(4)]))
    for j in range(4):
        rows = slice(32 * j, 32 * j + 32)
        for a in range(8):
            cols = slice(128 * a, 128 * a + 128)
            late = slice(wide + 128 * a, wide + 128 * a + 128)
            g_real = jnp.broadcast_to(tiles[0][j][a : a + 1, :], (32, 128))
            g_imag = jnp.broadcast_to(tiles[1][j][a : a + 1, :], (32, 128))
            s_real, s_imag = modes[rows, cols], modes[rows, late]
            w_real, w_imag = weight_ref[j, 0, :, cols], weight_ref[j, 1, :, cols]
            dweight_ref[j, 0, :, cols] = s_real * g_real + s_imag * g_imag
            dweight_ref[j, 1, :, cols] = s_real * g_imag - s_imag * g_real
            high, low = split(g_real * w_real + g_imag * w_imag)
            high_ref[rows, cols], low_ref[rows, cols] = high, low
            high, low = split(g_imag * w_real - g_real * w_imag)
            high_ref[rows, late], low_ref[rows, late] = high, low
    first = dot(inv_ref[...], high_ref[...], NT)
    planes = first[: 2 * nx] + first[2 * nx :] + dot(inv_ref[: 2 * nx, :], low_ref[...], NT)
    for part in range(2):
        out_ref[pl.ds(2 * u + part, nx, stride=lines), :] = planes[part * nx : (part + 1) * nx]


def middle_kernel(
    slab,
    ky_own,
    in_ref,
    field_ref,
    cot_ref,
    weight_ref,
    bias_ref,
    tzi_ref,
    ty_ref,
    fy_ref,
    tzf_ref,
    output_ref,
    gpre_ref,
    spec_ref,
    sums_ref,
    scratch,
    pre,
    kron_high,
    kron_low,
    bias_wide,
    outer,
    total,
):
    plane = pl.program_id(0)
    channels, ny, nz = field_ref.shape[1:]
    row_of = lambda ky: pl.multiple_of(block_row(ky, plane, slab, ky_own), 8)

    @pl.when(plane == 0)
    def _():
        spread_weight(jnp.transpose(weight_ref[...]), kron_high, kron_low)
        row = lax.broadcasted_iota(jnp.int32, (8 * channels, channels), 0) // 8
        column = lax.broadcasted_iota(jnp.int32, (8 * channels, channels), 1)
        picked = jnp.where(row == column, bias_ref[...], 0.0)
        bias_wide[...] = jnp.broadcast_to(jnp.sum(picked, axis=1, keepdims=True), bias_wide.shape)
        outer[...] = jnp.zeros_like(outer)
        total[...] = jnp.zeros_like(total)

    def emit(channel, values):
        pre[0, channel] = values

    inverse_plane(in_ref, row_of, tzi_ref, ty_ref, scratch, channels, emit)

    rate = math.sqrt(2.0 / math.pi)

    def body(step, carry):
        start = pl.multiple_of(step * 16, 16)
        high, low = split(cell_tile(field_ref, start))
        values = cell_tile(pre, start) + mix_cells(kron_high, kron_low, high, low)
        values = values + jnp.concatenate([bias_wide[...]] * (2 * nz // 128), axis=1)
        square = values * values
        bent = jnp.tanh(rate * values * (1.0 + 0.044715 * square))
        half = 0.5 + 0.5 * bent
        put_tile(output_ref, start, values * half)
        slope = half + (0.5 * rate) * values * (1.0 - bent * bent) * (1.0 + (3 * 0.044715) * square)
        gpre = cell_tile(cot_ref, start) * slope
        put_tile(gpre_ref, start, gpre)
        g_high, g_low = split(gpre)
        outer[...] += dot(high, g_high, NT) + dot(low, g_high, NT) + dot(high, g_low, NT)
        total[...] += gpre
        return carry

    lax.fori_loop(0, ny // 16, body, 0)

    forward_plane(lambda c: gpre_ref[0, c], channels, fy_ref, tzf_ref, scratch, spec_ref, row_of)

    @pl.when(plane == slab - 1)
    def _():
        highest = dict(precision=lax.Precision.HIGHEST, preferred_element_type=f32)
        row = lax.broadcasted_iota(jnp.int32, outer.shape, 0) % 8
        column = lax.broadcasted_iota(jnp.int32, outer.shape, 1) % 8
        kept = jnp.where(row == column, outer[...], 0.0)
        kept = jnp.sum(kept.reshape(channels, 8, 8 * channels), axis=1)
        row = lax.broadcasted_iota(jnp.int32, (8 * channels, channels), 0) // 8
        column = lax.broadcasted_iota(jnp.int32, (8 * channels, channels), 1)
        pick = (row == column).astype(f32)
        sums_ref[:channels, :] = lax.dot_general(kept, pick, (((1,), (0,)), ((), ())), **highest)
        ones = jnp.ones((8, total.shape[1]), f32)
        line = lax.dot_general(ones, total[...], NT, **highest)
        sums_ref[channels:, :] = lax.dot_general(line, pick, (((1,), (0,)), ((), ())), **highest)


def last_kernel(
    slab, ky_own, in_ref, gpre_ref, weight_ref, tzi_ref, ty_ref, out_ref, scratch, kron_high, kron_low
):
    plane = pl.program_id(0)
    channels, ny, nz = gpre_ref.shape[1:]
    row_of = lambda ky: pl.multiple_of(block_row(ky, plane, slab, ky_own), 8)

    @pl.when(plane == 0)
    def _():
        spread_weight(weight_ref[...], kron_high, kron_low)

    def emit(channel, values):
        out_ref[0, channel] = values

    inverse_plane(in_ref, row_of, tzi_ref, ty_ref, scratch, channels, emit)

    def body(step, carry):
        start = pl.multiple_of(step * 16, 16)
        high, low = split(cell_tile(gpre_ref, start))
        put_tile(out_ref, start, cell_tile(out_ref, start) + mix_cells(kron_high, kron_low, high, low))
        return carry

    lax.fori_loop(0, ny // 16, body, 0)


def whole(array):
    zeros = (0,) * array.ndim
    return pl.BlockSpec(array.shape, lambda *_: zeros)


def params(megabytes):
    return pltpu.CompilerParams(vmem_limit_bytes=megabytes * MIB, dimension_semantics=("arbitrary",))


def per_device(flow_field, cotangent, spec_weight, point_weight, pointwise_bias):
    slab, channels, ny, nz = flow_field.shape
    devices = lax.axis_size("space")
    nx = slab * devices
    pair_local = spec_weight.shape[0]
    assert pair_local % MODES == 0 or slab == 1
    assert channels == 32 and nz == 128 and pair_local % 4 == 0
    ky_own = max(1, pair_local // MODES)
    lines = pair_local // 2
    rows = nx * lines
    quads = pair_local // 4
    wide = KX * channels
    fwd_scale = float(nx * ny * nz) ** (-0.5)
    inv_scale = float(4 * MODES**3) ** (-0.5)

    fy_high, fy_low = halves(y_table(ny))
    fy = np.concatenate(
        [np.concatenate([fy_high, fy_high], axis=1), np.concatenate([fy_low, fy_low], axis=1)], axis=0
    )
    fy = jnp.asarray(fy)
    ty = jnp.asarray(stack3(y_table(ny).T, 1))
    tz_first = jnp.asarray(np.concatenate(halves(z_table(nz, 1.0, 1.0)), axis=0))
    tz_grad = jnp.asarray(np.concatenate(halves(z_table(nz, inv_scale, 2.0)), axis=0))
    tzi_out = jnp.asarray(stack3(z_table(nz, inv_scale, 2.0), 0))
    tzi_grad = jnp.asarray(stack3(z_table(nz, fwd_scale, 1.0), 0))
    fx = x_forward_table(nx, fwd_scale)
    fx_wide = jnp.asarray(np.repeat(stack3(fx, 0), channels, axis=1))
    gx = jnp.asarray(stack3(by_low(x_forward_table(nx, 1.0), 1).T, 1))
    inv = x_inverse_table(nx)
    inv_low = jnp.asarray(stack3(by_low(inv, 1), 1))
    inv_wide = jnp.asarray(np.repeat(np.concatenate(halves(inv), axis=0), channels, axis=1))

    plane_spec = pl.BlockSpec((1, channels, ny, nz), lambda p: (p, 0, 0, 0))
    line_shape = jax.ShapeDtypeStruct((rows, 128), f32)
    line_spec = pl.BlockSpec((rows, 128), lambda p: (0, 0))
    weight_spec = pl.BlockSpec((4, 2, channels, wide), lambda u: (u, 0, 0, 0))
    field_shape = jax.ShapeDtypeStruct(flow_field.shape, f32)
    mode_scratch = pltpu.VMEM((2 * KY * channels, nz), f32)
    kron_scratch = pltpu.VMEM((8 * channels, 8 * channels), bf16)

    def exchange(lines_out):
        blocks = lines_out.reshape(devices, rows // devices, 128)
        return lax.all_to_all(blocks, "space", split_axis=0, concat_axis=0, tiled=True).reshape(rows, 128)

    first = pl.pallas_call(
        functools.partial(first_kernel, slab, ky_own),
        grid=(slab,),
        in_specs=[plane_spec, whole(fy), whole(tz_first)],
        out_specs=line_spec,
        out_shape=line_shape,
        scratch_shapes=[mode_scratch],
        compiler_params=params(40),
        name="field_forward",
    )(flow_field, fy, tz_first)
    spec_x = exchange(first)

    mixed = pl.pallas_call(
        functools.partial(mix_kernel, nx, lines),
        grid=(quads,),
        in_specs=[line_spec, weight_spec, whole(fx_wide), whole(inv_low)],
        out_specs=line_spec,
        out_shape=line_shape,
        scratch_shapes=[pltpu.VMEM((512, 128), f32)],
        compiler_params=params(40),
        name="mode_mix",
    )(spec_x, spec_weight, fx_wide, inv_low)
    mixed = exchange(mixed)

    bias = pointwise_bias.reshape(1, channels)
    output, gpre, grad_lines, local_sums = pl.pallas_call(
        functools.partial(middle_kernel, slab, ky_own),
        grid=(slab,),
        in_specs=[
            line_spec,
            plane_spec,
            plane_spec,
            whole(point_weight),
            whole(bias),
            whole(tzi_out),
            whole(ty),
            whole(fy),
            whole(tz_grad),
        ],
        out_specs=[
            plane_spec,
            plane_spec,
            line_spec,
            pl.BlockSpec((channels + 8, channels), lambda p: (0, 0)),
        ],
        out_shape=[field_shape, field_shape, line_shape, jax.ShapeDtypeStruct((channels + 8, channels), f32)],
        scratch_shapes=[
            mode_scratch,
            pltpu.VMEM((1, channels, ny, nz), f32),
            kron_scratch,
            kron_scratch,
            pltpu.VMEM((8 * channels, 128), f32),
            pltpu.VMEM((8 * channels, 8 * channels), f32),
            pltpu.VMEM((8 * channels, 2 * nz), f32),
        ],
        compiler_params=params(56),
        name="middle",
    )(mixed, flow_field, cotangent, point_weight, bias, tzi_out, ty, fy, tz_grad)
    grad_x = exchange(grad_lines)
    gathered = lax.all_gather(local_sums, "space", axis=0, tiled=False)

    grad_mixed, grad_spec = pl.pallas_call(
        functools.partial(adjoint_kernel, nx, lines),
        grid=(quads,),
        in_specs=[
            line_spec,
            line_spec,
            weight_spec,
            whole(fx_wide),
            whole(gx),
            whole(inv_wide),
        ],
        out_specs=[line_spec, weight_spec],
        out_shape=[line_shape, jax.ShapeDtypeStruct(spec_weight.shape, f32)],
        scratch_shapes=[pltpu.VMEM((4 * channels, 2 * wide), bf16), pltpu.VMEM((4 * channels, 2 * wide), bf16)],
        compiler_params=params(48),
        name="mode_adjoint",
    )(spec_x, grad_x, spec_weight, fx_wide, gx, inv_wide)
    back = exchange(grad_mixed)

    grad_field = pl.pallas_call(
        functools.partial(last_kernel, slab, ky_own),
        grid=(slab,),
        in_specs=[line_spec, plane_spec, whole(point_weight), whole(tzi_grad), whole(ty)],
        out_specs=plane_spec,
        out_shape=field_shape,
        scratch_shapes=[mode_scratch, kron_scratch, kron_scratch],
        compiler_params=params(40),
        name="field_inverse",
    )(back, gpre, point_weight, tzi_grad, ty)

    summed = jnp.sum(gathered, axis=0) * fwd_scale
    return output, grad_field, grad_spec, summed[:channels], summed[channels]


def solution(mesh):
    cells = P(("group", "space"), None, None, None)
    return jax.shard_map(
        per_device,
        mesh=mesh,
        in_specs=(cells, cells, P("space", None, None, None), P(), P()),
        out_specs=(cells, cells, cells, P("group", None), P("group")),
        check_vma=False,
    )
```

```python
import functools
import math

import jax
import jax.numpy as jnp
import ml_dtypes
import numpy as np
from jax import lax
from jax.experimental import pallas as pl
from jax.experimental.pallas import tpu as pltpu
from jax.sharding import PartitionSpec as P

MODES = 16
KY = 2 * MODES
KX = 2 * MODES
MIB = 1024 * 1024
NT = (((1,), (1,)), ((), ()))
TN = (((0,), (0,)), ((), ()))
f32 = jnp.float32
bf16 = jnp.bfloat16


def signed(n):
    j = np.arange(n)
    return np.where(j < n // 2, j, j - n)


def phases(positions, waves, length):
    angle = ((positions[:, None] * waves[None, :]) % length) * (2.0 * math.pi / length)
    return np.cos(angle), np.sin(angle)


def halves(table):
    table = np.asarray(table, np.float32)
    high = table.astype(ml_dtypes.bfloat16)
    low = (table - high.astype(np.float32)).astype(ml_dtypes.bfloat16)
    return high, low


def stack3(table, axis):
    high, low = halves(table)
    return np.concatenate([high, high, low], axis=axis)


def y_table(ny):
    cos, sin = phases(np.arange(ny), signed(KY), ny)
    return np.concatenate([cos.T, -sin.T], axis=0)


def z_table(nz, scale, factor):
    cos, sin = phases(np.arange(nz), np.arange(MODES), nz)
    weight = scale * np.where(np.arange(MODES) == 0, 1.0, factor)
    cos, sin = cos.T * weight[:, None], sin.T * weight[:, None]
    real = np.concatenate([cos, sin], axis=1)
    imag = np.concatenate([-sin, cos], axis=1)
    both = np.stack([real, imag], axis=1).reshape(4, 4, 2, 2 * nz)
    return both.transpose(1, 0, 2, 3).reshape(2 * MODES, 2 * nz)


def x_forward_table(nx, scale):
    cos, sin = phases(np.arange(nx), signed(KX), nx)
    top = np.concatenate([cos, -sin], axis=1)
    bottom = np.concatenate([sin, cos], axis=1)
    return scale * np.concatenate([top, bottom], axis=0)


def x_inverse_table(nx):
    cos, sin = phases(np.arange(nx), signed(KX), nx)
    top = np.concatenate([cos, -sin], axis=1)
    bottom = np.concatenate([sin, cos], axis=1)
    return np.concatenate([top, bottom], axis=0)


def by_low(table, axis):
    order = np.arange(2 * KX).reshape(2, KX // 4, 4).transpose(0, 2, 1).reshape(-1)
    return np.take(table, order, axis=axis)


def split(values):
    high = values.astype(bf16)
    low = (values - high.astype(f32)).astype(bf16)
    return high, low


def data3(values):
    high, low = split(values)
    return jnp.concatenate([high, low, high], axis=0)


def dot(left, right, dims=(((1,), (0,)), ((), ()))):
    return lax.dot_general(left, right, dims, preferred_element_type=f32)


def group_transpose(tiles):
    group = lax.broadcasted_iota(jnp.int32, tiles[0].shape, 1) // 32
    result = []
    for m in range(4):
        moved = [pltpu.roll(tiles[n], ((n - m) * 32) % 128, 1) if n != m else tiles[n] for n in range(4)]
        low = jnp.where(group == 0, moved[0], moved[1])
        high = jnp.where(group == 2, moved[2], moved[3])
        result.append(jnp.where(group < 2, low, high))
    return result


def block_row(ky, plane, stride, ky_own):
    return (ky // ky_own) * stride + (plane * ky_own + ky % ky_own) * 8


def forward_plane(load_channel, channels, fy_ref, tz_ref, scratch, out_ref, row_of):
    nz = scratch.shape[1]
    size = KY * channels
    for c in range(0, channels, 2):
        pair = jnp.concatenate([load_channel(c), load_channel(c + 1)], axis=1)
        high, low = split(pair)
        both = dot(fy_ref[...], jnp.concatenate([high, low], axis=0))
        half = both[: 2 * KY] + both[2 * KY :]
        for e in range(2):
            for part in range(2):
                scratch[pl.ds(part * size + c + e, KY, stride=channels), :] = half[
                    part * KY : (part + 1) * KY, e * nz : (e + 1) * nz
                ]
    high, low = split(jnp.concatenate([scratch[:size], scratch[size:]], axis=1))
    first = dot(tz_ref[...], high, NT)
    rows = first[: 2 * MODES] + first[2 * MODES :] + dot(tz_ref[: 2 * MODES, :], low, NT)
    for q in range(KY // 4):
        tiles = [rows[8 * j : 8 * j + 8, q * 128 : (q + 1) * 128] for j in range(4)]
        for e, tile in enumerate(group_transpose(tiles)):
            out_ref[pl.ds(row_of(4 * q + e), 8), :] = tile


def inverse_plane(in_ref, row_of, tz_ref, ty_ref, scratch, channels, emit):
    nz = scratch.shape[1]
    size = KY * channels
    columns = [[] for _ in range(4)]
    for q in range(KY // 4):
        tiles = [in_ref[pl.ds(row_of(4 * q + e), 8), :] for e in range(4)]
        for j, tile in enumerate(group_transpose(tiles)):
            columns[j].append(tile)
    rows = jnp.concatenate([jnp.concatenate(c, axis=1) for c in columns], axis=0)
    modes = dot(data3(rows), tz_ref[...], TN)
    for part in range(2):
        scratch[part * size : (part + 1) * size, :] = modes[:, part * nz : (part + 1) * nz]
    for c in range(0, channels, 2):
        sides = []
        for e in range(2):
            parts = [
                scratch[pl.ds(part * size + c + e, KY, stride=channels), :] for part in range(2)
            ]
            sides.append(jnp.concatenate(parts, axis=0))
        pair = dot(ty_ref[...], data3(jnp.concatenate(sides, axis=1)))
        for e in range(2):
            emit(c + e, pair[:, e * nz : (e + 1) * nz])


def spread_weight(weight, high_ref, low_ref):
    size = weight.shape[0]
    row = lax.broadcasted_iota(jnp.int32, (8 * size, size), 0) // 8
    column = lax.broadcasted_iota(jnp.int32, (8 * size, size), 1)
    expand = (row == column).astype(f32)
    tall = lax.dot_general(
        expand, weight, (((1,), (0,)), ((), ())), precision=lax.Precision.HIGHEST, preferred_element_type=f32
    )
    wide = lax.dot_general(tall, expand, NT, precision=lax.Precision.HIGHEST, preferred_element_type=f32)
    row = lax.broadcasted_iota(jnp.int32, wide.shape, 0) % 8
    column = lax.broadcasted_iota(jnp.int32, wide.shape, 1) % 8
    high, low = split(jnp.where(row == column, wide, 0.0))
    high_ref[...] = high
    low_ref[...] = low


def cell_tile(ref, plane, start):
    sides = []
    for e in range(2):
        piece = ref[plane, :, pl.ds(start + 8 * e, 8), :]
        sides.append(piece.reshape(piece.shape[0] * 8, piece.shape[2]))
    return jnp.concatenate(sides, axis=1)


def put_tile(ref, plane, start, tile):
    channels, nz = ref.shape[1], ref.shape[3]
    for e in range(2):
        ref[plane, :, pl.ds(start + 8 * e, 8), :] = tile[:, e * nz : (e + 1) * nz].reshape(channels, 8, nz)


def mix_cells(high_ref, low_ref, high, low):
    return dot(high_ref[...], high) + dot(low_ref[...], high) + dot(high_ref[...], low)


def rows_at(plane, stride, ky_own):
    def row_of(ky):
        row = block_row(ky, plane, stride, ky_own)
        return row if isinstance(row, int) else pl.multiple_of(row, 8)

    return row_of


def transfers(pairs, sems):
    return [pltpu.make_async_copy(src, dst, sems.at[i]) for i, (src, dst) in enumerate(pairs)]


def chunks(channels):
    return [slice(8 * g, 8 * g + 8) for g in range(channels // 8)]


def first_kernel(stride, ky_own, field_hbm, fy_hbm, tz_hbm, out_ref, field_ref, fy_ref, tz_ref, scratch, sems, table_sems):
    slab, channels = field_ref.shape[:2]
    tables = transfers([(fy_hbm, fy_ref), (tz_hbm, tz_ref)], table_sems)
    parts = [(field_hbm.at[p, c], field_ref.at[p, c]) for p in range(slab) for c in chunks(channels)]
    for copy in tables + transfers(parts, sems):
        copy.start()
    for copy in tables:
        copy.wait()

    def body(p, carry):
        def load_channel(c):
            if c % 8 == 0:
                part = slice(c, c + 8)
                sem = sems.at[p * (channels // 8) + c // 8]
                pltpu.make_async_copy(field_hbm.at[p, part], field_ref.at[p, part], sem).wait()
            return field_ref[p, c]

        forward_plane(load_channel, channels, fy_ref, tz_ref, scratch, out_ref, rows_at(p, stride, ky_own))
        return carry

    lax.fori_loop(0, slab, body, 0)


def point_kernel(field_ref, weight_ref, bias_ref, out_ref, kron_high, kron_low, bias_wide):
    channels = field_ref.shape[1]

    @pl.when(pl.program_id(0) == 0)
    def _():
        spread_weight(jnp.transpose(weight_ref[...]), kron_high, kron_low)
        row = lax.broadcasted_iota(jnp.int32, (8 * channels, channels), 0) // 8
        column = lax.broadcasted_iota(jnp.int32, (8 * channels, channels), 1)
        picked = jnp.where(row == column, bias_ref[...], 0.0)
        bias_wide[...] = jnp.broadcast_to(jnp.sum(picked, axis=1, keepdims=True), bias_wide.shape)

    for start in range(0, field_ref.shape[2], 16):
        high, low = split(cell_tile(field_ref, 0, start))
        put_tile(out_ref, 0, start, mix_cells(kron_high, kron_low, high, low) + bias_wide[...])


def quad_rows(ref, nx, lines, u):
    return jnp.concatenate([ref[pl.ds(2 * u + part, nx, stride=lines), :] for part in range(2)], axis=0)


def data_rows(ref, nx, lines, u):
    high, low = split(jnp.transpose(quad_rows(ref, nx, lines, u)))
    return jnp.concatenate([high, low, high], axis=1)


def weight_loads(weight_hbm, weight_ref, table_pairs, sems):
    parts = [slice(256 * t, 256 * t + 256) for t in range(4)]
    pairs = table_pairs + [(weight_hbm.at[:, :, :, part], weight_ref.at[:, :, :, part]) for part in parts]
    copies = transfers(pairs, sems)
    for copy in copies:
        copy.start()
    return copies[: len(table_pairs)], copies[len(table_pairs) :]


def mix_kernel(
    nx, lines, in_ref, weight_hbm, fx_hbm, inv_hbm, out_ref, weight_ref, fx_ref, inv_ref, left, modes, sums, sems
):
    pairs = weight_ref.shape[0]
    wide = KX * 32
    tables, loads = weight_loads(weight_hbm, weight_ref, [(fx_hbm, fx_ref), (inv_hbm, inv_ref)], sems)
    for u in range(pairs // 4):
        left[128 * u : 128 * u + 128, :] = data_rows(in_ref, nx, lines, u)
    for copy in tables:
        copy.wait()
    for t in range(4):
        cols = slice(256 * t, 256 * t + 256)
        late = slice(wide + 256 * t, wide + 256 * t + 256)
        modes[:, :256] = dot(left[...], fx_ref[:, cols])
        modes[:, 256:] = dot(left[...], fx_ref[:, late])
        loads[t].wait()

        def body(pair, carry):
            rows = pl.ds(pl.multiple_of(32 * pair, 32), 32)
            real, imag = modes[rows, :256], modes[rows, 256:]
            w_real, w_imag = weight_ref[pair, 0, :, cols], weight_ref[pair, 1, :, cols]
            products = (real * w_real - imag * w_imag, imag * w_real + real * w_imag)
            for part in range(2):
                total = jnp.sum(products[part].reshape(4, 8, 256), axis=0)
                for e in range(2):
                    base = pl.multiple_of((2 * pair + part) * 64 + 8 * (2 * t + e), 8)
                    sums[pl.ds(base, 8), :] = total[:, 128 * e : 128 * e + 128]
            return carry

        lax.fori_loop(0, pairs, body, 0, unroll=4)
    for u in range(pairs // 4):
        tiles = [[], []]
        for j in range(4):
            for part in range(2):
                base = (2 * (4 * u + j) + part) * 64
                found = [sums[pl.ds(base + s, 8, stride=8), :] for s in range(8)]
                while len(found) > 1:
                    found = [found[k] + found[k + 1] for k in range(0, len(found), 2)]
                tiles[part].append(found[0])
        mixed = jnp.concatenate(group_transpose(tiles[0]) + group_transpose(tiles[1]), axis=0)
        planes = dot(inv_ref[...], data3(mixed))
        for part in range(2):
            out_ref[pl.ds(2 * u + part, nx, stride=lines), :] = planes[part * nx : (part + 1) * nx]


def gradient_tiles(grad_ref, gx_ref, nx, lines, u):
    grads = dot(gx_ref[...], data3(quad_rows(grad_ref, nx, lines, u)))
    tiles = []
    for part in range(2):
        tiles.append(group_transpose([grads[part * 32 + 8 * b : part * 32 + 8 * b + 8, :] for b in range(4)]))
    return tiles, grads


def weight_grad_kernel(nx, lines, in_ref, grad_ref, fx_ref, gx_ref, dweight_ref):
    u = pl.program_id(0)
    wide = KX * 32
    modes = dot(data3(quad_rows(in_ref, nx, lines, u)), fx_ref[...], TN)
    tiles, _ = gradient_tiles(grad_ref, gx_ref, nx, lines, u)
    for j in range(4):
        rows = slice(32 * j, 32 * j + 32)
        for a in range(8):
            cols = slice(128 * a, 128 * a + 128)
            late = slice(wide + 128 * a, wide + 128 * a + 128)
            g_real = jnp.broadcast_to(tiles[0][j][a : a + 1, :], (32, 128))
            g_imag = jnp.broadcast_to(tiles[1][j][a : a + 1, :], (32, 128))
            s_real, s_imag = modes[rows, cols], modes[rows, late]
            dweight_ref[j, 0, :, cols] = s_real * g_real + s_imag * g_imag
            dweight_ref[j, 1, :, cols] = s_real * g_imag - s_imag * g_real


def adjoint_kernel(
    slab,
    nx,
    lines,
    extra,
    grad_ref,
    weight_hbm,
    gx_hbm,
    inv_hbm,
    sums_ref,
    out_ref,
    weight_ref,
    gx_ref,
    inv_ref,
    rows_ref,
    left,
    total,
    sems,
):
    pairs = weight_ref.shape[0]
    devices = nx // slab
    stride = slab * lines + extra
    bias = None
    tables, loads = weight_loads(weight_hbm, weight_ref, [(gx_hbm, gx_ref), (inv_hbm, inv_ref)], sems)
    for copy in tables:
        copy.wait()
    for u in range(pairs // 4):
        tiles, grads = gradient_tiles(grad_ref, gx_ref, nx, lines, u)
        bias = grads[0:1, :] if u == 0 else bias
        for part in range(2):
            for j in range(4):
                base = (2 * (4 * u + j) + part) * 8
                rows_ref[base : base + 8, :] = tiles[part][j]
    early = lax.broadcasted_iota(jnp.int32, (32, 128), 1) % 32 < 16
    for t in range(4):
        loads[t].wait()

        def body(pair, carry):
            rows = pl.ds(pl.multiple_of(32 * pair, 32), 32)
            for e in range(2):
                cols = slice(256 * t + 128 * e, 256 * t + 128 * e + 128)
                g_real, g_imag = [
                    jnp.broadcast_to(rows_ref[pl.ds((2 * pair + part) * 8 + 2 * t + e, 1), :], (32, 128))
                    for part in range(2)
                ]
                w_real, w_imag = weight_ref[pair, 0, :, cols], weight_ref[pair, 1, :, cols]
                real = g_real * w_real + g_imag * w_imag
                imag = g_imag * w_real - g_real * w_imag
                folded = jnp.where(early, real + pltpu.roll(real, 112, 1), imag + pltpu.roll(imag, 16, 1))
                high, low = split(folded)
                left[rows, 128 * e : 128 * e + 128] = high
                left[rows, 256 + 128 * e : 384 + 128 * e] = low
            return carry

        lax.fori_loop(0, pairs, body, 0, unroll=4)
        table = inv_ref[256 * t : 256 * t + 256, :]
        product = dot(left[:, :256], table) + dot(left[:, 256:], table)
        if t == 0:
            total[...] = product
        else:
            total[...] += product
    lane = lax.broadcasted_iota(jnp.int32, (nx, 128), 1)
    carried = lax.axis_index("space") == 0
    for u in range(pairs // 4):
        both = total[128 * u : 128 * u + 128, :]
        planes = jnp.transpose(both[:, : 2 * nx] + both[:, 2 * nx :])
        real, imag = planes[:nx], planes[nx:]
        if u == 0:
            imag = jnp.where((lane < 32) & carried, jnp.broadcast_to(bias, (nx, 128)), imag)
        for part, values in ((0, real), (1, imag)):
            for p in range(slab):
                out_ref[pl.ds(p * lines + 2 * u + part, devices, stride=stride), :] = values[
                    p * devices : (p + 1) * devices
                ]
    for d in range(devices):
        out_ref[d * stride + slab * lines : d * stride + slab * lines + extra, :] = sums_ref[...]


def middle_kernel(
    stride,
    ky_own,
    in_ref,
    point_ref,
    cot_ref,
    tzi_ref,
    ty_ref,
    fy_ref,
    tzf_ref,
    output_hbm,
    gpre_hbm,
    spec_ref,
    output_ref,
    gpre_ref,
    scratch,
    sems,
):
    slab, channels = point_ref.shape[:2]
    rate = math.sqrt(2.0 / math.pi)

    def stores(p, g):
        part = slice(8 * g, 8 * g + 8)
        pairs = ((output_ref, output_hbm), (gpre_ref, gpre_hbm))
        return [
            pltpu.make_async_copy(src.at[p, part], dst.at[p, part], sems.at[k, p, g])
            for k, (src, dst) in enumerate(pairs)
        ]

    def body(p, carry):
        row_of = rows_at(p, stride, ky_own)

        def emit(channel, spectral):
            values = spectral + point_ref[p, channel]
            square = values * values
            bent = jnp.tanh(rate * values * (1.0 + 0.044715 * square))
            half = 0.5 + 0.5 * bent
            output_ref[p, channel] = values * half
            slope = half + (0.5 * rate) * values * (1.0 - bent * bent) * (1.0 + (3 * 0.044715) * square)
            gpre_ref[p, channel] = cot_ref[p, channel] * slope
            if channel % 8 == 7:
                for copy in stores(p, channel // 8):
                    copy.start()

        inverse_plane(in_ref, row_of, tzi_ref, ty_ref, scratch, channels, emit)
        forward_plane(lambda c: gpre_ref[p, c], channels, fy_ref, tzf_ref, scratch, spec_ref, row_of)
        return carry

    lax.fori_loop(0, slab, body, 0)
    for p in range(slab):
        for g in range(channels // 8):
            for copy in stores(p, g):
                copy.wait()


def back_kernel(field_ref, gpre_ref, weight_ref, out_ref, sums_ref, kron_high, kron_low, outer):
    channels = field_ref.shape[1]

    @pl.when(pl.program_id(0) == 0)
    def _():
        spread_weight(weight_ref[...], kron_high, kron_low)
        outer[...] = jnp.zeros_like(outer)

    for start in range(0, field_ref.shape[2], 16):
        high, low = split(cell_tile(field_ref, 0, start))
        g_high, g_low = split(cell_tile(gpre_ref, 0, start))
        put_tile(out_ref, 0, start, mix_cells(kron_high, kron_low, g_high, g_low))
        outer[...] += dot(high, g_high, NT) + dot(low, g_high, NT) + dot(high, g_low, NT)

    @pl.when(pl.program_id(0) == pl.num_programs(0) - 1)
    def _():
        row = lax.broadcasted_iota(jnp.int32, outer.shape, 0) % 8
        column = lax.broadcasted_iota(jnp.int32, outer.shape, 1) % 8
        kept = jnp.where(row == column, outer[...], 0.0)
        kept = jnp.sum(kept.reshape(channels, 8, 8 * channels), axis=1)
        row = lax.broadcasted_iota(jnp.int32, (8 * channels, channels), 0) // 8
        column = lax.broadcasted_iota(jnp.int32, (8 * channels, channels), 1)
        pick = (row == column).astype(f32)
        small = lax.dot_general(
            kept, pick, (((1,), (0,)), ((), ())), precision=lax.Precision.HIGHEST, preferred_element_type=f32
        )
        sums_ref[...] = jnp.concatenate([small[8 * g : 8 * g + 8] for g in range(4)], axis=1)


def last_kernel(
    stride,
    ky_own,
    devices,
    sums_at,
    scales,
    in_ref,
    part_ref,
    back_hbm,
    tzi_hbm,
    ty_hbm,
    out_hbm,
    point_ref,
    bias_ref,
    scratch,
    cells_ref,
    tzi_ref,
    ty_ref,
    in_sems,
    out_sems,
    table_sems,
):
    slab, channels = cells_ref.shape[:2]
    groups = channels // 8
    places = [(p, c) for p in range(slab) for c in chunks(channels)]
    tables = transfers([(tzi_hbm, tzi_ref), (ty_hbm, ty_ref)], table_sems)
    loads = transfers([(back_hbm.at[at], cells_ref.at[at]) for at in places], in_sems)
    stores = transfers([(cells_ref.at[at], out_hbm.at[at]) for at in places], out_sems)

    def one(p, g, store):
        at = (p, slice(8 * g, 8 * g + 8))
        if store:
            return pltpu.make_async_copy(cells_ref.at[at], out_hbm.at[at], out_sems.at[p * groups + g])
        return pltpu.make_async_copy(back_hbm.at[at], cells_ref.at[at], in_sems.at[p * groups + g])

    for copy in tables + loads:
        copy.start()
    step, first = sums_at
    total = part_ref[first : first + 8, :]
    for d in range(1, devices):
        total = total + part_ref[d * step + first : d * step + first + 8, :]
    for g in range(4):
        point_ref[8 * g : 8 * g + 8, :] = total[:, 32 * g : 32 * g + 32] * scales[0]
    bias_ref[...] = in_ref[1:2, 0:32] * scales[1]
    for copy in tables:
        copy.wait()

    def body(p, carry):
        def emit(channel, values):
            if channel % 8 == 0:
                one(p, channel // 8, False).wait()
            cells_ref[p, channel] = cells_ref[p, channel] + values
            if channel % 8 == 7:
                one(p, channel // 8, True).start()

        inverse_plane(in_ref, rows_at(p, stride, ky_own), tzi_ref, ty_ref, scratch, channels, emit)
        return carry

    lax.fori_loop(0, slab, body, 0)
    for copy in stores:
        copy.wait()


VM = pl.BlockSpec(memory_space=pltpu.VMEM)
HBM = pl.BlockSpec(memory_space=pltpu.HBM)


def whole(array):
    zeros = (0,) * array.ndim
    return pl.BlockSpec(array.shape, lambda *_: zeros)


def params(megabytes):
    return pltpu.CompilerParams(vmem_limit_bytes=megabytes * MIB)


def cost(microseconds):
    return pl.CostEstimate(flops=0, bytes_accessed=int(microseconds * 3e6), transcendentals=0)


def keep(array):
    return pltpu.VMEM(array.shape, array.dtype)


def far(array):
    return pltpu.with_memory_space_constraint(array, pltpu.HBM)


def near(array):
    return pltpu.with_memory_space_constraint(array, pltpu.VMEM)


def per_device(flow_field, cotangent, spec_weight, point_weight, pointwise_bias):
    slab, channels, ny, nz = flow_field.shape
    devices = lax.axis_size("space")
    nx = slab * devices
    pair_local = spec_weight.shape[0]
    assert pair_local % MODES == 0 or slab == 1
    assert channels == 32 and nz == 128 and pair_local % 4 == 0
    ky_own = max(1, pair_local // MODES)
    lines = pair_local // 2
    rows = nx * lines
    block = slab * lines
    stride = slab * ky_own * 8
    extra = 8
    quads = pair_local // 4
    wide = KX * channels
    fwd_scale = float(nx * ny * nz) ** (-0.5)
    inv_scale = float(4 * MODES**3) ** (-0.5)

    fy_high, fy_low = halves(y_table(ny))
    fy = np.concatenate(
        [np.concatenate([fy_high, fy_high], axis=1), np.concatenate([fy_low, fy_low], axis=1)], axis=0
    )
    fy = jnp.asarray(fy)
    tz_first = jnp.asarray(np.concatenate(halves(z_table(nz, 1.0, 1.0)), axis=0))
    ty = jnp.asarray(stack3(y_table(ny).T, 1))
    tz_grad = jnp.asarray(np.concatenate(halves(z_table(nz, inv_scale, 2.0)), axis=0))
    tzi_out = jnp.asarray(stack3(z_table(nz, inv_scale, 2.0), 0))
    tzi_grad = jnp.asarray(stack3(z_table(nz, fwd_scale, 1.0), 0))
    fx = x_forward_table(nx, fwd_scale)
    fx_wide = jnp.asarray(np.repeat(stack3(fx, 0), channels, axis=1))
    gx = jnp.asarray(stack3(by_low(x_forward_table(nx, 1.0), 1).T, 1))
    inv = x_inverse_table(nx)
    inv_low = jnp.asarray(stack3(by_low(inv, 1), 1))
    by_plane = inv.reshape(2, devices, slab, 2 * KX).transpose(0, 2, 1, 3).reshape(2 * nx, 2 * KX)
    inv_wide = np.concatenate(halves(by_plane), axis=0).reshape(4 * nx, 2, KX).transpose(2, 1, 0)
    inv_wide = jnp.asarray(np.repeat(inv_wide.reshape(2 * KX, 4 * nx), channels // 2, axis=0))

    line_shape = jax.ShapeDtypeStruct((rows, 128), f32)
    line_spec = pl.BlockSpec((rows, 128), lambda p: (0, 0))
    field_shape = pltpu.HBM(flow_field.shape, f32)
    mode_scratch = pltpu.VMEM((2 * KY * channels, nz), f32)
    kron_scratch = pltpu.VMEM((8 * channels, 8 * channels), bf16)
    chunk_count = slab * (channels // 8)
    chunk_sems = pltpu.SemaphoreType.DMA((chunk_count,))
    pair_sems = pltpu.SemaphoreType.DMA((2,))
    cuts = ny // 32
    cells_spec = pl.BlockSpec((1, channels, 32, nz), lambda s: (s // cuts, 0, s % cuts, 0))

    def exchange(lines_out):
        blocks = lines_out.reshape(devices, -1, 128)
        return lax.all_to_all(blocks, "space", split_axis=0, concat_axis=0, tiled=True)

    first = pl.pallas_call(
        functools.partial(first_kernel, stride, ky_own),
        in_specs=[HBM, HBM, HBM],
        out_specs=VM,
        out_shape=line_shape,
        scratch_shapes=[
            pltpu.VMEM(flow_field.shape, f32),
            keep(fy),
            keep(tz_first),
            mode_scratch,
            chunk_sems,
            pair_sems,
        ],
        compiler_params=params(16),
        cost_estimate=cost(4),
        name="field_forward",
    )(far(flow_field), far(fy), far(tz_first))
    spec_x = exchange(first).reshape(rows, 128)

    bias = pointwise_bias.reshape(1, channels)
    pointwise = pl.pallas_call(
        point_kernel,
        grid=(slab * cuts,),
        in_specs=[cells_spec, whole(point_weight), whole(bias)],
        out_specs=cells_spec,
        out_shape=field_shape,
        scratch_shapes=[kron_scratch, kron_scratch, pltpu.VMEM((8 * channels, 2 * nz), f32)],
        compiler_params=params(16),
        cost_estimate=cost(6),
        name="pointwise",
    )(far(flow_field), point_weight, bias)

    spec_x, pointwise = lax.optimization_barrier((spec_x, pointwise))
    mixed = pl.pallas_call(
        functools.partial(mix_kernel, nx, lines),
        in_specs=[VM, HBM, HBM, HBM],
        out_specs=VM,
        out_shape=line_shape,
        scratch_shapes=[
            keep(spec_weight),
            keep(fx_wide),
            keep(inv_low),
            pltpu.VMEM((32 * pair_local, 6 * nx), bf16),
            pltpu.VMEM((32 * pair_local, 512), f32),
            pltpu.VMEM((128 * pair_local, 128), f32),
            pltpu.SemaphoreType.DMA((6,)),
        ],
        compiler_params=params(24),
        cost_estimate=cost(5),
        name="mode_mix",
    )(spec_x, far(spec_weight), far(fx_wide), far(inv_low))
    mixed = exchange(mixed).reshape(rows, 128)

    output, gpre, grad_lines = pl.pallas_call(
        functools.partial(middle_kernel, stride, ky_own),
        in_specs=[VM] * 7,
        out_specs=[HBM, HBM, VM],
        out_shape=[field_shape, field_shape, line_shape],
        scratch_shapes=[
            pltpu.VMEM(flow_field.shape, f32),
            pltpu.VMEM(flow_field.shape, f32),
            mode_scratch,
            pltpu.SemaphoreType.DMA((2, slab, channels // 8)),
        ],
        compiler_params=params(24),
        cost_estimate=cost(10),
        name="middle",
    )(mixed, near(pointwise), near(cotangent), near(tzi_out), near(ty), near(fy), near(tz_grad))
    grad_x = exchange(grad_lines).reshape(rows, 128)

    back, local_sums = pl.pallas_call(
        back_kernel,
        grid=(slab * cuts,),
        in_specs=[cells_spec, cells_spec, whole(point_weight)],
        out_specs=[cells_spec, pl.BlockSpec((extra, 128), lambda s: (0, 0))],
        out_shape=[field_shape, jax.ShapeDtypeStruct((extra, 128), f32)],
        scratch_shapes=[kron_scratch, kron_scratch, pltpu.VMEM((8 * channels, 8 * channels), f32)],
        compiler_params=params(16),
        cost_estimate=cost(8),
        name="pointwise_back",
    )(far(flow_field), far(gpre), point_weight)

    sent = devices * (block + extra)
    grad_mixed = pl.pallas_call(
        functools.partial(adjoint_kernel, slab, nx, lines, extra),
        in_specs=[VM, HBM, HBM, HBM, VM],
        out_specs=VM,
        out_shape=jax.ShapeDtypeStruct((sent, 128), f32),
        scratch_shapes=[
            keep(spec_weight),
            keep(gx),
            keep(inv_wide),
            pltpu.VMEM((16 * pair_local, 128), f32),
            pltpu.VMEM((32 * pair_local, 512), bf16),
            pltpu.VMEM((32 * pair_local, 4 * nx), f32),
            pltpu.SemaphoreType.DMA((6,)),
        ],
        compiler_params=params(24),
        cost_estimate=cost(6),
        name="mode_adjoint",
    )(grad_x, far(spec_weight), far(gx), far(inv_wide), local_sums)
    received = exchange(grad_mixed)

    grad_spec = pl.pallas_call(
        functools.partial(weight_grad_kernel, nx, lines),
        grid=(quads,),
        in_specs=[line_spec, line_spec, whole(fx_wide), whole(gx)],
        out_specs=pl.BlockSpec((4, 2, channels, wide), lambda u: (u, 0, 0, 0)),
        out_shape=pltpu.HBM(spec_weight.shape, f32),
        compiler_params=params(16),
        cost_estimate=cost(6),
        name="weight_grad",
    )(spec_x, grad_x, far(fx_wide), far(gx))

    if pair_local >= MODES:
        lines_in = sums_in = received.reshape(sent, 128)
        stride_in, sums_at = stride + extra, (stride + extra, stride)
    else:
        lines_in = received[:, :block].reshape(rows, 128)
        sums_in = received[:, block:].reshape(devices * extra, 128)
        stride_in, sums_at = stride, (extra, 0)
    grad_field, grad_point, grad_bias = pl.pallas_call(
        functools.partial(
            last_kernel, stride_in, ky_own, devices, sums_at, (fwd_scale, fwd_scale / inv_scale)
        ),
        in_specs=[VM, VM, HBM, HBM, HBM],
        out_specs=[HBM, VM, VM],
        out_shape=[
            field_shape,
            jax.ShapeDtypeStruct((channels, channels), f32),
            jax.ShapeDtypeStruct((1, channels), f32),
        ],
        scratch_shapes=[
            mode_scratch,
            pltpu.VMEM(flow_field.shape, f32),
            keep(tzi_grad),
            keep(ty),
            chunk_sems,
            chunk_sems,
            pair_sems,
        ],
        compiler_params=params(16),
        cost_estimate=cost(8),
        name="field_inverse",
    )(lines_in, sums_in, far(back), far(tzi_grad), far(ty))

    return output, grad_field, grad_spec, grad_point, grad_bias.reshape(channels)


def solution(mesh):
    cells = P(("group", "space"), None, None, None)
    return jax.shard_map(
        per_device,
        mesh=mesh,
        in_specs=(cells, cells, P("space", None, None, None), P(), P()),
        out_specs=(cells, cells, cells, P("group", None), P("group")),
        check_vma=False,
    )
```

```python
import functools
import math

import jax
import jax.numpy as jnp
import ml_dtypes
import numpy as np
from jax import lax
from jax.experimental import pallas as pl
from jax.experimental.pallas import tpu as pltpu
from jax.sharding import PartitionSpec as P

MODES = 16
KY = 2 * MODES
KX = 2 * MODES
MIB = 1024 * 1024
NT = (((1,), (1,)), ((), ()))
TN = (((0,), (0,)), ((), ()))
f32 = jnp.float32
bf16 = jnp.bfloat16


def signed(n):
    j = np.arange(n)
    return np.where(j < n // 2, j, j - n)


def phases(positions, waves, length):
    angle = ((positions[:, None] * waves[None, :]) % length) * (2.0 * math.pi / length)
    return np.cos(angle), np.sin(angle)


def halves(table):
    table = np.asarray(table, np.float32)
    high = table.astype(ml_dtypes.bfloat16)
    low = (table - high.astype(np.float32)).astype(ml_dtypes.bfloat16)
    return high, low


def stack3(table, axis):
    high, low = halves(table)
    return np.concatenate([high, high, low], axis=axis)


def y_table(ny):
    cos, sin = phases(np.arange(ny), signed(KY), ny)
    return np.concatenate([cos.T, -sin.T], axis=0)


def z_table(nz, scale, factor):
    cos, sin = phases(np.arange(nz), np.arange(MODES), nz)
    weight = scale * np.where(np.arange(MODES) == 0, 1.0, factor)
    cos, sin = cos.T * weight[:, None], sin.T * weight[:, None]
    real = np.concatenate([cos, sin], axis=1)
    imag = np.concatenate([-sin, cos], axis=1)
    both = np.stack([real, imag], axis=1).reshape(4, 4, 2, 2 * nz)
    return both.transpose(1, 0, 2, 3).reshape(2 * MODES, 2 * nz)


def x_forward_table(nx, scale):
    cos, sin = phases(np.arange(nx), signed(KX), nx)
    top = np.concatenate([cos, -sin], axis=1)
    bottom = np.concatenate([sin, cos], axis=1)
    return scale * np.concatenate([top, bottom], axis=0)


def x_inverse_table(nx):
    cos, sin = phases(np.arange(nx), signed(KX), nx)
    top = np.concatenate([cos, -sin], axis=1)
    bottom = np.concatenate([sin, cos], axis=1)
    return np.concatenate([top, bottom], axis=0)


def by_low(table, axis):
    order = np.arange(2 * KX).reshape(2, KX // 4, 4).transpose(0, 2, 1).reshape(-1)
    return np.take(table, order, axis=axis)


def split(values):
    high = values.astype(bf16)
    low = (values - high.astype(f32)).astype(bf16)
    return high, low


def data3(values):
    high, low = split(values)
    return jnp.concatenate([high, low, high], axis=0)


def dot(left, right, dims=(((1,), (0,)), ((), ()))):
    return lax.dot_general(left, right, dims, preferred_element_type=f32)


def group_transpose(tiles):
    group = lax.broadcasted_iota(jnp.int32, tiles[0].shape, 1) // 32
    result = []
    for m in range(4):
        moved = [pltpu.roll(tiles[n], ((n - m) * 32) % 128, 1) if n != m else tiles[n] for n in range(4)]
        low = jnp.where(group == 0, moved[0], moved[1])
        high = jnp.where(group == 2, moved[2], moved[3])
        result.append(jnp.where(group < 2, low, high))
    return result


def block_row(ky, plane, stride, ky_own):
    return (ky // ky_own) * stride + (plane * ky_own + ky % ky_own) * 8


def forward_pair(c, channels, pair, fy_ref, scratch):
    nz = scratch.shape[1]
    size = KY * channels
    high, low = split(pair)
    both = dot(fy_ref[...], jnp.concatenate([high, low], axis=0))
    half = both[: 2 * KY] + both[2 * KY :]
    for e in range(2):
        for part in range(2):
            scratch[pl.ds(part * size + c + e, KY, stride=channels), :] = half[
                part * KY : (part + 1) * KY, e * nz : (e + 1) * nz
            ]


def forward_finish(channels, tz_ref, scratch, out_ref, row_of):
    size = KY * channels
    high, low = split(jnp.concatenate([scratch[:size], scratch[size:]], axis=1))
    first = dot(tz_ref[...], high, NT)
    rows = first[: 2 * MODES] + first[2 * MODES :] + dot(tz_ref[: 2 * MODES, :], low, NT)
    for q in range(KY // 4):
        tiles = [rows[8 * j : 8 * j + 8, q * 128 : (q + 1) * 128] for j in range(4)]
        for e, tile in enumerate(group_transpose(tiles)):
            out_ref[pl.ds(row_of(4 * q + e), 8), :] = tile


def inverse_plane(in_ref, row_of, tz_ref, ty_ref, scratch, channels, emit, after, before=lambda h: None):
    nz = scratch.shape[1]
    size = KY * channels
    columns = [[] for _ in range(4)]
    for q in range(KY // 4):
        tiles = [in_ref[pl.ds(row_of(4 * q + e), 8), :] for e in range(4)]
        for j, tile in enumerate(group_transpose(tiles)):
            columns[j].append(tile)
    rows = jnp.concatenate([jnp.concatenate(c, axis=1) for c in columns], axis=0)
    modes = dot(data3(rows), tz_ref[...], TN)
    for part in range(2):
        scratch[part * size : (part + 1) * size, :] = modes[:, part * nz : (part + 1) * nz]

    def group(h, carry):
        before(h)
        for k in range(0, 16, 2):
            sides = []
            for e in range(2):
                parts = [scratch[pl.ds(part * size + 16 * h + k + e, KY, stride=channels), :] for part in range(2)]
                sides.append(jnp.concatenate(parts, axis=0))
            emit(16 * h + k, dot(ty_ref[...], data3(jnp.concatenate(sides, axis=1))))
        after(h)
        return carry

    lax.fori_loop(0, channels // 16, group, 0)


def two(ref, p, c):
    return jnp.concatenate([ref[p, c], ref[p, c + 1]], axis=1)


def put_two(ref, p, c, values):
    nz = values.shape[1] // 2
    ref[p, c], ref[p, c + 1] = values[:, :nz], values[:, nz:]


def spread_weight(weight, kron_ref):
    size = weight.shape[0]
    row = lax.broadcasted_iota(jnp.int32, (8 * size, size), 0) // 8
    column = lax.broadcasted_iota(jnp.int32, (8 * size, size), 1)
    expand = (row == column).astype(f32)
    tall = lax.dot_general(
        expand, weight, (((1,), (0,)), ((), ())), precision=lax.Precision.HIGHEST, preferred_element_type=f32
    )
    wide = lax.dot_general(tall, expand, NT, precision=lax.Precision.HIGHEST, preferred_element_type=f32)
    row = lax.broadcasted_iota(jnp.int32, wide.shape, 0) % 8
    column = lax.broadcasted_iota(jnp.int32, wide.shape, 1) % 8
    kron_ref[...] = jnp.concatenate(split(jnp.where(row == column, wide, 0.0)), axis=0)


def cell_tile(ref, plane, start):
    sides = []
    for e in range(2):
        piece = ref[plane, :, pl.ds(start + 8 * e, 8), :]
        sides.append(piece.reshape(piece.shape[0] * 8, piece.shape[2]))
    return jnp.concatenate(sides, axis=1)


def put_tile(ref, plane, start, tile):
    channels, nz = ref.shape[1], ref.shape[3]
    for e in range(2):
        ref[plane, :, pl.ds(start + 8 * e, 8), :] = tile[:, e * nz : (e + 1) * nz].reshape(channels, 8, nz)


def mix_cells(kron_ref, high, low):
    size = high.shape[0]
    both = dot(kron_ref[...], high)
    return both[:size] + both[size:] + dot(kron_ref[:size, :], low)


def rows_at(plane, stride, ky_own):
    def row_of(ky):
        row = block_row(ky, plane, stride, ky_own)
        return row if isinstance(row, int) else pl.multiple_of(row, 8)

    return row_of


def transfers(pairs, sems):
    return [pltpu.make_async_copy(src, dst, sems.at[i]) for i, (src, dst) in enumerate(pairs)]


def chunks(channels):
    return [slice(8 * g, 8 * g + 8) for g in range(channels // 8)]


def first_kernel(stride, ky_own, field_hbm, fy_hbm, tz_hbm, out_ref, field_ref, fy_ref, tz_ref, scratch, sems, table_sems):
    slab, channels = field_ref.shape[:2]
    tables = transfers([(fy_hbm, fy_ref), (tz_hbm, tz_ref)], table_sems)
    parts = [(field_hbm.at[p, c], field_ref.at[p, c]) for p in range(slab) for c in chunks(channels)]
    for copy in tables + transfers(parts, sems):
        copy.start()
    for copy in tables:
        copy.wait()

    def body(p, carry):
        for c in range(0, channels, 2):
            if c % 16 == 0:
                for g in (c // 8, c // 8 + 1):
                    part = slice(8 * g, 8 * g + 8)
                    sem = sems.at[p * (channels // 8) + g]
                    pltpu.make_async_copy(field_hbm.at[p, part], field_ref.at[p, part], sem).wait()
            forward_pair(c, channels, two(field_ref, p, c), fy_ref, scratch)
        forward_finish(channels, tz_ref, scratch, out_ref, rows_at(p, stride, ky_own))
        return carry

    lax.fori_loop(0, slab, body, 0)


def cell_copies(array_hbm, array_ref, sems, store=False):
    cuts = array_ref.shape[2] // 32

    def copy(n):
        at = (n // cuts, slice(None), pl.ds(32 * (n % cuts), 32))
        ends = (array_hbm.at[at], array_ref.at[at])
        return pltpu.make_async_copy(*(ends[::-1] if store else ends), sems.at[n])

    return copy, array_ref.shape[0] * cuts


def mix_field(field_hbm, out_hbm, cells_ref, kron, offset, in_sems, out_sems, prepare):
    load, count = cell_copies(field_hbm, cells_ref, in_sems)
    store, _ = cell_copies(out_hbm, cells_ref, out_sems, True)
    for n in range(count):
        load(n).start()
    prepare()
    cuts = cells_ref.shape[2] // 32

    def body(n, carry):
        load(n).wait()
        for e in range(2):
            start = pl.multiple_of(32 * (n % cuts) + 16 * e, 16)
            high, low = split(cell_tile(cells_ref, n // cuts, start))
            values = mix_cells(kron, high, low)
            put_tile(cells_ref, n // cuts, start, values if offset is None else values + offset[...])
        store(n).start()
        return carry

    lax.fori_loop(0, count, body, 0)
    for n in range(count):
        store(n).wait()


def point_kernel(field_hbm, weight_ref, bias_ref, out_hbm, cells_ref, kron, bias_wide, in_sems, out_sems):
    channels = cells_ref.shape[1]

    def prepare():
        spread_weight(jnp.transpose(weight_ref[...]), kron)
        row = lax.broadcasted_iota(jnp.int32, (8 * channels, channels), 0) // 8
        column = lax.broadcasted_iota(jnp.int32, (8 * channels, channels), 1)
        picked = jnp.where(row == column, bias_ref[...], 0.0)
        bias_wide[...] = jnp.broadcast_to(jnp.sum(picked, axis=1, keepdims=True), bias_wide.shape)

    mix_field(field_hbm, out_hbm, cells_ref, kron, bias_wide, in_sems, out_sems, prepare)


def quad_rows(ref, nx, lines, u):
    return jnp.concatenate([ref[pl.ds(2 * u + part, nx, stride=lines), :] for part in range(2)], axis=0)


def data_rows(ref, nx, lines, u):
    high, low = split(jnp.transpose(quad_rows(ref, nx, lines, u)))
    return jnp.concatenate([high, low, high], axis=1)


def weight_loads(weight_hbm, weight_ref, table_pairs, sems):
    parts = [slice(256 * t, 256 * t + 256) for t in range(4)]
    pairs = table_pairs + [(weight_hbm.at[:, :, :, part], weight_ref.at[:, :, :, part]) for part in parts]
    copies = transfers(pairs, sems)
    for copy in copies:
        copy.start()
    return copies[: len(table_pairs)], copies[len(table_pairs) :]


def mix_kernel(
    nx, lines, in_ref, weight_hbm, fx_hbm, inv_hbm, out_ref, weight_ref, fx_ref, inv_ref, left, modes, sums, sems
):
    pairs = weight_ref.shape[0]
    wide = KX * 32
    tables, loads = weight_loads(weight_hbm, weight_ref, [(fx_hbm, fx_ref), (inv_hbm, inv_ref)], sems)
    for u in range(pairs // 4):
        left[128 * u : 128 * u + 128, :] = data_rows(in_ref, nx, lines, u)
    for copy in tables:
        copy.wait()
    for t in range(4):
        cols = slice(256 * t, 256 * t + 256)
        late = slice(wide + 256 * t, wide + 256 * t + 256)
        modes[:, :256] = dot(left[...], fx_ref[:, cols])
        modes[:, 256:] = dot(left[...], fx_ref[:, late])
        loads[t].wait()

        def body(pair, carry):
            rows = pl.ds(pl.multiple_of(32 * pair, 32), 32)
            real, imag = modes[rows, :256], modes[rows, 256:]
            w_real, w_imag = weight_ref[pair, 0, :, cols], weight_ref[pair, 1, :, cols]
            products = (real * w_real - imag * w_imag, imag * w_real + real * w_imag)
            for part in range(2):
                total = jnp.sum(products[part].reshape(4, 8, 256), axis=0)
                for e in range(2):
                    base = pl.multiple_of((2 * pair + part) * 64 + 8 * (2 * t + e), 8)
                    sums[pl.ds(base, 8), :] = total[:, 128 * e : 128 * e + 128]
            return carry

        lax.fori_loop(0, pairs, body, 0, unroll=4)
    for u in range(pairs // 4):
        tiles = [[], []]
        for j in range(4):
            for part in range(2):
                base = (2 * (4 * u + j) + part) * 64
                found = [sums[pl.ds(base + s, 8, stride=8), :] for s in range(8)]
                while len(found) > 1:
                    found = [found[k] + found[k + 1] for k in range(0, len(found), 2)]
                tiles[part].append(found[0])
        mixed = jnp.concatenate(group_transpose(tiles[0]) + group_transpose(tiles[1]), axis=0)
        planes = dot(inv_ref[...], data3(mixed))
        for part in range(2):
            out_ref[pl.ds(2 * u + part, nx, stride=lines), :] = planes[part * nx : (part + 1) * nx]


def gradient_tiles(grad_ref, gx_ref, nx, lines, u):
    grads = dot(gx_ref[...], data3(quad_rows(grad_ref, nx, lines, u)))
    tiles = []
    for part in range(2):
        tiles.append(group_transpose([grads[part * 32 + 8 * b : part * 32 + 8 * b + 8, :] for b in range(4)]))
    return tiles, grads


def gradient_rows(grad_ref, gx_ref, nx, lines, quads, rows_ref):
    bias = None
    for u in range(quads):
        tiles, grads = gradient_tiles(grad_ref, gx_ref, nx, lines, u)
        bias = grads[0:1, :] if u == 0 else bias
        for part in range(2):
            for j in range(4):
                base = (2 * (4 * u + j) + part) * 8
                rows_ref[base : base + 8, :] = tiles[part][j]
    return bias


def weight_grad_kernel(
    nx, lines, in_ref, grad_ref, fx_hbm, gx_hbm, out_hbm, fx_ref, gx_ref, left, modes, rows_ref, grads_ref, sems, table_sems
):
    pairs = grads_ref.shape[1]
    wide = KX * 32
    tables = transfers([(gx_hbm, gx_ref), (fx_hbm, fx_ref)], table_sems)
    for copy in tables:
        copy.start()
    for u in range(pairs // 4):
        left[128 * u : 128 * u + 128, :] = data_rows(in_ref, nx, lines, u)
    for copy in tables:
        copy.wait()
    gradient_rows(grad_ref, gx_ref, nx, lines, pairs // 4, rows_ref)
    parts = [(grads_ref.at[t], out_hbm.at[:, :, :, pl.ds(256 * t, 256)]) for t in range(4)]
    stores = transfers(parts, sems)
    for t in range(4):
        modes[:, :256] = dot(left[...], fx_ref[:, 256 * t : 256 * t + 256])
        modes[:, 256:] = dot(left[...], fx_ref[:, wide + 256 * t : wide + 256 * t + 256])

        def body(pair, carry):
            rows = pl.ds(pl.multiple_of(32 * pair, 32), 32)
            for e in range(2):
                g_real, g_imag = [
                    jnp.broadcast_to(rows_ref[pl.ds((2 * pair + part) * 8 + 2 * t + e, 1), :], (32, 128))
                    for part in range(2)
                ]
                cols = slice(128 * e, 128 * e + 128)
                real, imag = modes[rows, cols], modes[rows, 256 + 128 * e : 384 + 128 * e]
                grads_ref[t, pair, 0, :, cols] = real * g_real + imag * g_imag
                grads_ref[t, pair, 1, :, cols] = real * g_imag - imag * g_real
            return carry

        lax.fori_loop(0, pairs, body, 0, unroll=4)
        stores[t].start()
    for copy in stores:
        copy.wait()


def adjoint_kernel(
    slab,
    nx,
    lines,
    extra,
    grad_ref,
    weight_hbm,
    gx_hbm,
    inv_hbm,
    sums_ref,
    out_ref,
    weight_ref,
    gx_ref,
    inv_ref,
    rows_ref,
    soon,
    late,
    total,
    sems,
):
    pairs = weight_ref.shape[0]
    devices = nx // slab
    stride = slab * lines + extra
    tables, loads = weight_loads(weight_hbm, weight_ref, [(gx_hbm, gx_ref), (inv_hbm, inv_ref)], sems)
    for copy in tables:
        copy.wait()
    bias = gradient_rows(grad_ref, gx_ref, nx, lines, pairs // 4, rows_ref)
    total[...] = jnp.zeros_like(total)
    late[...] = jnp.zeros_like(late)
    early = lax.broadcasted_iota(jnp.int32, (32, 128), 1) % 32 < 16
    count = pairs // 2

    def products(t, first, target):
        for k in range(count):
            pair = first + k
            for e in range(2):
                cols = pl.ds(pl.multiple_of(256 * t + 128 * e, 128), 128)
                g_real, g_imag = [
                    jnp.broadcast_to(rows_ref[pl.ds((2 * pair + part) * 8 + 2 * t + e, 1), :], (32, 128))
                    for part in range(2)
                ]
                w_real, w_imag = weight_ref[pair, 0, :, cols], weight_ref[pair, 1, :, cols]
                real = g_real * w_real + g_imag * w_imag
                imag = g_imag * w_real - g_real * w_imag
                folded = jnp.where(early, real + pltpu.roll(real, 112, 1), imag + pltpu.roll(imag, 16, 1))
                high, low = split(folded)
                target[32 * k : 32 * k + 32, 128 * e : 128 * e + 128] = high
                target[32 * k : 32 * k + 32, 256 + 128 * e : 384 + 128 * e] = low

    def gather(t, source, first):
        table = inv_ref[pl.ds(pl.multiple_of(256 * t, 256), 256), :]
        rows = slice(32 * first, 32 * (first + count))
        total[rows, :] += dot(source[:, :256], table) + dot(source[:, 256:], table)

    def body(t, carry):
        part = pl.ds(pl.multiple_of(256 * t, 256), 256)
        pltpu.make_async_copy(
            weight_hbm.at[:, :, :, part], weight_ref.at[:, :, :, part], sems.at[len(tables) + t]
        ).wait()
        gather(jnp.maximum(t - 1, 0), late, count)
        products(t, 0, soon)
        gather(t, soon, 0)
        products(t, count, late)
        return carry

    lax.fori_loop(0, 4, body, 0)
    gather(3, late, count)
    lane = lax.broadcasted_iota(jnp.int32, (nx, 128), 1)
    carried = lax.axis_index("space") == 0
    for u in range(pairs // 4):
        both = total[128 * u : 128 * u + 128, :]
        planes = jnp.transpose(both[:, : 2 * nx] + both[:, 2 * nx :])
        real, imag = planes[:nx], planes[nx:]
        if u == 0:
            imag = jnp.where((lane < 32) & carried, jnp.broadcast_to(bias, (nx, 128)), imag)
        for part, values in ((0, real), (1, imag)):
            for p in range(slab):
                out_ref[pl.ds(p * lines + 2 * u + part, devices, stride=stride), :] = values[
                    p * devices : (p + 1) * devices
                ]
    for d in range(devices):
        out_ref[d * stride + slab * lines : d * stride + slab * lines + extra, :] = sums_ref[...]


def middle_kernel(
    stride,
    ky_own,
    in_ref,
    point_ref,
    cot_ref,
    tzi_ref,
    ty_ref,
    fy_ref,
    tzf_ref,
    output_hbm,
    gpre_hbm,
    spec_ref,
    output_ref,
    gpre_ref,
    scratch,
    sems,
):
    slab, channels = point_ref.shape[:2]
    rate = math.sqrt(2.0 / math.pi)

    def stores(p, g):
        part = pl.ds(8 * g, 8)
        pairs = ((output_ref, output_hbm), (gpre_ref, gpre_hbm))
        return [
            pltpu.make_async_copy(src.at[p, part], dst.at[p, part], sems.at[k, p, g])
            for k, (src, dst) in enumerate(pairs)
        ]

    def body(p, carry):
        row_of = rows_at(p, stride, ky_own)

        def emit(c, spectral):
            values = spectral + two(point_ref, p, c)
            square = values * values
            half = 0.5 + 0.5 * jnp.tanh(values * (rate + (0.044715 * rate) * square))
            result = values * half
            put_two(output_ref, p, c, result)
            slope = half + result * (1.0 - half) * (2.0 * rate + (6 * 0.044715 * rate) * square)
            put_two(gpre_ref, p, c, two(cot_ref, p, c) * slope)

        def after(h):
            for g in range(2):
                for copy in stores(p, 2 * h + g):
                    copy.start()

        inverse_plane(in_ref, row_of, tzi_ref, ty_ref, scratch, channels, emit, after)

        def pair(k, carry):
            forward_pair(2 * k, channels, two(gpre_ref, p, 2 * k), fy_ref, scratch)
            return carry

        lax.fori_loop(0, channels // 2, pair, 0, unroll=8)
        forward_finish(channels, tzf_ref, scratch, spec_ref, row_of)
        return carry

    lax.fori_loop(0, slab, body, 0)
    for p in range(slab):
        for g in range(channels // 8):
            for copy in stores(p, g):
                copy.wait()


def back_kernel(gpre_hbm, weight_ref, out_hbm, cells_ref, kron, in_sems, out_sems):
    prepare = lambda: spread_weight(weight_ref[...], kron)
    mix_field(gpre_hbm, out_hbm, cells_ref, kron, None, in_sems, out_sems, prepare)


def outer_kernel(field_hbm, gpre_hbm, sums_ref, field_ref, gpre_ref, outer, field_sems, gpre_sems):
    channels = field_ref.shape[1]
    load, count = cell_copies(field_hbm, field_ref, field_sems)
    load_gpre, _ = cell_copies(gpre_hbm, gpre_ref, gpre_sems)
    for n in range(count):
        load(n).start()
        load_gpre(n).start()
    outer[...] = jnp.zeros_like(outer)
    cuts = field_ref.shape[2] // 32

    def body(n, carry):
        load(n).wait()
        load_gpre(n).wait()
        total = outer[...]
        for e in range(2):
            start = pl.multiple_of(32 * (n % cuts) + 16 * e, 16)
            high, low = split(cell_tile(field_ref, n // cuts, start))
            g_high, g_low = split(cell_tile(gpre_ref, n // cuts, start))
            both = dot(jnp.concatenate([high, low], axis=0), g_high, NT)
            total = total + (both[: 8 * channels] + both[8 * channels :] + dot(high, g_low, NT))
        outer[...] = total
        return carry

    lax.fori_loop(0, count, body, 0)
    row = lax.broadcasted_iota(jnp.int32, outer.shape, 0) % 8
    column = lax.broadcasted_iota(jnp.int32, outer.shape, 1) % 8
    kept = jnp.where(row == column, outer[...], 0.0)
    kept = jnp.sum(kept.reshape(channels, 8, 8 * channels), axis=1)
    row = lax.broadcasted_iota(jnp.int32, (8 * channels, channels), 0) // 8
    column = lax.broadcasted_iota(jnp.int32, (8 * channels, channels), 1)
    pick = (row == column).astype(f32)
    small = lax.dot_general(
        kept, pick, (((1,), (0,)), ((), ())), precision=lax.Precision.HIGHEST, preferred_element_type=f32
    )
    sums_ref[...] = jnp.concatenate([small[8 * g : 8 * g + 8] for g in range(4)], axis=1)


def last_kernel(
    stride,
    ky_own,
    devices,
    sums_at,
    scales,
    in_ref,
    part_ref,
    back_hbm,
    tzi_hbm,
    ty_hbm,
    out_hbm,
    point_ref,
    bias_ref,
    scratch,
    cells_ref,
    tzi_ref,
    ty_ref,
    in_sems,
    out_sems,
    table_sems,
):
    slab, channels = cells_ref.shape[:2]
    groups = channels // 8
    places = [(p, c) for p in range(slab) for c in chunks(channels)]
    tables = transfers([(tzi_hbm, tzi_ref), (ty_hbm, ty_ref)], table_sems)
    loads = transfers([(back_hbm.at[at], cells_ref.at[at]) for at in places], in_sems)
    stores = transfers([(cells_ref.at[at], out_hbm.at[at]) for at in places], out_sems)

    def one(p, g, store):
        at = (p, pl.ds(8 * g, 8))
        if store:
            return pltpu.make_async_copy(cells_ref.at[at], out_hbm.at[at], out_sems.at[p * groups + g])
        return pltpu.make_async_copy(back_hbm.at[at], cells_ref.at[at], in_sems.at[p * groups + g])

    for copy in tables + loads:
        copy.start()
    step, first = sums_at
    total = part_ref[first : first + 8, :]
    for d in range(1, devices):
        total = total + part_ref[d * step + first : d * step + first + 8, :]
    for g in range(4):
        point_ref[8 * g : 8 * g + 8, :] = total[:, 32 * g : 32 * g + 32] * scales[0]
    bias_ref[...] = in_ref[1:2, 0:32] * scales[1]
    for copy in tables:
        copy.wait()

    def body(p, carry):
        def before(h):
            one(p, 2 * h, False).wait()
            one(p, 2 * h + 1, False).wait()

        def emit(c, values):
            put_two(cells_ref, p, c, two(cells_ref, p, c) + values)

        def after(h):
            one(p, 2 * h, True).start()
            one(p, 2 * h + 1, True).start()

        inverse_plane(
            in_ref, rows_at(p, stride, ky_own), tzi_ref, ty_ref, scratch, channels, emit, after, before
        )
        return carry

    lax.fori_loop(0, slab, body, 0)
    for copy in stores:
        copy.wait()


VM = pl.BlockSpec(memory_space=pltpu.VMEM)
HBM = pl.BlockSpec(memory_space=pltpu.HBM)


def params(megabytes):
    return pltpu.CompilerParams(vmem_limit_bytes=megabytes * MIB)


def cost(microseconds):
    return pl.CostEstimate(flops=0, bytes_accessed=int(microseconds * 3e6), transcendentals=0)


def keep(array):
    return pltpu.VMEM(array.shape, array.dtype)


def far(array):
    return pltpu.with_memory_space_constraint(array, pltpu.HBM)


def near(array):
    return pltpu.with_memory_space_constraint(array, pltpu.VMEM)


def per_device(flow_field, cotangent, spec_weight, point_weight, pointwise_bias):
    slab, channels, ny, nz = flow_field.shape
    devices = lax.axis_size("space")
    nx = slab * devices
    pair_local = spec_weight.shape[0]
    assert pair_local % MODES == 0 or slab == 1
    assert channels == 32 and nz == 128 and pair_local % 4 == 0
    ky_own = max(1, pair_local // MODES)
    lines = pair_local // 2
    rows = nx * lines
    block = slab * lines
    stride = slab * ky_own * 8
    extra = 8
    wide = KX * channels
    fwd_scale = float(nx * ny * nz) ** (-0.5)
    inv_scale = float(4 * MODES**3) ** (-0.5)

    fy_high, fy_low = halves(y_table(ny))
    fy = np.concatenate(
        [np.concatenate([fy_high, fy_high], axis=1), np.concatenate([fy_low, fy_low], axis=1)], axis=0
    )
    fy = jnp.asarray(fy)
    tz_first = jnp.asarray(np.concatenate(halves(z_table(nz, 1.0, 1.0)), axis=0))
    ty = jnp.asarray(stack3(y_table(ny).T, 1))
    tz_grad = jnp.asarray(np.concatenate(halves(z_table(nz, inv_scale, 2.0)), axis=0))
    tzi_out = jnp.asarray(stack3(z_table(nz, inv_scale, 2.0), 0))
    tzi_grad = jnp.asarray(stack3(z_table(nz, fwd_scale, 1.0), 0))
    fx = x_forward_table(nx, fwd_scale)
    fx_wide = jnp.asarray(np.repeat(stack3(fx, 0), channels, axis=1))
    gx = jnp.asarray(stack3(by_low(x_forward_table(nx, 1.0), 1).T, 1))
    inv = x_inverse_table(nx)
    inv_low = jnp.asarray(stack3(by_low(inv, 1), 1))
    by_plane = inv.reshape(2, devices, slab, 2 * KX).transpose(0, 2, 1, 3).reshape(2 * nx, 2 * KX)
    inv_wide = np.concatenate(halves(by_plane), axis=0).reshape(4 * nx, 2, KX).transpose(2, 1, 0)
    inv_wide = jnp.asarray(np.repeat(inv_wide.reshape(2 * KX, 4 * nx), channels // 2, axis=0))

    line_shape = jax.ShapeDtypeStruct((rows, 128), f32)
    field_shape = pltpu.HBM(flow_field.shape, f32)
    mode_scratch = pltpu.VMEM((2 * KY * channels, nz), f32)
    kron_scratch = pltpu.VMEM((16 * channels, 8 * channels), bf16)
    chunk_count = slab * (channels // 8)
    chunk_sems = pltpu.SemaphoreType.DMA((chunk_count,))
    pair_sems = pltpu.SemaphoreType.DMA((2,))
    cell_sems = pltpu.SemaphoreType.DMA((slab * (ny // 32),))

    def exchange(lines_out):
        blocks = lines_out.reshape(devices, -1, 128)
        return lax.all_to_all(blocks, "space", split_axis=0, concat_axis=0, tiled=True)

    first = pl.pallas_call(
        functools.partial(first_kernel, stride, ky_own),
        in_specs=[HBM, HBM, HBM],
        out_specs=VM,
        out_shape=line_shape,
        scratch_shapes=[
            pltpu.VMEM(flow_field.shape, f32),
            keep(fy),
            keep(tz_first),
            mode_scratch,
            chunk_sems,
            pair_sems,
        ],
        compiler_params=params(16),
        cost_estimate=cost(4),
        name="field_forward",
    )(far(flow_field), far(fy), far(tz_first))
    spec_x = exchange(first).reshape(rows, 128)

    bias = pointwise_bias.reshape(1, channels)
    pointwise = pl.pallas_call(
        point_kernel,
        in_specs=[HBM, VM, VM],
        out_specs=HBM,
        out_shape=field_shape,
        scratch_shapes=[
            keep(flow_field),
            kron_scratch,
            pltpu.VMEM((8 * channels, 2 * nz), f32),
            cell_sems,
            cell_sems,
        ],
        compiler_params=params(16),
        cost_estimate=cost(6),
        name="pointwise",
    )(far(flow_field), point_weight, bias)

    spec_x, pointwise = lax.optimization_barrier((spec_x, pointwise))
    mixed = pl.pallas_call(
        functools.partial(mix_kernel, nx, lines),
        in_specs=[VM, HBM, HBM, HBM],
        out_specs=VM,
        out_shape=line_shape,
        scratch_shapes=[
            keep(spec_weight),
            keep(fx_wide),
            keep(inv_low),
            pltpu.VMEM((32 * pair_local, 6 * nx), bf16),
            pltpu.VMEM((32 * pair_local, 512), f32),
            pltpu.VMEM((128 * pair_local, 128), f32),
            pltpu.SemaphoreType.DMA((6,)),
        ],
        compiler_params=params(24),
        cost_estimate=cost(5),
        name="mode_mix",
    )(spec_x, far(spec_weight), far(fx_wide), far(inv_low))
    mixed = exchange(mixed).reshape(rows, 128)

    output, gpre, grad_lines = pl.pallas_call(
        functools.partial(middle_kernel, stride, ky_own),
        in_specs=[VM] * 7,
        out_specs=[HBM, HBM, VM],
        out_shape=[field_shape, field_shape, line_shape],
        scratch_shapes=[
            pltpu.VMEM(flow_field.shape, f32),
            pltpu.VMEM(flow_field.shape, f32),
            mode_scratch,
            pltpu.SemaphoreType.DMA((2, slab, channels // 8)),
        ],
        compiler_params=params(24),
        cost_estimate=cost(10),
        name="middle",
    )(mixed, near(pointwise), near(cotangent), near(tzi_out), near(ty), near(fy), near(tz_grad))
    grad_x = exchange(grad_lines).reshape(rows, 128)

    local_sums = pl.pallas_call(
        outer_kernel,
        in_specs=[HBM, HBM],
        out_specs=VM,
        out_shape=jax.ShapeDtypeStruct((extra, 128), f32),
        scratch_shapes=[
            keep(flow_field),
            keep(flow_field),
            pltpu.VMEM((8 * channels, 8 * channels), f32),
            cell_sems,
            cell_sems,
        ],
        compiler_params=params(16),
        cost_estimate=cost(6),
        name="outer_sums",
    )(far(flow_field), far(gpre))

    sent = devices * (block + extra)
    grad_mixed = pl.pallas_call(
        functools.partial(adjoint_kernel, slab, nx, lines, extra),
        in_specs=[VM, HBM, HBM, HBM, VM],
        out_specs=VM,
        out_shape=jax.ShapeDtypeStruct((sent, 128), f32),
        scratch_shapes=[
            keep(spec_weight),
            keep(gx),
            keep(inv_wide),
            pltpu.VMEM((16 * pair_local, 128), f32),
            pltpu.VMEM((16 * pair_local, 512), bf16),
            pltpu.VMEM((16 * pair_local, 512), bf16),
            pltpu.VMEM((32 * pair_local, 4 * nx), f32),
            pltpu.SemaphoreType.DMA((6,)),
        ],
        compiler_params=params(24),
        cost_estimate=cost(6),
        name="mode_adjoint",
    )(grad_x, far(spec_weight), far(gx), far(inv_wide), local_sums)
    grad_spec = pl.pallas_call(
        functools.partial(weight_grad_kernel, nx, lines),
        in_specs=[VM, VM, HBM, HBM],
        out_specs=HBM,
        out_shape=pltpu.HBM(spec_weight.shape, f32),
        scratch_shapes=[
            keep(fx_wide),
            keep(gx),
            pltpu.VMEM((32 * pair_local, 6 * nx), bf16),
            pltpu.VMEM((32 * pair_local, 512), f32),
            pltpu.VMEM((16 * pair_local, 128), f32),
            pltpu.VMEM((4, pair_local, 2, channels, wide // 4), f32),
            pltpu.SemaphoreType.DMA((4,)),
            pair_sems,
        ],
        compiler_params=params(24),
        cost_estimate=cost(6),
        name="weight_grad",
    )(spec_x, grad_x, far(fx_wide), far(gx))

    gpre, grad_mixed = lax.optimization_barrier((gpre, grad_mixed))
    received = exchange(grad_mixed)
    back = pl.pallas_call(
        back_kernel,
        in_specs=[HBM, VM],
        out_specs=HBM,
        out_shape=field_shape,
        scratch_shapes=[keep(flow_field), kron_scratch, cell_sems, cell_sems],
        compiler_params=params(16),
        cost_estimate=cost(6),
        name="pointwise_back",
    )(far(gpre), point_weight)

    if pair_local >= MODES:
        lines_in = sums_in = received.reshape(sent, 128)
        stride_in, sums_at = stride + extra, (stride + extra, stride)
    else:
        lines_in = received[:, :block].reshape(rows, 128)
        sums_in = received[:, block:].reshape(devices * extra, 128)
        stride_in, sums_at = stride, (extra, 0)
    grad_field, grad_point, grad_bias = pl.pallas_call(
        functools.partial(
            last_kernel, stride_in, ky_own, devices, sums_at, (fwd_scale, fwd_scale / inv_scale)
        ),
        in_specs=[VM, VM, HBM, HBM, HBM],
        out_specs=[HBM, VM, VM],
        out_shape=[
            field_shape,
            jax.ShapeDtypeStruct((channels, channels), f32),
            jax.ShapeDtypeStruct((1, channels), f32),
        ],
        scratch_shapes=[
            mode_scratch,
            pltpu.VMEM(flow_field.shape, f32),
            keep(tzi_grad),
            keep(ty),
            chunk_sems,
            chunk_sems,
            pair_sems,
        ],
        compiler_params=params(16),
        cost_estimate=cost(8),
        name="field_inverse",
    )(lines_in, sums_in, far(back), far(tzi_grad), far(ty))

    return output, grad_field, grad_spec, grad_point, grad_bias.reshape(channels)


def solution(mesh):
    cells = P(("group", "space"), None, None, None)
    return jax.shard_map(
        per_device,
        mesh=mesh,
        in_specs=(cells, cells, P("space", None, None, None), P(), P()),
        out_specs=(cells, cells, cells, P("group", None), P("group")),
        check_vma=False,
    )
```

```python
import functools
import math

import jax
import jax.numpy as jnp
import ml_dtypes
import numpy as np
from jax import lax
from jax.experimental import pallas as pl
from jax.experimental.pallas import tpu as pltpu
from jax.sharding import PartitionSpec as P

MODES = 16
KY = 2 * MODES
KX = 2 * MODES
MIB = 1024 * 1024
NT = (((1,), (1,)), ((), ()))
TN = (((0,), (0,)), ((), ()))
f32 = jnp.float32
bf16 = jnp.bfloat16


def signed(n):
    j = np.arange(n)
    return np.where(j < n // 2, j, j - n)


def phases(positions, waves, length):
    angle = ((positions[:, None] * waves[None, :]) % length) * (2.0 * math.pi / length)
    return np.cos(angle), np.sin(angle)


def halves(table):
    table = np.asarray(table, np.float32)
    high = table.astype(ml_dtypes.bfloat16)
    low = (table - high.astype(np.float32)).astype(ml_dtypes.bfloat16)
    return high, low


def stack3(table, axis):
    high, low = halves(table)
    return np.concatenate([high, high, low], axis=axis)


def y_table(ny):
    cos, sin = phases(np.arange(ny), np.arange(MODES + 1), ny)
    order = [MODES] + list(range(1, MODES))
    return np.concatenate([cos.T[:MODES], -sin.T[order], cos.T[MODES:], np.zeros((7, ny))], axis=0)


def z_table(nz, scale, factor):
    cos, sin = phases(np.arange(nz), np.arange(MODES), nz)
    weight = scale * np.where(np.arange(MODES) == 0, 1.0, factor)
    cos, sin = cos.T * weight[:, None], sin.T * weight[:, None]
    real = np.concatenate([cos, sin], axis=1)
    imag = np.concatenate([-sin, cos], axis=1)
    both = np.stack([real, imag], axis=1).reshape(4, 4, 2, 2 * nz)
    return both.transpose(1, 0, 2, 3).reshape(2 * MODES, 2 * nz)


def x_forward_table(nx, scale):
    cos, sin = phases(np.arange(nx), signed(KX), nx)
    top = np.concatenate([cos, -sin], axis=1)
    bottom = np.concatenate([sin, cos], axis=1)
    return scale * np.concatenate([top, bottom], axis=0)


def x_inverse_table(nx):
    cos, sin = phases(np.arange(nx), signed(KX), nx)
    top = np.concatenate([cos, -sin], axis=1)
    bottom = np.concatenate([sin, cos], axis=1)
    return np.concatenate([top, bottom], axis=0)


def by_low(table, axis):
    order = np.arange(2 * KX).reshape(2, KX // 4, 4).transpose(0, 2, 1).reshape(-1)
    return np.take(table, order, axis=axis)


def split(values):
    high = values.astype(bf16)
    low = (values - high.astype(f32)).astype(bf16)
    return high, low


def data3(values):
    high, low = split(values)
    return jnp.concatenate([high, low, high], axis=0)


def dot(left, right, dims=(((1,), (0,)), ((), ()))):
    return lax.dot_general(left, right, dims, preferred_element_type=f32)


def group_transpose(tiles):
    group = lax.broadcasted_iota(jnp.int32, tiles[0].shape, 1) // 32
    result = []
    for m in range(4):
        moved = [pltpu.roll(tiles[n], ((n - m) * 32) % 128, 1) if n != m else tiles[n] for n in range(4)]
        low = jnp.where(group == 0, moved[0], moved[1])
        high = jnp.where(group == 2, moved[2], moved[3])
        result.append(jnp.where(group < 2, low, high))
    return result


def block_row(ky, plane, stride, ky_own):
    return (ky // ky_own) * stride + (plane * ky_own + ky % ky_own) * 8


COS16 = MODES * 32
SINES = COS16 + 128
SLOTS = SINES + MODES * 32


def forward_pair(c, channels, pair, fy_ref, scratch):
    nz = scratch.shape[1]
    high, low = split(pair)
    both = dot(fy_ref[...], jnp.concatenate([high, low], axis=0))
    half = both[: 2 * MODES + 8] + both[2 * MODES + 8 :]
    for e in range(2):
        side = slice(e * nz, (e + 1) * nz)
        scratch[pl.ds(c + e, MODES, stride=channels), :] = half[:MODES, side]
        scratch[pl.ds(SINES + c + e, MODES, stride=channels), :] = half[MODES : 2 * MODES, side]
        scratch[pl.ds(COS16 + c + e, 1), :] = half[2 * MODES : 2 * MODES + 1, side]


def forward_finish(channels, tz_ref, scratch, out_ref, row_of):
    count = 2 * MODES
    sides = []
    for part, rows in ((0, slice(0, SINES)), (1, slice(SINES, SLOTS))):
        both = dot(tz_ref[2 * part * count : 2 * (part + 1) * count, :], jnp.concatenate(split(scratch[rows, :]), axis=1), NT)
        sides.append(both[:count] + both[count:])
    first = lax.broadcasted_iota(jnp.int32, (8, 128), 1) < 32
    for q in range(MODES // 4):
        tiles = ([], [])
        for j in range(4):
            rows, cols = slice(8 * j, 8 * j + 8), slice(q * 128, (q + 1) * 128)
            even, odd = sides[0][rows, cols], sides[1][rows, cols]
            last = sides[0][rows, COS16 : COS16 + 128]
            tiles[0].append(jnp.where(first, even, even + odd) if q == 0 else even + odd)
            tiles[1].append((jnp.where(first, last, even) if q == 0 else even) - odd)
        for sign in range(2):
            for e, tile in enumerate(group_transpose(tiles[sign])):
                k = 4 * q + e
                ky = k if sign == 0 else (KY - k if k else MODES)
                out_ref[pl.ds(row_of(ky), 8), :] = tile


def inverse_plane(in_ref, row_of, tz_ref, ty_ref, scratch, channels, emit, after, before=lambda h: None):
    nz = scratch.shape[1]
    tile = lambda ky: in_ref[pl.ds(row_of(ky), 8), :]
    columns = ([[] for _ in range(4)], [[] for _ in range(4)])
    for q in range(MODES // 4):
        sums, differences = [], []
        for k in range(4 * q, 4 * q + 4):
            sums.append(tile(k) + tile(KY - k) if k else tile(0))
            differences.append(tile(k) - tile(KY - k) if k else -tile(MODES))
        for sign, tiles in ((0, sums), (1, differences)):
            for j, found in enumerate(group_transpose(tiles)):
                columns[sign][j].append(found)
    for j, found in enumerate(group_transpose([tile(MODES)] * 4)):
        columns[0][j].append(found)
    depth = tz_ref.shape[0] // 2
    for sign, rows in ((0, slice(0, SINES)), (1, slice(SINES, SLOTS))):
        data = jnp.concatenate([jnp.concatenate(c, axis=1) for c in columns[sign]], axis=0)
        scratch[rows, :] = dot(data3(data), tz_ref[sign * depth : (sign + 1) * depth, :], TN)
    at = lax.broadcasted_iota(jnp.int32, (8, 2 * nz), 0)
    slant = jnp.where((at == 3) | (at == 5) | (at == 4), -1.0, 1.0) * jnp.where(at % 2 == 1, math.sqrt(0.5), 1.0)
    wave = jnp.where(at % 4 == 2, 0.0, slant)

    def group(h, carry):
        before(h)
        for k in range(0, 16, 2):
            c = 16 * h + k
            sides, tops = [], []
            for e in range(2):
                parts = [scratch[pl.ds(first + c + e, MODES, stride=channels), :] for first in (0, SINES)]
                sides.append(jnp.concatenate(parts, axis=0))
                tops.append(scratch[pl.ds(COS16 + c + e, 1), :])
            pair = dot(ty_ref[...], data3(jnp.concatenate(sides, axis=1)))
            extra = wave * jnp.concatenate(tops, axis=1)
            emit(c, pair + jnp.concatenate([extra] * (pair.shape[0] // 8), axis=0))
        after(h)
        return carry

    lax.fori_loop(0, channels // 16, group, 0)


def two(ref, p, c):
    return jnp.concatenate([ref[p, c], ref[p, c + 1]], axis=1)


def put_two(ref, p, c, values):
    nz = values.shape[1] // 2
    ref[p, c], ref[p, c + 1] = values[:, :nz], values[:, nz:]


def spread_weight(weight, kron_ref):
    size = weight.shape[0]
    row = lax.broadcasted_iota(jnp.int32, (8 * size, size), 0) // 8
    column = lax.broadcasted_iota(jnp.int32, (8 * size, size), 1)
    expand = (row == column).astype(f32)
    tall = lax.dot_general(
        expand, weight, (((1,), (0,)), ((), ())), precision=lax.Precision.HIGHEST, preferred_element_type=f32
    )
    wide = lax.dot_general(tall, expand, NT, precision=lax.Precision.HIGHEST, preferred_element_type=f32)
    row = lax.broadcasted_iota(jnp.int32, wide.shape, 0) % 8
    column = lax.broadcasted_iota(jnp.int32, wide.shape, 1) % 8
    kron_ref[...] = jnp.concatenate(split(jnp.where(row == column, wide, 0.0)), axis=0)


def cell_tile(ref, plane, start):
    sides = []
    for e in range(2):
        piece = ref[plane, :, pl.ds(start + 8 * e, 8), :]
        sides.append(piece.reshape(piece.shape[0] * 8, piece.shape[2]))
    return jnp.concatenate(sides, axis=1)


def put_tile(ref, plane, start, tile):
    channels, nz = ref.shape[1], ref.shape[3]
    for e in range(2):
        ref[plane, :, pl.ds(start + 8 * e, 8), :] = tile[:, e * nz : (e + 1) * nz].reshape(channels, 8, nz)


def mix_cells(kron_ref, high, low):
    size = high.shape[0]
    both = dot(kron_ref[...], high)
    return both[:size] + both[size:] + dot(kron_ref[:size, :], low)


def rows_at(plane, stride, ky_own):
    def row_of(ky):
        row = block_row(ky, plane, stride, ky_own)
        return row if isinstance(row, int) else pl.multiple_of(row, 8)

    return row_of


def transfers(pairs, sems):
    return [pltpu.make_async_copy(src, dst, sems.at[i]) for i, (src, dst) in enumerate(pairs)]


def chunks(channels):
    return [slice(8 * g, 8 * g + 8) for g in range(channels // 8)]


def first_kernel(stride, ky_own, field_hbm, fy_hbm, tz_hbm, out_ref, field_ref, fy_ref, tz_ref, scratch, sems, table_sems):
    slab, channels = field_ref.shape[:2]
    tables = transfers([(fy_hbm, fy_ref), (tz_hbm, tz_ref)], table_sems)
    parts = [(field_hbm.at[p, c], field_ref.at[p, c]) for p in range(slab) for c in chunks(channels)]
    for copy in tables + transfers(parts, sems):
        copy.start()
    for copy in tables:
        copy.wait()

    def body(p, carry):
        for c in range(0, channels, 2):
            if c % 16 == 0:
                for g in (c // 8, c // 8 + 1):
                    part = slice(8 * g, 8 * g + 8)
                    sem = sems.at[p * (channels // 8) + g]
                    pltpu.make_async_copy(field_hbm.at[p, part], field_ref.at[p, part], sem).wait()
            forward_pair(c, channels, two(field_ref, p, c), fy_ref, scratch)
        forward_finish(channels, tz_ref, scratch, out_ref, rows_at(p, stride, ky_own))
        return carry

    lax.fori_loop(0, slab, body, 0)


def cell_copies(array_hbm, array_ref, sems, store=False):
    cuts = array_ref.shape[2] // 32

    def copy(n):
        at = (n // cuts, slice(None), pl.ds(32 * (n % cuts), 32))
        ends = (array_hbm.at[at], array_ref.at[at])
        return pltpu.make_async_copy(*(ends[::-1] if store else ends), sems.at[n])

    return copy, array_ref.shape[0] * cuts


def mix_field(field_hbm, out_hbm, cells_ref, kron, offset, in_sems, out_sems, prepare):
    load, count = cell_copies(field_hbm, cells_ref, in_sems)
    store, _ = cell_copies(out_hbm, cells_ref, out_sems, True)
    for n in range(count):
        load(n).start()
    prepare()
    cuts = cells_ref.shape[2] // 32

    def body(n, carry):
        load(n).wait()
        for e in range(2):
            start = pl.multiple_of(32 * (n % cuts) + 16 * e, 16)
            high, low = split(cell_tile(cells_ref, n // cuts, start))
            values = mix_cells(kron, high, low)
            put_tile(cells_ref, n // cuts, start, values if offset is None else values + offset[...])
        store(n).start()
        return carry

    lax.fori_loop(0, count, body, 0)
    for n in range(count):
        store(n).wait()


def point_kernel(field_hbm, weight_ref, bias_ref, out_hbm, cells_ref, kron, bias_wide, in_sems, out_sems):
    channels = cells_ref.shape[1]

    def prepare():
        spread_weight(jnp.transpose(weight_ref[...]), kron)
        row = lax.broadcasted_iota(jnp.int32, (8 * channels, channels), 0) // 8
        column = lax.broadcasted_iota(jnp.int32, (8 * channels, channels), 1)
        picked = jnp.where(row == column, bias_ref[...], 0.0)
        bias_wide[...] = jnp.broadcast_to(jnp.sum(picked, axis=1, keepdims=True), bias_wide.shape)

    mix_field(field_hbm, out_hbm, cells_ref, kron, bias_wide, in_sems, out_sems, prepare)


def quad_rows(ref, nx, lines, u):
    return jnp.concatenate([ref[pl.ds(2 * u + part, nx, stride=lines), :] for part in range(2)], axis=0)


def data_rows(ref, nx, lines, u):
    high, low = split(jnp.transpose(quad_rows(ref, nx, lines, u)))
    return jnp.concatenate([high, low, high], axis=1)


def weight_loads(weight_hbm, weight_ref, table_pairs, sems):
    parts = [slice(256 * t, 256 * t + 256) for t in range(4)]
    pairs = table_pairs + [(weight_hbm.at[:, :, :, part], weight_ref.at[:, :, :, part]) for part in parts]
    copies = transfers(pairs, sems)
    for copy in copies:
        copy.start()
    return copies[: len(table_pairs)], copies[len(table_pairs) :]


def mix_kernel(
    nx, lines, in_ref, weight_hbm, fx_hbm, inv_hbm, out_ref, weight_ref, fx_ref, inv_ref, left, modes, sums, sems
):
    pairs = weight_ref.shape[0]
    wide = KX * 32
    tables, loads = weight_loads(weight_hbm, weight_ref, [(fx_hbm, fx_ref), (inv_hbm, inv_ref)], sems)
    for u in range(pairs // 4):
        left[128 * u : 128 * u + 128, :] = data_rows(in_ref, nx, lines, u)
    for copy in tables:
        copy.wait()
    for t in range(4):
        cols = slice(256 * t, 256 * t + 256)
        late = slice(wide + 256 * t, wide + 256 * t + 256)
        modes[:, :256] = dot(left[...], fx_ref[:, cols])
        modes[:, 256:] = dot(left[...], fx_ref[:, late])
        loads[t].wait()

        def body(pair, carry):
            rows = pl.ds(pl.multiple_of(32 * pair, 32), 32)
            real, imag = modes[rows, :256], modes[rows, 256:]
            w_real, w_imag = weight_ref[pair, 0, :, cols], weight_ref[pair, 1, :, cols]
            products = (real * w_real - imag * w_imag, imag * w_real + real * w_imag)
            for part in range(2):
                total = jnp.sum(products[part].reshape(4, 8, 256), axis=0)
                for e in range(2):
                    base = pl.multiple_of((2 * pair + part) * 64 + 8 * (2 * t + e), 8)
                    sums[pl.ds(base, 8), :] = total[:, 128 * e : 128 * e + 128]
            return carry

        lax.fori_loop(0, pairs, body, 0, unroll=4)
    for u in range(pairs // 4):
        tiles = [[], []]
        for j in range(4):
            for part in range(2):
                base = (2 * (4 * u + j) + part) * 64
                found = [sums[pl.ds(base + s, 8, stride=8), :] for s in range(8)]
                while len(found) > 1:
                    found = [found[k] + found[k + 1] for k in range(0, len(found), 2)]
                tiles[part].append(found[0])
        mixed = jnp.concatenate(group_transpose(tiles[0]) + group_transpose(tiles[1]), axis=0)
        planes = dot(inv_ref[...], data3(mixed))
        for part in range(2):
            out_ref[pl.ds(2 * u + part, nx, stride=lines), :] = planes[part * nx : (part + 1) * nx]


def gradient_tiles(grad_ref, gx_ref, nx, lines, u):
    grads = dot(gx_ref[...], data3(quad_rows(grad_ref, nx, lines, u)))
    tiles = []
    for part in range(2):
        tiles.append(group_transpose([grads[part * 32 + 8 * b : part * 32 + 8 * b + 8, :] for b in range(4)]))
    return tiles, grads


def gradient_rows(grad_ref, gx_ref, nx, lines, quads, rows_ref):
    bias = None
    for u in range(quads):
        tiles, grads = gradient_tiles(grad_ref, gx_ref, nx, lines, u)
        bias = grads[0:1, :] if u == 0 else bias
        for part in range(2):
            for j in range(4):
                base = (2 * (4 * u + j) + part) * 8
                rows_ref[base : base + 8, :] = tiles[part][j]
    return bias


def weight_grad_kernel(
    nx, lines, in_ref, grad_ref, fx_hbm, gx_hbm, out_hbm, fx_ref, gx_ref, left, modes, rows_ref, grads_ref, sems, table_sems
):
    pairs = grads_ref.shape[1]
    wide = KX * 32
    tables = transfers([(gx_hbm, gx_ref), (fx_hbm, fx_ref)], table_sems)
    for copy in tables:
        copy.start()
    for u in range(pairs // 4):
        left[128 * u : 128 * u + 128, :] = data_rows(in_ref, nx, lines, u)
    for copy in tables:
        copy.wait()
    gradient_rows(grad_ref, gx_ref, nx, lines, pairs // 4, rows_ref)
    parts = [(grads_ref.at[t], out_hbm.at[:, :, :, pl.ds(256 * t, 256)]) for t in range(4)]
    stores = transfers(parts, sems)
    for t in range(4):
        modes[:, :256] = dot(left[...], fx_ref[:, 256 * t : 256 * t + 256])
        modes[:, 256:] = dot(left[...], fx_ref[:, wide + 256 * t : wide + 256 * t + 256])

        def body(pair, carry):
            rows = pl.ds(pl.multiple_of(32 * pair, 32), 32)
            for e in range(2):
                g_real, g_imag = [
                    jnp.broadcast_to(rows_ref[pl.ds((2 * pair + part) * 8 + 2 * t + e, 1), :], (32, 128))
                    for part in range(2)
                ]
                cols = slice(128 * e, 128 * e + 128)
                real, imag = modes[rows, cols], modes[rows, 256 + 128 * e : 384 + 128 * e]
                grads_ref[t, pair, 0, :, cols] = real * g_real + imag * g_imag
                grads_ref[t, pair, 1, :, cols] = real * g_imag - imag * g_real
            return carry

        lax.fori_loop(0, pairs, body, 0, unroll=4)
        stores[t].start()
    for copy in stores:
        copy.wait()


def adjoint_kernel(
    slab,
    nx,
    lines,
    extra,
    grad_ref,
    weight_hbm,
    gx_hbm,
    inv_hbm,
    sums_ref,
    out_ref,
    weight_ref,
    gx_ref,
    inv_ref,
    rows_ref,
    soon,
    late,
    total,
    sems,
):
    pairs = weight_ref.shape[0]
    devices = nx // slab
    stride = slab * lines + extra
    tables, loads = weight_loads(weight_hbm, weight_ref, [(gx_hbm, gx_ref), (inv_hbm, inv_ref)], sems)
    for copy in tables:
        copy.wait()
    bias = gradient_rows(grad_ref, gx_ref, nx, lines, pairs // 4, rows_ref)
    total[...] = jnp.zeros_like(total)
    late[...] = jnp.zeros_like(late)
    early = lax.broadcasted_iota(jnp.int32, (32, 128), 1) % 32 < 16
    count = pairs // 2

    def products(t, first, target):
        for k in range(count):
            pair = first + k
            for e in range(2):
                cols = pl.ds(pl.multiple_of(256 * t + 128 * e, 128), 128)
                g_real, g_imag = [
                    jnp.broadcast_to(rows_ref[pl.ds((2 * pair + part) * 8 + 2 * t + e, 1), :], (32, 128))
                    for part in range(2)
                ]
                w_real, w_imag = weight_ref[pair, 0, :, cols], weight_ref[pair, 1, :, cols]
                real = g_real * w_real + g_imag * w_imag
                imag = g_imag * w_real - g_real * w_imag
                folded = jnp.where(early, real + pltpu.roll(real, 112, 1), imag + pltpu.roll(imag, 16, 1))
                high, low = split(folded)
                target[32 * k : 32 * k + 32, 128 * e : 128 * e + 128] = high
                target[32 * k : 32 * k + 32, 256 + 128 * e : 384 + 128 * e] = low

    def gather(t, source, first):
        table = inv_ref[pl.ds(pl.multiple_of(256 * t, 256), 256), :]
        rows = slice(32 * first, 32 * (first + count))
        total[rows, :] += dot(source[:, :256], table) + dot(source[:, 256:], table)

    def body(t, carry):
        part = pl.ds(pl.multiple_of(256 * t, 256), 256)
        pltpu.make_async_copy(
            weight_hbm.at[:, :, :, part], weight_ref.at[:, :, :, part], sems.at[len(tables) + t]
        ).wait()
        gather(jnp.maximum(t - 1, 0), late, count)
        products(t, 0, soon)
        gather(t, soon, 0)
        products(t, count, late)
        return carry

    lax.fori_loop(0, 4, body, 0)
    gather(3, late, count)
    lane = lax.broadcasted_iota(jnp.int32, (nx, 128), 1)
    carried = lax.axis_index("space") == 0
    for u in range(pairs // 4):
        both = total[128 * u : 128 * u + 128, :]
        planes = jnp.transpose(both[:, : 2 * nx] + both[:, 2 * nx :])
        real, imag = planes[:nx], planes[nx:]
        if u == 0:
            imag = jnp.where((lane < 32) & carried, jnp.broadcast_to(bias, (nx, 128)), imag)
        for part, values in ((0, real), (1, imag)):
            for p in range(slab):
                out_ref[pl.ds(p * lines + 2 * u + part, devices, stride=stride), :] = values[
                    p * devices : (p + 1) * devices
                ]
    for d in range(devices):
        out_ref[d * stride + slab * lines : d * stride + slab * lines + extra, :] = sums_ref[...]


def middle_kernel(
    stride,
    ky_own,
    in_ref,
    point_ref,
    cot_ref,
    tzi_ref,
    ty_ref,
    fy_ref,
    tzf_ref,
    output_hbm,
    gpre_hbm,
    spec_ref,
    output_ref,
    gpre_ref,
    scratch,
    sems,
):
    slab, channels = point_ref.shape[:2]
    rate = math.sqrt(2.0 / math.pi)

    def stores(p, g):
        part = pl.ds(8 * g, 8)
        pairs = ((output_ref, output_hbm), (gpre_ref, gpre_hbm))
        return [
            pltpu.make_async_copy(src.at[p, part], dst.at[p, part], sems.at[k, p, g])
            for k, (src, dst) in enumerate(pairs)
        ]

    def body(p, carry):
        row_of = rows_at(p, stride, ky_own)

        def emit(c, spectral):
            values = spectral + two(point_ref, p, c)
            square = values * values
            half = 0.5 + 0.5 * jnp.tanh(values * (rate + (0.044715 * rate) * square))
            result = values * half
            put_two(output_ref, p, c, result)
            slope = half + result * (1.0 - half) * (2.0 * rate + (6 * 0.044715 * rate) * square)
            put_two(gpre_ref, p, c, two(cot_ref, p, c) * slope)

        def after(h):
            for g in range(2):
                for copy in stores(p, 2 * h + g):
                    copy.start()

        inverse_plane(in_ref, row_of, tzi_ref, ty_ref, scratch, channels, emit, after)

        def pair(k, carry):
            forward_pair(2 * k, channels, two(gpre_ref, p, 2 * k), fy_ref, scratch)
            return carry

        lax.fori_loop(0, channels // 2, pair, 0, unroll=8)
        forward_finish(channels, tzf_ref, scratch, spec_ref, row_of)
        return carry

    lax.fori_loop(0, slab, body, 0)
    for p in range(slab):
        for g in range(channels // 8):
            for copy in stores(p, g):
                copy.wait()


def back_kernel(gpre_hbm, weight_ref, out_hbm, cells_ref, kron, in_sems, out_sems):
    prepare = lambda: spread_weight(weight_ref[...], kron)
    mix_field(gpre_hbm, out_hbm, cells_ref, kron, None, in_sems, out_sems, prepare)


def outer_kernel(field_hbm, gpre_hbm, sums_ref, field_ref, gpre_ref, outer, field_sems, gpre_sems):
    channels = field_ref.shape[1]
    load, count = cell_copies(field_hbm, field_ref, field_sems)
    load_gpre, _ = cell_copies(gpre_hbm, gpre_ref, gpre_sems)
    for n in range(count):
        load(n).start()
        load_gpre(n).start()
    outer[...] = jnp.zeros_like(outer)
    cuts = field_ref.shape[2] // 32

    def body(n, carry):
        load(n).wait()
        load_gpre(n).wait()
        total = outer[...]
        for e in range(2):
            start = pl.multiple_of(32 * (n % cuts) + 16 * e, 16)
            high, low = split(cell_tile(field_ref, n // cuts, start))
            g_high, g_low = split(cell_tile(gpre_ref, n // cuts, start))
            both = dot(jnp.concatenate([high, low], axis=0), g_high, NT)
            total = total + (both[: 8 * channels] + both[8 * channels :] + dot(high, g_low, NT))
        outer[...] = total
        return carry

    lax.fori_loop(0, count, body, 0)
    row = lax.broadcasted_iota(jnp.int32, outer.shape, 0) % 8
    column = lax.broadcasted_iota(jnp.int32, outer.shape, 1) % 8
    kept = jnp.where(row == column, outer[...], 0.0)
    kept = jnp.sum(kept.reshape(channels, 8, 8 * channels), axis=1)
    row = lax.broadcasted_iota(jnp.int32, (8 * channels, channels), 0) // 8
    column = lax.broadcasted_iota(jnp.int32, (8 * channels, channels), 1)
    pick = (row == column).astype(f32)
    small = lax.dot_general(
        kept, pick, (((1,), (0,)), ((), ())), precision=lax.Precision.HIGHEST, preferred_element_type=f32
    )
    sums_ref[...] = jnp.concatenate([small[8 * g : 8 * g + 8] for g in range(4)], axis=1)


def last_kernel(
    stride,
    ky_own,
    devices,
    sums_at,
    scales,
    in_ref,
    part_ref,
    back_hbm,
    tzi_hbm,
    ty_hbm,
    out_hbm,
    point_ref,
    bias_ref,
    scratch,
    cells_ref,
    tzi_ref,
    ty_ref,
    in_sems,
    out_sems,
    table_sems,
):
    slab, channels = cells_ref.shape[:2]
    groups = channels // 8
    places = [(p, c) for p in range(slab) for c in chunks(channels)]
    tables = transfers([(tzi_hbm, tzi_ref), (ty_hbm, ty_ref)], table_sems)
    loads = transfers([(back_hbm.at[at], cells_ref.at[at]) for at in places], in_sems)
    stores = transfers([(cells_ref.at[at], out_hbm.at[at]) for at in places], out_sems)

    def one(p, g, store):
        at = (p, pl.ds(8 * g, 8))
        if store:
            return pltpu.make_async_copy(cells_ref.at[at], out_hbm.at[at], out_sems.at[p * groups + g])
        return pltpu.make_async_copy(back_hbm.at[at], cells_ref.at[at], in_sems.at[p * groups + g])

    for copy in tables + loads:
        copy.start()
    step, first = sums_at
    total = part_ref[first : first + 8, :]
    for d in range(1, devices):
        total = total + part_ref[d * step + first : d * step + first + 8, :]
    for g in range(4):
        point_ref[8 * g : 8 * g + 8, :] = total[:, 32 * g : 32 * g + 32] * scales[0]
    bias_ref[...] = in_ref[1:2, 0:32] * scales[1]
    for copy in tables:
        copy.wait()

    def body(p, carry):
        def before(h):
            one(p, 2 * h, False).wait()
            one(p, 2 * h + 1, False).wait()

        def emit(c, values):
            put_two(cells_ref, p, c, two(cells_ref, p, c) + values)

        def after(h):
            one(p, 2 * h, True).start()
            one(p, 2 * h + 1, True).start()

        inverse_plane(
            in_ref, rows_at(p, stride, ky_own), tzi_ref, ty_ref, scratch, channels, emit, after, before
        )
        return carry

    lax.fori_loop(0, slab, body, 0)
    for copy in stores:
        copy.wait()


VM = pl.BlockSpec(memory_space=pltpu.VMEM)
HBM = pl.BlockSpec(memory_space=pltpu.HBM)


def params(megabytes):
    return pltpu.CompilerParams(vmem_limit_bytes=megabytes * MIB)


def cost(microseconds):
    return pl.CostEstimate(flops=0, bytes_accessed=int(microseconds * 3e6), transcendentals=0)


def keep(array):
    return pltpu.VMEM(array.shape, array.dtype)


def far(array):
    return pltpu.with_memory_space_constraint(array, pltpu.HBM)


def near(array):
    return pltpu.with_memory_space_constraint(array, pltpu.VMEM)


def per_device(flow_field, cotangent, spec_weight, point_weight, pointwise_bias):
    slab, channels, ny, nz = flow_field.shape
    devices = lax.axis_size("space")
    nx = slab * devices
    pair_local = spec_weight.shape[0]
    assert pair_local % MODES == 0 or slab == 1
    assert channels == 32 and ny == nz == 128 and pair_local % 4 == 0
    ky_own = max(1, pair_local // MODES)
    lines = pair_local // 2
    rows = nx * lines
    block = slab * lines
    stride = slab * ky_own * 8
    extra = 8
    wide = KX * channels
    fwd_scale = float(nx * ny * nz) ** (-0.5)
    inv_scale = float(4 * MODES**3) ** (-0.5)

    def twice(table):
        high, low = halves(table)
        return np.concatenate([np.tile(high, (1, 2)), np.tile(low, (1, 2))], axis=0)

    def forward_z(table):
        return jnp.asarray(np.concatenate([twice(table[:, :nz]), twice(table[:, nz:])], axis=0))

    def inverse_z(table):
        return jnp.asarray(np.concatenate([stack3(table[:, :nz], 0), stack3(table[:, nz:], 0)], axis=0))

    fy = jnp.asarray(twice(y_table(ny)))
    ty = jnp.asarray(stack3(y_table(ny)[: 2 * MODES].T, 1))
    tz_first = forward_z(z_table(nz, 1.0, 1.0))
    tz_grad = forward_z(z_table(nz, inv_scale, 2.0))
    tzi_out = inverse_z(z_table(nz, inv_scale, 2.0))
    tzi_grad = inverse_z(z_table(nz, fwd_scale, 1.0))
    fx = x_forward_table(nx, fwd_scale)
    fx_wide = jnp.asarray(np.repeat(stack3(fx, 0), channels, axis=1))
    gx = jnp.asarray(stack3(by_low(x_forward_table(nx, 1.0), 1).T, 1))
    inv = x_inverse_table(nx)
    inv_low = jnp.asarray(stack3(by_low(inv, 1), 1))
    by_plane = inv.reshape(2, devices, slab, 2 * KX).transpose(0, 2, 1, 3).reshape(2 * nx, 2 * KX)
    inv_wide = np.concatenate(halves(by_plane), axis=0).reshape(4 * nx, 2, KX).transpose(2, 1, 0)
    inv_wide = jnp.asarray(np.repeat(inv_wide.reshape(2 * KX, 4 * nx), channels // 2, axis=0))

    line_shape = jax.ShapeDtypeStruct((rows, 128), f32)
    field_shape = pltpu.HBM(flow_field.shape, f32)
    mode_scratch = pltpu.VMEM((SLOTS, nz), f32)
    kron_scratch = pltpu.VMEM((16 * channels, 8 * channels), bf16)
    chunk_count = slab * (channels // 8)
    chunk_sems = pltpu.SemaphoreType.DMA((chunk_count,))
    pair_sems = pltpu.SemaphoreType.DMA((2,))
    cell_sems = pltpu.SemaphoreType.DMA((slab * (ny // 32),))

    def exchange(lines_out):
        blocks = lines_out.reshape(devices, -1, 128)
        return lax.all_to_all(blocks, "space", split_axis=0, concat_axis=0, tiled=True)

    first = pl.pallas_call(
        functools.partial(first_kernel, stride, ky_own),
        in_specs=[HBM, HBM, HBM],
        out_specs=VM,
        out_shape=line_shape,
        scratch_shapes=[
            pltpu.VMEM(flow_field.shape, f32),
            keep(fy),
            keep(tz_first),
            mode_scratch,
            chunk_sems,
            pair_sems,
        ],
        compiler_params=params(16),
        cost_estimate=cost(4),
        name="field_forward",
    )(far(flow_field), far(fy), far(tz_first))
    spec_x = exchange(first).reshape(rows, 128)

    bias = pointwise_bias.reshape(1, channels)
    pointwise = pl.pallas_call(
        point_kernel,
        in_specs=[HBM, VM, VM],
        out_specs=HBM,
        out_shape=field_shape,
        scratch_shapes=[
            keep(flow_field),
            kron_scratch,
            pltpu.VMEM((8 * channels, 2 * nz), f32),
            cell_sems,
            cell_sems,
        ],
        compiler_params=params(16),
        cost_estimate=cost(6),
        name="pointwise",
    )(far(flow_field), point_weight, bias)

    spec_x, pointwise = lax.optimization_barrier((spec_x, pointwise))
    mixed = pl.pallas_call(
        functools.partial(mix_kernel, nx, lines),
        in_specs=[VM, HBM, HBM, HBM],
        out_specs=VM,
        out_shape=line_shape,
        scratch_shapes=[
            keep(spec_weight),
            keep(fx_wide),
            keep(inv_low),
            pltpu.VMEM((32 * pair_local, 6 * nx), bf16),
            pltpu.VMEM((32 * pair_local, 512), f32),
            pltpu.VMEM((128 * pair_local, 128), f32),
            pltpu.SemaphoreType.DMA((6,)),
        ],
        compiler_params=params(24),
        cost_estimate=cost(5),
        name="mode_mix",
    )(spec_x, far(spec_weight), far(fx_wide), far(inv_low))
    mixed = exchange(mixed).reshape(rows, 128)

    output, gpre, grad_lines = pl.pallas_call(
        functools.partial(middle_kernel, stride, ky_own),
        in_specs=[VM] * 7,
        out_specs=[HBM, HBM, VM],
        out_shape=[field_shape, field_shape, line_shape],
        scratch_shapes=[
            pltpu.VMEM(flow_field.shape, f32),
            pltpu.VMEM(flow_field.shape, f32),
            mode_scratch,
            pltpu.SemaphoreType.DMA((2, slab, channels // 8)),
        ],
        compiler_params=params(24),
        cost_estimate=cost(10),
        name="middle",
    )(mixed, near(pointwise), near(cotangent), near(tzi_out), near(ty), near(fy), near(tz_grad))
    grad_x = exchange(grad_lines).reshape(rows, 128)

    local_sums = pl.pallas_call(
        outer_kernel,
        in_specs=[HBM, HBM],
        out_specs=VM,
        out_shape=jax.ShapeDtypeStruct((extra, 128), f32),
        scratch_shapes=[
            keep(flow_field),
            keep(flow_field),
            pltpu.VMEM((8 * channels, 8 * channels), f32),
            cell_sems,
            cell_sems,
        ],
        compiler_params=params(16),
        cost_estimate=cost(6),
        name="outer_sums",
    )(far(flow_field), far(gpre))

    sent = devices * (block + extra)
    grad_mixed = pl.pallas_call(
        functools.partial(adjoint_kernel, slab, nx, lines, extra),
        in_specs=[VM, HBM, HBM, HBM, VM],
        out_specs=VM,
        out_shape=jax.ShapeDtypeStruct((sent, 128), f32),
        scratch_shapes=[
            keep(spec_weight),
            keep(gx),
            keep(inv_wide),
            pltpu.VMEM((16 * pair_local, 128), f32),
            pltpu.VMEM((16 * pair_local, 512), bf16),
            pltpu.VMEM((16 * pair_local, 512), bf16),
            pltpu.VMEM((32 * pair_local, 4 * nx), f32),
            pltpu.SemaphoreType.DMA((6,)),
        ],
        compiler_params=params(24),
        cost_estimate=cost(6),
        name="mode_adjoint",
    )(grad_x, far(spec_weight), far(gx), far(inv_wide), local_sums)
    grad_spec = pl.pallas_call(
        functools.partial(weight_grad_kernel, nx, lines),
        in_specs=[VM, VM, HBM, HBM],
        out_specs=HBM,
        out_shape=pltpu.HBM(spec_weight.shape, f32),
        scratch_shapes=[
            keep(fx_wide),
            keep(gx),
            pltpu.VMEM((32 * pair_local, 6 * nx), bf16),
            pltpu.VMEM((32 * pair_local, 512), f32),
            pltpu.VMEM((16 * pair_local, 128), f32),
            pltpu.VMEM((4, pair_local, 2, channels, wide // 4), f32),
            pltpu.SemaphoreType.DMA((4,)),
            pair_sems,
        ],
        compiler_params=params(24),
        cost_estimate=cost(6),
        name="weight_grad",
    )(spec_x, grad_x, far(fx_wide), far(gx))

    gpre, grad_mixed = lax.optimization_barrier((gpre, grad_mixed))
    received = exchange(grad_mixed)
    back = pl.pallas_call(
        back_kernel,
        in_specs=[HBM, VM],
        out_specs=HBM,
        out_shape=field_shape,
        scratch_shapes=[keep(flow_field), kron_scratch, cell_sems, cell_sems],
        compiler_params=params(16),
        cost_estimate=cost(6),
        name="pointwise_back",
    )(far(gpre), point_weight)

    if pair_local >= MODES:
        lines_in = sums_in = received.reshape(sent, 128)
        stride_in, sums_at = stride + extra, (stride + extra, stride)
    else:
        lines_in = received[:, :block].reshape(rows, 128)
        sums_in = received[:, block:].reshape(devices * extra, 128)
        stride_in, sums_at = stride, (extra, 0)
    grad_field, grad_point, grad_bias = pl.pallas_call(
        functools.partial(
            last_kernel, stride_in, ky_own, devices, sums_at, (fwd_scale, fwd_scale / inv_scale)
        ),
        in_specs=[VM, VM, HBM, HBM, HBM],
        out_specs=[HBM, VM, VM],
        out_shape=[
            field_shape,
            jax.ShapeDtypeStruct((channels, channels), f32),
            jax.ShapeDtypeStruct((1, channels), f32),
        ],
        scratch_shapes=[
            mode_scratch,
            pltpu.VMEM(flow_field.shape, f32),
            keep(tzi_grad),
            keep(ty),
            chunk_sems,
            chunk_sems,
            pair_sems,
        ],
        compiler_params=params(16),
        cost_estimate=cost(8),
        name="field_inverse",
    )(lines_in, sums_in, far(back), far(tzi_grad), far(ty))

    return output, grad_field, grad_spec, grad_point, grad_bias.reshape(channels)


def solution(mesh):
    cells = P(("group", "space"), None, None, None)
    return jax.shard_map(
        per_device,
        mesh=mesh,
        in_specs=(cells, cells, P("space", None, None, None), P(), P()),
        out_specs=(cells, cells, cells, P("group", None), P("group")),
        check_vma=False,
    )
```

```python
import functools
import math

import jax
import jax.numpy as jnp
import ml_dtypes
import numpy as np
from jax import lax
from jax.experimental import pallas as pl
from jax.experimental.pallas import tpu as pltpu
from jax.sharding import PartitionSpec as P

MODES = 16
KY = 2 * MODES
KX = 2 * MODES
MIB = 1024 * 1024
NT = (((1,), (1,)), ((), ()))
TN = (((0,), (0,)), ((), ()))
f32 = jnp.float32
bf16 = jnp.bfloat16


def signed(n):
    j = np.arange(n)
    return np.where(j < n // 2, j, j - n)


def phases(positions, waves, length):
    angle = ((positions[:, None] * waves[None, :]) % length) * (2.0 * math.pi / length)
    return np.cos(angle), np.sin(angle)


def halves(table):
    table = np.asarray(table, np.float32)
    high = table.astype(ml_dtypes.bfloat16)
    low = (table - high.astype(np.float32)).astype(ml_dtypes.bfloat16)
    return high, low


def stack3(table, axis):
    high, low = halves(table)
    return np.concatenate([high, high, low], axis=axis)


def y_table(ny):
    cos, sin = phases(np.arange(ny), np.arange(MODES + 1), ny)
    order = [MODES] + list(range(1, MODES))
    return np.concatenate([cos.T[:MODES], -sin.T[order], cos.T[MODES:], np.zeros((7, ny))], axis=0)


def z_table(nz, scale, factor):
    cos, sin = phases(np.arange(nz), np.arange(MODES), nz)
    weight = scale * np.where(np.arange(MODES) == 0, 1.0, factor)
    cos, sin = cos.T * weight[:, None], sin.T * weight[:, None]
    real = np.concatenate([cos, sin], axis=1)
    imag = np.concatenate([-sin, cos], axis=1)
    both = np.stack([real, imag], axis=1).reshape(4, 4, 2, 2 * nz)
    return both.transpose(1, 0, 2, 3).reshape(2 * MODES, 2 * nz)


def x_forward_table(nx, scale):
    cos, sin = phases(np.arange(nx), signed(KX), nx)
    top = np.concatenate([cos, -sin], axis=1)
    bottom = np.concatenate([sin, cos], axis=1)
    return scale * np.concatenate([top, bottom], axis=0)


def x_inverse_table(nx):
    cos, sin = phases(np.arange(nx), signed(KX), nx)
    top = np.concatenate([cos, -sin], axis=1)
    bottom = np.concatenate([sin, cos], axis=1)
    return np.concatenate([top, bottom], axis=0)


def by_low(table, axis):
    order = np.arange(2 * KX).reshape(2, KX // 4, 4).transpose(0, 2, 1).reshape(-1)
    return np.take(table, order, axis=axis)


def split(values):
    high = values.astype(bf16)
    low = (values - high.astype(f32)).astype(bf16)
    return high, low


def data3(values):
    high, low = split(values)
    return jnp.concatenate([high, low, high], axis=0)


def dot(left, right, dims=(((1,), (0,)), ((), ()))):
    return lax.dot_general(left, right, dims, preferred_element_type=f32)


def group_transpose(tiles):
    group = lax.broadcasted_iota(jnp.int32, tiles[0].shape, 1) // 32
    result = []
    for m in range(4):
        moved = [pltpu.roll(tiles[n], ((n - m) * 32) % 128, 1) if n != m else tiles[n] for n in range(4)]
        low = jnp.where(group == 0, moved[0], moved[1])
        high = jnp.where(group == 2, moved[2], moved[3])
        result.append(jnp.where(group < 2, low, high))
    return result


def block_row(ky, plane, stride, ky_own):
    return (ky // ky_own) * stride + (plane * ky_own + ky % ky_own) * 8


COS16 = MODES * 32
SINES = COS16 + 128
SLOTS = SINES + MODES * 32


def forward_pair(c, channels, pair, fy_ref, scratch):
    nz = scratch.shape[1]
    high, low = split(pair)
    both = dot(fy_ref[...], jnp.concatenate([high, low], axis=0))
    half = both[: 2 * MODES + 8] + both[2 * MODES + 8 :]
    for e in range(2):
        side = slice(e * nz, (e + 1) * nz)
        scratch[pl.ds(c + e, MODES, stride=channels), :] = half[:MODES, side]
        scratch[pl.ds(SINES + c + e, MODES, stride=channels), :] = half[MODES : 2 * MODES, side]
        scratch[pl.ds(COS16 + c + e, 1), :] = half[2 * MODES : 2 * MODES + 1, side]


def forward_finish(channels, tz_ref, scratch, out_ref, row_of):
    count = 2 * MODES
    sides = []
    for part, rows in ((0, slice(0, SINES)), (1, slice(SINES, SLOTS))):
        both = dot(tz_ref[2 * part * count : 2 * (part + 1) * count, :], jnp.concatenate(split(scratch[rows, :]), axis=1), NT)
        sides.append(both[:count] + both[count:])
    first = lax.broadcasted_iota(jnp.int32, (8, 128), 1) < 32
    for q in range(MODES // 4):
        tiles = ([], [])
        for j in range(4):
            rows, cols = slice(8 * j, 8 * j + 8), slice(q * 128, (q + 1) * 128)
            even, odd = sides[0][rows, cols], sides[1][rows, cols]
            last = sides[0][rows, COS16 : COS16 + 128]
            tiles[0].append(jnp.where(first, even, even + odd) if q == 0 else even + odd)
            tiles[1].append((jnp.where(first, last, even) if q == 0 else even) - odd)
        for sign in range(2):
            for e, tile in enumerate(group_transpose(tiles[sign])):
                k = 4 * q + e
                ky = k if sign == 0 else (KY - k if k else MODES)
                out_ref[pl.ds(row_of(ky), 8), :] = tile


def inverse_plane(in_ref, row_of, tz_ref, ty_ref, scratch, channels, emit, after, before=lambda h: None):
    nz = scratch.shape[1]
    tile = lambda ky: in_ref[pl.ds(row_of(ky), 8), :]
    columns = ([[] for _ in range(4)], [[] for _ in range(4)])
    for q in range(MODES // 4):
        sums, differences = [], []
        for k in range(4 * q, 4 * q + 4):
            sums.append(tile(k) + tile(KY - k) if k else tile(0))
            differences.append(tile(k) - tile(KY - k) if k else -tile(MODES))
        for sign, tiles in ((0, sums), (1, differences)):
            for j, found in enumerate(group_transpose(tiles)):
                columns[sign][j].append(found)
    for j, found in enumerate(group_transpose([tile(MODES)] * 4)):
        columns[0][j].append(found)
    depth = tz_ref.shape[0] // 2
    for sign, rows in ((0, slice(0, SINES)), (1, slice(SINES, SLOTS))):
        data = jnp.concatenate([jnp.concatenate(c, axis=1) for c in columns[sign]], axis=0)
        scratch[rows, :] = dot(data3(data), tz_ref[sign * depth : (sign + 1) * depth, :], TN)
    at = lax.broadcasted_iota(jnp.int32, (8, 2 * nz), 0)
    slant = jnp.where((at == 3) | (at == 5) | (at == 4), -1.0, 1.0) * jnp.where(at % 2 == 1, math.sqrt(0.5), 1.0)
    wave = jnp.where(at % 4 == 2, 0.0, slant)

    def group(h, carry):
        before(h)
        for k in range(0, 16, 2):
            c = 16 * h + k
            sides, tops = [], []
            for e in range(2):
                parts = [scratch[pl.ds(first + c + e, MODES, stride=channels), :] for first in (0, SINES)]
                sides.append(jnp.concatenate(parts, axis=0))
                tops.append(scratch[pl.ds(COS16 + c + e, 1), :])
            pair = dot(ty_ref[...], data3(jnp.concatenate(sides, axis=1)))
            extra = wave * jnp.concatenate(tops, axis=1)
            emit(c, pair + jnp.concatenate([extra] * (pair.shape[0] // 8), axis=0))
        after(h)
        return carry

    lax.fori_loop(0, channels // 16, group, 0)


def two(ref, p, c):
    return jnp.concatenate([ref[p, c], ref[p, c + 1]], axis=1)


def put_two(ref, p, c, values):
    nz = values.shape[1] // 2
    ref[p, c], ref[p, c + 1] = values[:, :nz], values[:, nz:]


def spread_weight(weight, kron_ref):
    size = weight.shape[0]
    row = lax.broadcasted_iota(jnp.int32, (8 * size, size), 0) // 8
    column = lax.broadcasted_iota(jnp.int32, (8 * size, size), 1)
    expand = (row == column).astype(f32)
    tall = lax.dot_general(
        expand, weight, (((1,), (0,)), ((), ())), precision=lax.Precision.HIGHEST, preferred_element_type=f32
    )
    wide = lax.dot_general(tall, expand, NT, precision=lax.Precision.HIGHEST, preferred_element_type=f32)
    row = lax.broadcasted_iota(jnp.int32, wide.shape, 0) % 8
    column = lax.broadcasted_iota(jnp.int32, wide.shape, 1) % 8
    kron_ref[...] = jnp.concatenate(split(jnp.where(row == column, wide, 0.0)), axis=0)


def cell_tile(ref, plane, start):
    sides = []
    for e in range(2):
        piece = ref[plane, :, pl.ds(start + 8 * e, 8), :]
        sides.append(piece.reshape(piece.shape[0] * 8, piece.shape[2]))
    return jnp.concatenate(sides, axis=1)


def put_tile(ref, plane, start, tile):
    channels, nz = ref.shape[1], ref.shape[3]
    for e in range(2):
        ref[plane, :, pl.ds(start + 8 * e, 8), :] = tile[:, e * nz : (e + 1) * nz].reshape(channels, 8, nz)


def mix_cells(kron_ref, high, low):
    size = high.shape[0]
    both = dot(kron_ref[...], high)
    return both[:size] + both[size:] + dot(kron_ref[:size, :], low)


def rows_at(plane, stride, ky_own):
    def row_of(ky):
        row = block_row(ky, plane, stride, ky_own)
        return row if isinstance(row, int) else pl.multiple_of(row, 8)

    return row_of


def transfers(pairs, sems):
    return [pltpu.make_async_copy(src, dst, sems.at[i]) for i, (src, dst) in enumerate(pairs)]


def chunks(channels):
    return [slice(8 * g, 8 * g + 8) for g in range(channels // 8)]


def first_kernel(stride, ky_own, field_hbm, fy_hbm, tz_hbm, out_ref, field_ref, fy_ref, tz_ref, scratch, sems, table_sems):
    slab, channels = field_ref.shape[:2]
    tables = transfers([(fy_hbm, fy_ref), (tz_hbm, tz_ref)], table_sems)
    parts = [(field_hbm.at[p, c], field_ref.at[p, c]) for p in range(slab) for c in chunks(channels)]
    loads = transfers(parts, sems)
    for copy in tables[:1] + loads[:2] + tables[1:] + loads[2:]:
        copy.start()
    tables[0].wait()

    def body(p, carry):
        for c in range(0, channels, 2):
            if c % 16 == 0:
                for g in (c // 8, c // 8 + 1):
                    part = slice(8 * g, 8 * g + 8)
                    sem = sems.at[p * (channels // 8) + g]
                    pltpu.make_async_copy(field_hbm.at[p, part], field_ref.at[p, part], sem).wait()
            forward_pair(c, channels, two(field_ref, p, c), fy_ref, scratch)

        @pl.when(p == 0)
        def _():
            tables[1].wait()

        forward_finish(channels, tz_ref, scratch, out_ref, rows_at(p, stride, ky_own))
        return carry

    lax.fori_loop(0, slab, body, 0)


def cell_copies(array_hbm, array_ref, sems, store=False):
    cuts = array_ref.shape[2] // 32

    def copy(n):
        at = (n // cuts, slice(None), pl.ds(32 * (n % cuts), 32))
        ends = (array_hbm.at[at], array_ref.at[at])
        return pltpu.make_async_copy(*(ends[::-1] if store else ends), sems.at[n])

    return copy, array_ref.shape[0] * cuts


def mix_field(field_hbm, out_hbm, cells_ref, kron, offset, in_sems, out_sems, prepare):
    load, count = cell_copies(field_hbm, cells_ref, in_sems)
    store, _ = cell_copies(out_hbm, cells_ref, out_sems, True)
    for n in range(count):
        load(n).start()
    prepare()
    cuts = cells_ref.shape[2] // 32

    def body(n, carry):
        load(n).wait()
        for e in range(2):
            start = pl.multiple_of(32 * (n % cuts) + 16 * e, 16)
            high, low = split(cell_tile(cells_ref, n // cuts, start))
            values = mix_cells(kron, high, low)
            put_tile(cells_ref, n // cuts, start, values if offset is None else values + offset[...])
        store(n).start()
        return carry

    lax.fori_loop(0, count, body, 0)
    for n in range(count):
        store(n).wait()


def point_kernel(field_hbm, weight_ref, bias_ref, out_hbm, cells_ref, kron, bias_wide, in_sems, out_sems):
    channels = cells_ref.shape[1]

    def prepare():
        spread_weight(jnp.transpose(weight_ref[...]), kron)
        row = lax.broadcasted_iota(jnp.int32, (8 * channels, channels), 0) // 8
        column = lax.broadcasted_iota(jnp.int32, (8 * channels, channels), 1)
        picked = jnp.where(row == column, bias_ref[...], 0.0)
        bias_wide[...] = jnp.broadcast_to(jnp.sum(picked, axis=1, keepdims=True), bias_wide.shape)

    mix_field(field_hbm, out_hbm, cells_ref, kron, bias_wide, in_sems, out_sems, prepare)


def quad_rows(ref, nx, lines, u):
    return jnp.concatenate([ref[pl.ds(2 * u + part, nx, stride=lines), :] for part in range(2)], axis=0)


def data_rows(ref, nx, lines, u):
    high, low = split(jnp.transpose(quad_rows(ref, nx, lines, u)))
    return jnp.concatenate([high, low, high], axis=1)


def weight_part(ref, t, h):
    half = ref.shape[0] // 2
    start = 256 * t if isinstance(t, int) else pl.multiple_of(256 * t, 256)
    return ref.at[half * h : half * (h + 1), :, :, pl.ds(start, 256)]


def weight_loads(weight_hbm, weight_ref, tables, sems):
    parts = [(weight_part(weight_hbm, t, h), weight_part(weight_ref, t, h)) for t in range(4) for h in range(2)]
    copies = transfers(tables + parts, sems)
    for copy in copies[:1] + copies[2:3] + copies[1:2] + copies[3:]:
        copy.start()
    return copies[:2], copies[2:]


def mix_kernel(
    nx, lines, in_ref, weight_hbm, fx_hbm, inv_hbm, out_ref, weight_ref, fx_ref, inv_ref, left, modes, sums, sems
):
    pairs = weight_ref.shape[0]
    wide = KX * 32
    tables, loads = weight_loads(weight_hbm, weight_ref, [(fx_hbm, fx_ref), (inv_hbm, inv_ref)], sems)
    for u in range(pairs // 4):
        left[128 * u : 128 * u + 128, :] = data_rows(in_ref, nx, lines, u)
    tables[0].wait()
    for t in range(4):
        cols = slice(256 * t, 256 * t + 256)
        late = slice(wide + 256 * t, wide + 256 * t + 256)
        modes[:, :256] = dot(left[...], fx_ref[:, cols])
        modes[:, 256:] = dot(left[...], fx_ref[:, late])

        def body(pair, carry):
            rows = pl.ds(pl.multiple_of(32 * pair, 32), 32)
            real, imag = modes[rows, :256], modes[rows, 256:]
            w_real, w_imag = weight_ref[pair, 0, :, cols], weight_ref[pair, 1, :, cols]
            products = (real * w_real - imag * w_imag, imag * w_real + real * w_imag)
            for part in range(2):
                total = jnp.sum(products[part].reshape(4, 8, 256), axis=0)
                for e in range(2):
                    base = pl.multiple_of((2 * pair + part) * 64 + 8 * (2 * t + e), 8)
                    sums[pl.ds(base, 8), :] = total[:, 128 * e : 128 * e + 128]
            return carry

        for h in range(2):
            loads[2 * t + h].wait()
            lax.fori_loop(h * (pairs // 2), (h + 1) * (pairs // 2), body, 0, unroll=min(4, pairs // 2))
    tables[1].wait()
    for u in range(pairs // 4):
        tiles = [[], []]
        for j in range(4):
            for part in range(2):
                base = (2 * (4 * u + j) + part) * 64
                found = [sums[pl.ds(base + s, 8, stride=8), :] for s in range(8)]
                while len(found) > 1:
                    found = [found[k] + found[k + 1] for k in range(0, len(found), 2)]
                tiles[part].append(found[0])
        mixed = jnp.concatenate(group_transpose(tiles[0]) + group_transpose(tiles[1]), axis=0)
        planes = dot(inv_ref[...], data3(mixed))
        for part in range(2):
            out_ref[pl.ds(2 * u + part, nx, stride=lines), :] = planes[part * nx : (part + 1) * nx]


def gradient_tiles(grad_ref, gx_ref, nx, lines, u):
    grads = dot(gx_ref[...], data3(quad_rows(grad_ref, nx, lines, u)))
    tiles = []
    for part in range(2):
        tiles.append(group_transpose([grads[part * 32 + 8 * b : part * 32 + 8 * b + 8, :] for b in range(4)]))
    return tiles, grads


def gradient_rows(grad_ref, gx_ref, nx, lines, quads, rows_ref):
    bias = None
    for u in range(quads):
        tiles, grads = gradient_tiles(grad_ref, gx_ref, nx, lines, u)
        bias = grads[0:1, :] if u == 0 else bias
        for part in range(2):
            for j in range(4):
                base = (2 * (4 * u + j) + part) * 8
                rows_ref[base : base + 8, :] = tiles[part][j]
    return bias


def weight_grad_kernel(
    nx, lines, in_ref, grad_ref, fx_hbm, gx_hbm, out_hbm, fx_ref, gx_ref, left, modes, rows_ref, grads_ref, sems, table_sems
):
    pairs = grads_ref.shape[1]
    wide = KX * 32
    tables = transfers([(gx_hbm, gx_ref), (fx_hbm, fx_ref)], table_sems)
    for copy in tables:
        copy.start()
    for u in range(pairs // 4):
        left[128 * u : 128 * u + 128, :] = data_rows(in_ref, nx, lines, u)
    for copy in tables:
        copy.wait()
    gradient_rows(grad_ref, gx_ref, nx, lines, pairs // 4, rows_ref)
    parts = [(grads_ref.at[t], out_hbm.at[:, :, :, pl.ds(256 * t, 256)]) for t in range(4)]
    stores = transfers(parts, sems)
    for t in range(4):
        modes[:, :256] = dot(left[...], fx_ref[:, 256 * t : 256 * t + 256])
        modes[:, 256:] = dot(left[...], fx_ref[:, wide + 256 * t : wide + 256 * t + 256])

        def body(pair, carry):
            rows = pl.ds(pl.multiple_of(32 * pair, 32), 32)
            for e in range(2):
                g_real, g_imag = [
                    jnp.broadcast_to(rows_ref[pl.ds((2 * pair + part) * 8 + 2 * t + e, 1), :], (32, 128))
                    for part in range(2)
                ]
                cols = slice(128 * e, 128 * e + 128)
                real, imag = modes[rows, cols], modes[rows, 256 + 128 * e : 384 + 128 * e]
                grads_ref[t, pair, 0, :, cols] = real * g_real + imag * g_imag
                grads_ref[t, pair, 1, :, cols] = real * g_imag - imag * g_real
            return carry

        lax.fori_loop(0, pairs, body, 0, unroll=4)
        stores[t].start()
    for copy in stores:
        copy.wait()


def adjoint_kernel(
    slab,
    nx,
    lines,
    extra,
    grad_ref,
    weight_hbm,
    gx_hbm,
    inv_hbm,
    sums_ref,
    out_ref,
    weight_ref,
    gx_ref,
    inv_ref,
    rows_ref,
    soon,
    late,
    total,
    sems,
):
    pairs = weight_ref.shape[0]
    devices = nx // slab
    stride = slab * lines + extra
    tables, loads = weight_loads(weight_hbm, weight_ref, [(gx_hbm, gx_ref), (inv_hbm, inv_ref)], sems)
    tables[0].wait()
    bias = gradient_rows(grad_ref, gx_ref, nx, lines, pairs // 4, rows_ref)
    total[...] = jnp.zeros_like(total)
    late[...] = jnp.zeros_like(late)
    tables[1].wait()
    early = lax.broadcasted_iota(jnp.int32, (32, 128), 1) % 32 < 16
    count = pairs // 2

    def arrive(t, h):
        ends = (weight_part(weight_hbm, t, h), weight_part(weight_ref, t, h))
        pltpu.make_async_copy(*ends, sems.at[2 + 2 * t + h]).wait()

    def products(t, first, target):
        for k in range(count):
            pair = first + k
            for e in range(2):
                cols = pl.ds(pl.multiple_of(256 * t + 128 * e, 128), 128)
                g_real, g_imag = [
                    jnp.broadcast_to(rows_ref[pl.ds((2 * pair + part) * 8 + 2 * t + e, 1), :], (32, 128))
                    for part in range(2)
                ]
                w_real, w_imag = weight_ref[pair, 0, :, cols], weight_ref[pair, 1, :, cols]
                real = g_real * w_real + g_imag * w_imag
                imag = g_imag * w_real - g_real * w_imag
                folded = jnp.where(early, real + pltpu.roll(real, 112, 1), imag + pltpu.roll(imag, 16, 1))
                high, low = split(folded)
                target[32 * k : 32 * k + 32, 128 * e : 128 * e + 128] = high
                target[32 * k : 32 * k + 32, 256 + 128 * e : 384 + 128 * e] = low

    def gather(t, source, first):
        table = inv_ref[pl.ds(pl.multiple_of(256 * t, 256), 256), :]
        rows = slice(32 * first, 32 * (first + count))
        total[rows, :] += dot(source[:, :256], table) + dot(source[:, 256:], table)

    def body(t, carry):
        arrive(t, 0)
        gather(jnp.maximum(t - 1, 0), late, count)
        products(t, 0, soon)
        arrive(t, 1)
        gather(t, soon, 0)
        products(t, count, late)
        return carry

    lax.fori_loop(0, 4, body, 0)
    gather(3, late, count)
    lane = lax.broadcasted_iota(jnp.int32, (nx, 128), 1)
    carried = lax.axis_index("space") == 0
    for u in range(pairs // 4):
        both = total[128 * u : 128 * u + 128, :]
        planes = jnp.transpose(both[:, : 2 * nx] + both[:, 2 * nx :])
        real, imag = planes[:nx], planes[nx:]
        if u == 0:
            imag = jnp.where((lane < 32) & carried, jnp.broadcast_to(bias, (nx, 128)), imag)
        for part, values in ((0, real), (1, imag)):
            for p in range(slab):
                out_ref[pl.ds(p * lines + 2 * u + part, devices, stride=stride), :] = values[
                    p * devices : (p + 1) * devices
                ]
    for d in range(devices):
        out_ref[d * stride + slab * lines : d * stride + slab * lines + extra, :] = sums_ref[...]


def middle_kernel(
    stride,
    ky_own,
    in_ref,
    point_ref,
    cot_ref,
    tzi_ref,
    ty_ref,
    fy_ref,
    tzf_ref,
    output_hbm,
    gpre_hbm,
    spec_ref,
    output_ref,
    gpre_ref,
    scratch,
    sems,
):
    slab, channels = point_ref.shape[:2]
    rate = math.sqrt(2.0 / math.pi)

    def stores(p, g):
        part = pl.ds(8 * g, 8)
        pairs = ((output_ref, output_hbm), (gpre_ref, gpre_hbm))
        return [
            pltpu.make_async_copy(src.at[p, part], dst.at[p, part], sems.at[k, p, g])
            for k, (src, dst) in enumerate(pairs)
        ]

    def body(p, carry):
        row_of = rows_at(p, stride, ky_own)

        def emit(c, spectral):
            values = spectral + two(point_ref, p, c)
            square = values * values
            half = 0.5 + 0.5 * jnp.tanh(values * (rate + (0.044715 * rate) * square))
            result = values * half
            put_two(output_ref, p, c, result)
            slope = half + result * (1.0 - half) * (2.0 * rate + (6 * 0.044715 * rate) * square)
            put_two(gpre_ref, p, c, two(cot_ref, p, c) * slope)

        def after(h):
            for g in range(2):
                for copy in stores(p, 2 * h + g):
                    copy.start()

        inverse_plane(in_ref, row_of, tzi_ref, ty_ref, scratch, channels, emit, after)

        def pair(k, carry):
            forward_pair(2 * k, channels, two(gpre_ref, p, 2 * k), fy_ref, scratch)
            return carry

        lax.fori_loop(0, channels // 2, pair, 0, unroll=16)
        forward_finish(channels, tzf_ref, scratch, spec_ref, row_of)
        return carry

    lax.fori_loop(0, slab, body, 0)
    for p in range(slab):
        for g in range(channels // 8):
            for copy in stores(p, g):
                copy.wait()


def outer_kernel(
    field_hbm, gpre_hbm, weight_ref, sums_ref, back_hbm, field_ref, gpre_ref, kron, outer, field_sems, gpre_sems, out_sems
):
    channels = field_ref.shape[1]
    load, count = cell_copies(field_hbm, field_ref, field_sems)
    load_gpre, _ = cell_copies(gpre_hbm, gpre_ref, gpre_sems)
    store, _ = cell_copies(back_hbm, gpre_ref, out_sems, True)
    for n in range(count):
        load(n).start()
        load_gpre(n).start()
    outer[...] = jnp.zeros_like(outer)
    spread_weight(weight_ref[...], kron)
    cuts = field_ref.shape[2] // 32

    def body(n, carry):
        load(n).wait()
        load_gpre(n).wait()
        total = outer[...]
        for e in range(2):
            start = pl.multiple_of(32 * (n % cuts) + 16 * e, 16)
            high, low = split(cell_tile(field_ref, n // cuts, start))
            g_high, g_low = split(cell_tile(gpre_ref, n // cuts, start))
            both = dot(jnp.concatenate([high, low], axis=0), g_high, NT)
            total = total + (both[: 8 * channels] + both[8 * channels :] + dot(high, g_low, NT))
            put_tile(gpre_ref, n // cuts, start, mix_cells(kron, g_high, g_low))
        outer[...] = total
        store(n).start()
        return carry

    lax.fori_loop(0, count, body, 0)
    for n in range(count):
        store(n).wait()
    row = lax.broadcasted_iota(jnp.int32, outer.shape, 0) % 8
    column = lax.broadcasted_iota(jnp.int32, outer.shape, 1) % 8
    kept = jnp.where(row == column, outer[...], 0.0)
    kept = jnp.sum(kept.reshape(channels, 8, 8 * channels), axis=1)
    row = lax.broadcasted_iota(jnp.int32, (8 * channels, channels), 0) // 8
    column = lax.broadcasted_iota(jnp.int32, (8 * channels, channels), 1)
    pick = (row == column).astype(f32)
    small = lax.dot_general(
        kept, pick, (((1,), (0,)), ((), ())), precision=lax.Precision.HIGHEST, preferred_element_type=f32
    )
    sums_ref[...] = jnp.concatenate([small[8 * g : 8 * g + 8] for g in range(4)], axis=1)


def last_kernel(
    stride,
    ky_own,
    devices,
    sums_at,
    scales,
    in_ref,
    part_ref,
    back_hbm,
    tzi_hbm,
    ty_hbm,
    out_hbm,
    point_ref,
    bias_ref,
    scratch,
    cells_ref,
    tzi_ref,
    ty_ref,
    in_sems,
    out_sems,
    table_sems,
):
    slab, channels = cells_ref.shape[:2]
    groups = channels // 8
    places = [(p, c) for p in range(slab) for c in chunks(channels)]
    tables = transfers([(tzi_hbm, tzi_ref), (ty_hbm, ty_ref)], table_sems)
    loads = transfers([(back_hbm.at[at], cells_ref.at[at]) for at in places], in_sems)
    stores = transfers([(cells_ref.at[at], out_hbm.at[at]) for at in places], out_sems)

    def one(p, g, store):
        at = (p, pl.ds(8 * g, 8))
        if store:
            return pltpu.make_async_copy(cells_ref.at[at], out_hbm.at[at], out_sems.at[p * groups + g])
        return pltpu.make_async_copy(back_hbm.at[at], cells_ref.at[at], in_sems.at[p * groups + g])

    for copy in tables + loads:
        copy.start()
    step, first = sums_at
    total = part_ref[first : first + 8, :]
    for d in range(1, devices):
        total = total + part_ref[d * step + first : d * step + first + 8, :]
    for g in range(4):
        point_ref[8 * g : 8 * g + 8, :] = total[:, 32 * g : 32 * g + 32] * scales[0]
    bias_ref[...] = in_ref[1:2, 0:32] * scales[1]
    for copy in tables:
        copy.wait()

    def body(p, carry):
        def before(h):
            one(p, 2 * h, False).wait()
            one(p, 2 * h + 1, False).wait()

        def emit(c, values):
            put_two(cells_ref, p, c, two(cells_ref, p, c) + values)

        def after(h):
            one(p, 2 * h, True).start()
            one(p, 2 * h + 1, True).start()

        inverse_plane(
            in_ref, rows_at(p, stride, ky_own), tzi_ref, ty_ref, scratch, channels, emit, after, before
        )
        return carry

    lax.fori_loop(0, slab, body, 0)
    for copy in stores:
        copy.wait()


VM = pl.BlockSpec(memory_space=pltpu.VMEM)
HBM = pl.BlockSpec(memory_space=pltpu.HBM)


def params(megabytes):
    return pltpu.CompilerParams(vmem_limit_bytes=megabytes * MIB)


def cost(microseconds):
    return pl.CostEstimate(flops=0, bytes_accessed=int(microseconds * 3e6), transcendentals=0)


def keep(array):
    return pltpu.VMEM(array.shape, array.dtype)


def far(array):
    return pltpu.with_memory_space_constraint(array, pltpu.HBM)


def near(array):
    return pltpu.with_memory_space_constraint(array, pltpu.VMEM)


def per_device(flow_field, cotangent, spec_weight, point_weight, pointwise_bias):
    slab, channels, ny, nz = flow_field.shape
    devices = lax.axis_size("space")
    nx = slab * devices
    pair_local = spec_weight.shape[0]
    assert pair_local % MODES == 0 or slab == 1
    assert channels == 32 and ny == nz == 128 and pair_local % 4 == 0
    ky_own = max(1, pair_local // MODES)
    lines = pair_local // 2
    rows = nx * lines
    block = slab * lines
    stride = slab * ky_own * 8
    extra = 8
    wide = KX * channels
    fwd_scale = float(nx * ny * nz) ** (-0.5)
    inv_scale = float(4 * MODES**3) ** (-0.5)

    def twice(table):
        high, low = halves(table)
        return np.concatenate([np.tile(high, (1, 2)), np.tile(low, (1, 2))], axis=0)

    def forward_z(table):
        return jnp.asarray(np.concatenate([twice(table[:, :nz]), twice(table[:, nz:])], axis=0))

    def inverse_z(table):
        return jnp.asarray(np.concatenate([stack3(table[:, :nz], 0), stack3(table[:, nz:], 0)], axis=0))

    fy = jnp.asarray(twice(y_table(ny)))
    ty = jnp.asarray(stack3(y_table(ny)[: 2 * MODES].T, 1))
    tz_first = forward_z(z_table(nz, 1.0, 1.0))
    tz_grad = forward_z(z_table(nz, inv_scale, 2.0))
    tzi_out = inverse_z(z_table(nz, inv_scale, 2.0))
    tzi_grad = inverse_z(z_table(nz, fwd_scale, 1.0))
    fx = x_forward_table(nx, fwd_scale)
    fx_wide = jnp.asarray(np.repeat(stack3(fx, 0), channels, axis=1))
    gx = jnp.asarray(stack3(by_low(x_forward_table(nx, 1.0), 1).T, 1))
    inv = x_inverse_table(nx)
    inv_low = jnp.asarray(stack3(by_low(inv, 1), 1))
    by_plane = inv.reshape(2, devices, slab, 2 * KX).transpose(0, 2, 1, 3).reshape(2 * nx, 2 * KX)
    inv_wide = np.concatenate(halves(by_plane), axis=0).reshape(4 * nx, 2, KX).transpose(2, 1, 0)
    inv_wide = jnp.asarray(np.repeat(inv_wide.reshape(2 * KX, 4 * nx), channels // 2, axis=0))

    line_shape = jax.ShapeDtypeStruct((rows, 128), f32)
    field_shape = pltpu.HBM(flow_field.shape, f32)
    mode_scratch = pltpu.VMEM((SLOTS, nz), f32)
    kron_scratch = pltpu.VMEM((16 * channels, 8 * channels), bf16)
    chunk_count = slab * (channels // 8)
    chunk_sems = pltpu.SemaphoreType.DMA((chunk_count,))
    pair_sems = pltpu.SemaphoreType.DMA((2,))
    cell_sems = pltpu.SemaphoreType.DMA((slab * (ny // 32),))

    def exchange(lines_out):
        blocks = lines_out.reshape(devices, -1, 128)
        return lax.all_to_all(blocks, "space", split_axis=0, concat_axis=0, tiled=True)

    first = pl.pallas_call(
        functools.partial(first_kernel, stride, ky_own),
        in_specs=[HBM, HBM, HBM],
        out_specs=VM,
        out_shape=line_shape,
        scratch_shapes=[
            pltpu.VMEM(flow_field.shape, f32),
            keep(fy),
            keep(tz_first),
            mode_scratch,
            chunk_sems,
            pair_sems,
        ],
        compiler_params=params(16),
        cost_estimate=cost(4),
        name="field_forward",
    )(far(flow_field), far(fy), far(tz_first))
    spec_x = exchange(first).reshape(rows, 128)

    bias = pointwise_bias.reshape(1, channels)
    pointwise = pl.pallas_call(
        point_kernel,
        in_specs=[HBM, VM, VM],
        out_specs=HBM,
        out_shape=field_shape,
        scratch_shapes=[
            keep(flow_field),
            kron_scratch,
            pltpu.VMEM((8 * channels, 2 * nz), f32),
            cell_sems,
            cell_sems,
        ],
        compiler_params=params(16),
        cost_estimate=cost(6),
        name="pointwise",
    )(far(flow_field), point_weight, bias)

    spec_x, pointwise = lax.optimization_barrier((spec_x, pointwise))
    mixed = pl.pallas_call(
        functools.partial(mix_kernel, nx, lines),
        in_specs=[VM, HBM, HBM, HBM],
        out_specs=VM,
        out_shape=line_shape,
        scratch_shapes=[
            keep(spec_weight),
            keep(fx_wide),
            keep(inv_low),
            pltpu.VMEM((32 * pair_local, 6 * nx), bf16),
            pltpu.VMEM((32 * pair_local, 512), f32),
            pltpu.VMEM((128 * pair_local, 128), f32),
            pltpu.SemaphoreType.DMA((10,)),
        ],
        compiler_params=params(24),
        cost_estimate=cost(5),
        name="mode_mix",
    )(spec_x, far(spec_weight), far(fx_wide), far(inv_low))
    mixed = exchange(mixed).reshape(rows, 128)

    output, gpre, grad_lines = pl.pallas_call(
        functools.partial(middle_kernel, stride, ky_own),
        in_specs=[VM] * 7,
        out_specs=[HBM, HBM, VM],
        out_shape=[field_shape, field_shape, line_shape],
        scratch_shapes=[
            pltpu.VMEM(flow_field.shape, f32),
            pltpu.VMEM(flow_field.shape, f32),
            mode_scratch,
            pltpu.SemaphoreType.DMA((2, slab, channels // 8)),
        ],
        compiler_params=params(24),
        cost_estimate=cost(10),
        name="middle",
    )(mixed, near(pointwise), near(cotangent), near(tzi_out), near(ty), near(fy), near(tz_grad))
    grad_x = exchange(grad_lines).reshape(rows, 128)

    local_sums, back = pl.pallas_call(
        outer_kernel,
        in_specs=[HBM, HBM, VM],
        out_specs=[VM, HBM],
        out_shape=[jax.ShapeDtypeStruct((extra, 128), f32), field_shape],
        scratch_shapes=[
            keep(flow_field),
            keep(flow_field),
            kron_scratch,
            pltpu.VMEM((8 * channels, 8 * channels), f32),
            cell_sems,
            cell_sems,
            cell_sems,
        ],
        compiler_params=params(16),
        cost_estimate=cost(8),
        name="outer_and_back",
    )(far(flow_field), far(gpre), point_weight)

    sent = devices * (block + extra)
    grad_mixed = pl.pallas_call(
        functools.partial(adjoint_kernel, slab, nx, lines, extra),
        in_specs=[VM, HBM, HBM, HBM, VM],
        out_specs=VM,
        out_shape=jax.ShapeDtypeStruct((sent, 128), f32),
        scratch_shapes=[
            keep(spec_weight),
            keep(gx),
            keep(inv_wide),
            pltpu.VMEM((16 * pair_local, 128), f32),
            pltpu.VMEM((16 * pair_local, 512), bf16),
            pltpu.VMEM((16 * pair_local, 512), bf16),
            pltpu.VMEM((32 * pair_local, 4 * nx), f32),
            pltpu.SemaphoreType.DMA((10,)),
        ],
        compiler_params=params(24),
        cost_estimate=cost(6),
        name="mode_adjoint",
    )(grad_x, far(spec_weight), far(gx), far(inv_wide), local_sums)
    grad_spec = pl.pallas_call(
        functools.partial(weight_grad_kernel, nx, lines),
        in_specs=[VM, VM, HBM, HBM],
        out_specs=HBM,
        out_shape=pltpu.HBM(spec_weight.shape, f32),
        scratch_shapes=[
            keep(fx_wide),
            keep(gx),
            pltpu.VMEM((32 * pair_local, 6 * nx), bf16),
            pltpu.VMEM((32 * pair_local, 512), f32),
            pltpu.VMEM((16 * pair_local, 128), f32),
            pltpu.VMEM((4, pair_local, 2, channels, wide // 4), f32),
            pltpu.SemaphoreType.DMA((4,)),
            pair_sems,
        ],
        compiler_params=params(24),
        cost_estimate=cost(6),
        name="weight_grad",
    )(spec_x, grad_x, far(fx_wide), far(gx))

    received = exchange(grad_mixed)

    if pair_local >= MODES:
        lines_in = sums_in = received.reshape(sent, 128)
        stride_in, sums_at = stride + extra, (stride + extra, stride)
    else:
        lines_in = received[:, :block].reshape(rows, 128)
        sums_in = received[:, block:].reshape(devices * extra, 128)
        stride_in, sums_at = stride, (extra, 0)
    grad_field, grad_point, grad_bias = pl.pallas_call(
        functools.partial(
            last_kernel, stride_in, ky_own, devices, sums_at, (fwd_scale, fwd_scale / inv_scale)
        ),
        in_specs=[VM, VM, HBM, HBM, HBM],
        out_specs=[HBM, VM, VM],
        out_shape=[
            field_shape,
            jax.ShapeDtypeStruct((channels, channels), f32),
            jax.ShapeDtypeStruct((1, channels), f32),
        ],
        scratch_shapes=[
            mode_scratch,
            pltpu.VMEM(flow_field.shape, f32),
            keep(tzi_grad),
            keep(ty),
            chunk_sems,
            chunk_sems,
            pair_sems,
        ],
        compiler_params=params(16),
        cost_estimate=cost(8),
        name="field_inverse",
    )(lines_in, sums_in, far(back), far(tzi_grad), far(ty))

    return output, grad_field, grad_spec, grad_point, grad_bias.reshape(channels)


def solution(mesh):
    cells = P(("group", "space"), None, None, None)
    return jax.shard_map(
        per_device,
        mesh=mesh,
        in_specs=(cells, cells, P("space", None, None, None), P(), P()),
        out_specs=(cells, cells, cells, P("group", None), P("group")),
        check_vma=False,
    )
```

```python
import functools
import math

import jax
import jax.numpy as jnp
import ml_dtypes
import numpy as np
from jax import lax
from jax.experimental import pallas as pl
from jax.experimental.pallas import tpu as pltpu
from jax.sharding import PartitionSpec as P

MODES = 16
KY = 2 * MODES
KX = 2 * MODES
MIB = 1024 * 1024
NT = (((1,), (1,)), ((), ()))
TN = (((0,), (0,)), ((), ()))
f32 = jnp.float32
bf16 = jnp.bfloat16


def signed(n):
    j = np.arange(n)
    return np.where(j < n // 2, j, j - n)


def phases(positions, waves, length):
    angle = ((positions[:, None] * waves[None, :]) % length) * (2.0 * math.pi / length)
    return np.cos(angle), np.sin(angle)


def halves(table):
    table = np.asarray(table, np.float32)
    high = table.astype(ml_dtypes.bfloat16)
    low = (table - high.astype(np.float32)).astype(ml_dtypes.bfloat16)
    return high, low


def stack3(table, axis):
    high, low = halves(table)
    return np.concatenate([high, high, low], axis=axis)


def y_table(ny):
    cos, sin = phases(np.arange(ny), np.arange(MODES + 1), ny)
    order = [MODES] + list(range(1, MODES))
    return np.concatenate([cos.T[:MODES], -sin.T[order], cos.T[MODES:], np.zeros((7, ny))], axis=0)


def z_table(nz, scale, factor):
    cos, sin = phases(np.arange(nz), np.arange(MODES), nz)
    weight = scale * np.where(np.arange(MODES) == 0, 1.0, factor)
    cos, sin = cos.T * weight[:, None], sin.T * weight[:, None]
    real = np.concatenate([cos, sin], axis=1)
    imag = np.concatenate([-sin, cos], axis=1)
    both = np.stack([real, imag], axis=1).reshape(4, 4, 2, 2 * nz)
    return both.transpose(1, 0, 2, 3).reshape(2 * MODES, 2 * nz)


def x_forward_table(nx, scale):
    cos, sin = phases(np.arange(nx), signed(KX), nx)
    top = np.concatenate([cos, -sin], axis=1)
    bottom = np.concatenate([sin, cos], axis=1)
    return scale * np.concatenate([top, bottom], axis=0)


def x_inverse_table(nx):
    cos, sin = phases(np.arange(nx), signed(KX), nx)
    top = np.concatenate([cos, -sin], axis=1)
    bottom = np.concatenate([sin, cos], axis=1)
    return np.concatenate([top, bottom], axis=0)


def by_low(table, axis):
    order = np.arange(2 * KX).reshape(2, KX // 4, 4).transpose(0, 2, 1).reshape(-1)
    return np.take(table, order, axis=axis)


def split(values):
    high = values.astype(bf16)
    low = (values - high.astype(f32)).astype(bf16)
    return high, low


def data3(values):
    high, low = split(values)
    return jnp.concatenate([high, low, high], axis=0)


def dot(left, right, dims=(((1,), (0,)), ((), ()))):
    return lax.dot_general(left, right, dims, preferred_element_type=f32)


def group_transpose(tiles):
    group = lax.broadcasted_iota(jnp.int32, tiles[0].shape, 1) // 32
    result = []
    for m in range(4):
        moved = [pltpu.roll(tiles[n], ((n - m) * 32) % 128, 1) if n != m else tiles[n] for n in range(4)]
        low = jnp.where(group == 0, moved[0], moved[1])
        high = jnp.where(group == 2, moved[2], moved[3])
        result.append(jnp.where(group < 2, low, high))
    return result


def block_row(ky, plane, stride, ky_own):
    return (ky // ky_own) * stride + (plane * ky_own + ky % ky_own) * 8


COS16 = MODES * 32
SINES = COS16 + 128
SLOTS = SINES + MODES * 32


def forward_pair(c, channels, pair, fy_ref, scratch):
    nz = scratch.shape[1]
    high, low = split(pair)
    both = dot(fy_ref[...], jnp.concatenate([high, low], axis=0))
    half = both[: 2 * MODES + 8] + both[2 * MODES + 8 :]
    for e in range(2):
        side = slice(e * nz, (e + 1) * nz)
        scratch[pl.ds(c + e, MODES, stride=channels), :] = half[:MODES, side]
        scratch[pl.ds(SINES + c + e, MODES, stride=channels), :] = half[MODES : 2 * MODES, side]
        scratch[pl.ds(COS16 + c + e, 1), :] = half[2 * MODES : 2 * MODES + 1, side]


def forward_finish(channels, tz_ref, scratch, out_ref, row_of):
    count = 2 * MODES
    sides = []
    for part, rows in ((0, slice(0, SINES)), (1, slice(SINES, SLOTS))):
        both = dot(tz_ref[2 * part * count : 2 * (part + 1) * count, :], jnp.concatenate(split(scratch[rows, :]), axis=1), NT)
        sides.append(both[:count] + both[count:])
    first = lax.broadcasted_iota(jnp.int32, (8, 128), 1) < 32
    for q in range(MODES // 4):
        tiles = ([], [])
        for j in range(4):
            rows, cols = slice(8 * j, 8 * j + 8), slice(q * 128, (q + 1) * 128)
            even, odd = sides[0][rows, cols], sides[1][rows, cols]
            last = sides[0][rows, COS16 : COS16 + 128]
            tiles[0].append(jnp.where(first, even, even + odd) if q == 0 else even + odd)
            tiles[1].append((jnp.where(first, last, even) if q == 0 else even) - odd)
        for sign in range(2):
            for e, tile in enumerate(group_transpose(tiles[sign])):
                k = 4 * q + e
                ky = k if sign == 0 else (KY - k if k else MODES)
                out_ref[pl.ds(row_of(ky), 8), :] = tile


def inverse_plane(in_ref, row_of, tz_ref, ty_ref, scratch, channels, emit, after, before=lambda h: None):
    nz = scratch.shape[1]
    tile = lambda ky: in_ref[pl.ds(row_of(ky), 8), :]
    columns = ([[] for _ in range(4)], [[] for _ in range(4)])
    for q in range(MODES // 4):
        sums, differences = [], []
        for k in range(4 * q, 4 * q + 4):
            sums.append(tile(k) + tile(KY - k) if k else tile(0))
            differences.append(tile(k) - tile(KY - k) if k else -tile(MODES))
        for sign, tiles in ((0, sums), (1, differences)):
            for j, found in enumerate(group_transpose(tiles)):
                columns[sign][j].append(found)
    for j, found in enumerate(group_transpose([tile(MODES)] * 4)):
        columns[0][j].append(found)
    depth = tz_ref.shape[0] // 2
    for sign, rows in ((0, slice(0, SINES)), (1, slice(SINES, SLOTS))):
        data = jnp.concatenate([jnp.concatenate(c, axis=1) for c in columns[sign]], axis=0)
        scratch[rows, :] = dot(data3(data), tz_ref[sign * depth : (sign + 1) * depth, :], TN)
    at = lax.broadcasted_iota(jnp.int32, (8, 2 * nz), 0)
    slant = jnp.where((at == 3) | (at == 5) | (at == 4), -1.0, 1.0) * jnp.where(at % 2 == 1, math.sqrt(0.5), 1.0)
    wave = jnp.where(at % 4 == 2, 0.0, slant)

    def group(h, carry):
        before(h)
        for k in range(0, 16, 2):
            c = 16 * h + k
            sides, tops = [], []
            for e in range(2):
                parts = [scratch[pl.ds(first + c + e, MODES, stride=channels), :] for first in (0, SINES)]
                sides.append(jnp.concatenate(parts, axis=0))
                tops.append(scratch[pl.ds(COS16 + c + e, 1), :])
            pair = dot(ty_ref[...], data3(jnp.concatenate(sides, axis=1)))
            extra = wave * jnp.concatenate(tops, axis=1)
            emit(c, pair + jnp.concatenate([extra] * (pair.shape[0] // 8), axis=0))
        after(h)
        return carry

    lax.fori_loop(0, channels // 16, group, 0)


def two(ref, p, c):
    return jnp.concatenate([ref[p, c], ref[p, c + 1]], axis=1)


def put_two(ref, p, c, values):
    nz = values.shape[1] // 2
    ref[p, c], ref[p, c + 1] = values[:, :nz], values[:, nz:]


def spread_weight(weight, kron_ref):
    size = weight.shape[0]
    row = lax.broadcasted_iota(jnp.int32, (8 * size, size), 0) // 8
    column = lax.broadcasted_iota(jnp.int32, (8 * size, size), 1)
    expand = (row == column).astype(f32)
    tall = lax.dot_general(
        expand, weight, (((1,), (0,)), ((), ())), precision=lax.Precision.HIGHEST, preferred_element_type=f32
    )
    wide = lax.dot_general(tall, expand, NT, precision=lax.Precision.HIGHEST, preferred_element_type=f32)
    row = lax.broadcasted_iota(jnp.int32, wide.shape, 0) % 8
    column = lax.broadcasted_iota(jnp.int32, wide.shape, 1) % 8
    kron_ref[...] = jnp.concatenate(split(jnp.where(row == column, wide, 0.0)), axis=0)


def cell_tile(ref, plane, start):
    sides = []
    for e in range(2):
        piece = ref[plane, :, pl.ds(start + 8 * e, 8), :]
        sides.append(piece.reshape(piece.shape[0] * 8, piece.shape[2]))
    return jnp.concatenate(sides, axis=1)


def put_tile(ref, plane, start, tile):
    channels, nz = ref.shape[1], ref.shape[3]
    for e in range(2):
        ref[plane, :, pl.ds(start + 8 * e, 8), :] = tile[:, e * nz : (e + 1) * nz].reshape(channels, 8, nz)


def mix_cells(kron_ref, high, low):
    size = high.shape[0]
    both = dot(kron_ref[...], high)
    return both[:size] + both[size:] + dot(kron_ref[:size, :], low)


def rows_at(plane, stride, ky_own):
    def row_of(ky):
        row = block_row(ky, plane, stride, ky_own)
        return row if isinstance(row, int) else pl.multiple_of(row, 8)

    return row_of


def transfers(pairs, sems):
    return [pltpu.make_async_copy(src, dst, sems.at[i]) for i, (src, dst) in enumerate(pairs)]


def chunks(channels):
    return [slice(8 * g, 8 * g + 8) for g in range(channels // 8)]


def first_kernel(stride, ky_own, field_hbm, fy_hbm, tz_hbm, out_ref, field_ref, fy_ref, tz_ref, scratch, sems, table_sems):
    slab, channels = field_ref.shape[:2]
    tables = transfers([(fy_hbm, fy_ref), (tz_hbm, tz_ref)], table_sems)
    parts = [(field_hbm.at[p, c], field_ref.at[p, c]) for p in range(slab) for c in chunks(channels)]
    loads = transfers(parts, sems)
    for copy in tables[:1] + loads[:2] + tables[1:] + loads[2:]:
        copy.start()
    tables[0].wait()

    def body(p, carry):
        for c in range(0, channels, 2):
            if c % 16 == 0:
                for g in (c // 8, c // 8 + 1):
                    part = slice(8 * g, 8 * g + 8)
                    sem = sems.at[p * (channels // 8) + g]
                    pltpu.make_async_copy(field_hbm.at[p, part], field_ref.at[p, part], sem).wait()
            forward_pair(c, channels, two(field_ref, p, c), fy_ref, scratch)

        @pl.when(p == 0)
        def _():
            tables[1].wait()

        forward_finish(channels, tz_ref, scratch, out_ref, rows_at(p, stride, ky_own))
        return carry

    lax.fori_loop(0, slab, body, 0)


def cell_copies(array_hbm, array_ref, sems, store=False):
    cuts = array_ref.shape[2] // 32

    def copy(n):
        at = (n // cuts, slice(None), pl.ds(32 * (n % cuts), 32))
        ends = (array_hbm.at[at], array_ref.at[at])
        return pltpu.make_async_copy(*(ends[::-1] if store else ends), sems.at[n])

    return copy, array_ref.shape[0] * cuts


def mix_field(field_hbm, out_hbm, cells_ref, kron, offset, in_sems, out_sems, prepare):
    load, count = cell_copies(field_hbm, cells_ref, in_sems)
    store, _ = cell_copies(out_hbm, cells_ref, out_sems, True)
    for n in range(count):
        load(n).start()
    prepare()
    cuts = cells_ref.shape[2] // 32

    def body(n, carry):
        load(n).wait()
        for e in range(2):
            start = pl.multiple_of(32 * (n % cuts) + 16 * e, 16)
            high, low = split(cell_tile(cells_ref, n // cuts, start))
            values = mix_cells(kron, high, low)
            put_tile(cells_ref, n // cuts, start, values if offset is None else values + offset[...])
        store(n).start()
        return carry

    lax.fori_loop(0, count, body, 0)
    for n in range(count):
        store(n).wait()


def point_kernel(field_hbm, weight_ref, bias_ref, out_hbm, cells_ref, kron, bias_wide, in_sems, out_sems):
    channels = cells_ref.shape[1]

    def prepare():
        spread_weight(jnp.transpose(weight_ref[...]), kron)
        row = lax.broadcasted_iota(jnp.int32, (8 * channels, channels), 0) // 8
        column = lax.broadcasted_iota(jnp.int32, (8 * channels, channels), 1)
        picked = jnp.where(row == column, bias_ref[...], 0.0)
        bias_wide[...] = jnp.broadcast_to(jnp.sum(picked, axis=1, keepdims=True), bias_wide.shape)

    mix_field(field_hbm, out_hbm, cells_ref, kron, bias_wide, in_sems, out_sems, prepare)


def quad_rows(ref, nx, lines, u):
    return jnp.concatenate([ref[pl.ds(2 * u + part, nx, stride=lines), :] for part in range(2)], axis=0)


def data_rows(ref, nx, lines, u):
    high, low = split(jnp.transpose(quad_rows(ref, nx, lines, u)))
    return jnp.concatenate([high, low, high], axis=1)


def weight_part(ref, t, h):
    half = ref.shape[0] // 2
    start = 256 * t if isinstance(t, int) else pl.multiple_of(256 * t, 256)
    return ref.at[half * h : half * (h + 1), :, :, pl.ds(start, 256)]


def weight_loads(weight_hbm, weight_ref, tables, sems):
    parts = [(weight_part(weight_hbm, t, h), weight_part(weight_ref, t, h)) for t in range(4) for h in range(2)]
    copies = transfers(tables + parts, sems)
    for copy in copies[:1] + copies[2:3] + copies[1:2] + copies[3:]:
        copy.start()
    return copies[:2], copies[2:]


def mix_kernel(
    nx, lines, in_ref, weight_hbm, fx_hbm, inv_hbm, out_ref, weight_ref, fx_ref, inv_ref, left, modes, sums, sems
):
    pairs = weight_ref.shape[0]
    wide = KX * 32
    tables, loads = weight_loads(weight_hbm, weight_ref, [(fx_hbm, fx_ref), (inv_hbm, inv_ref)], sems)
    for u in range(pairs // 4):
        left[128 * u : 128 * u + 128, :] = data_rows(in_ref, nx, lines, u)
    tables[0].wait()
    for t in range(4):
        cols = slice(256 * t, 256 * t + 256)
        late = slice(wide + 256 * t, wide + 256 * t + 256)
        modes[:, :256] = dot(left[...], fx_ref[:, cols])
        modes[:, 256:] = dot(left[...], fx_ref[:, late])

        def body(pair, carry):
            rows = pl.ds(pl.multiple_of(32 * pair, 32), 32)
            real, imag = modes[rows, :256], modes[rows, 256:]
            w_real, w_imag = weight_ref[pair, 0, :, cols], weight_ref[pair, 1, :, cols]
            products = (real * w_real - imag * w_imag, imag * w_real + real * w_imag)
            for part in range(2):
                total = jnp.sum(products[part].reshape(4, 8, 256), axis=0)
                for e in range(2):
                    base = pl.multiple_of((2 * pair + part) * 64 + 8 * (2 * t + e), 8)
                    sums[pl.ds(base, 8), :] = total[:, 128 * e : 128 * e + 128]
            return carry

        for h in range(2):
            loads[2 * t + h].wait()
            lax.fori_loop(h * (pairs // 2), (h + 1) * (pairs // 2), body, 0, unroll=min(8, pairs // 2))
    tables[1].wait()
    for u in range(pairs // 4):
        tiles = [[], []]
        for j in range(4):
            for part in range(2):
                base = (2 * (4 * u + j) + part) * 64
                found = [sums[pl.ds(base + s, 8, stride=8), :] for s in range(8)]
                while len(found) > 1:
                    found = [found[k] + found[k + 1] for k in range(0, len(found), 2)]
                tiles[part].append(found[0])
        mixed = jnp.concatenate(group_transpose(tiles[0]) + group_transpose(tiles[1]), axis=0)
        planes = dot(inv_ref[...], data3(mixed))
        for part in range(2):
            out_ref[pl.ds(2 * u + part, nx, stride=lines), :] = planes[part * nx : (part + 1) * nx]


def gradient_tiles(grad_ref, gx_ref, nx, lines, u):
    grads = dot(gx_ref[...], data3(quad_rows(grad_ref, nx, lines, u)))
    tiles = []
    for part in range(2):
        tiles.append(group_transpose([grads[part * 32 + 8 * b : part * 32 + 8 * b + 8, :] for b in range(4)]))
    return tiles, grads


def gradient_rows(grad_ref, gx_ref, nx, lines, quads, rows_ref):
    bias = None
    for u in range(quads):
        tiles, grads = gradient_tiles(grad_ref, gx_ref, nx, lines, u)
        bias = grads[0:1, :] if u == 0 else bias
        for part in range(2):
            for j in range(4):
                base = (2 * (4 * u + j) + part) * 8
                rows_ref[base : base + 8, :] = tiles[part][j]
    return bias


def weight_grad_kernel(
    nx, lines, in_ref, grad_ref, fx_hbm, gx_hbm, out_hbm, fx_ref, gx_ref, left, modes, rows_ref, grads_ref, sems, table_sems
):
    pairs = grads_ref.shape[1]
    wide = KX * 32
    tables = transfers([(gx_hbm, gx_ref), (fx_hbm, fx_ref)], table_sems)
    for copy in tables:
        copy.start()
    for u in range(pairs // 4):
        left[128 * u : 128 * u + 128, :] = data_rows(in_ref, nx, lines, u)
    for copy in tables:
        copy.wait()
    gradient_rows(grad_ref, gx_ref, nx, lines, pairs // 4, rows_ref)
    parts = [(grads_ref.at[t], out_hbm.at[:, :, :, pl.ds(256 * t, 256)]) for t in range(4)]
    stores = transfers(parts, sems)
    for t in range(4):
        modes[:, :256] = dot(left[...], fx_ref[:, 256 * t : 256 * t + 256])
        modes[:, 256:] = dot(left[...], fx_ref[:, wide + 256 * t : wide + 256 * t + 256])

        def body(pair, carry):
            rows = pl.ds(pl.multiple_of(32 * pair, 32), 32)
            for e in range(2):
                g_real, g_imag = [
                    jnp.broadcast_to(rows_ref[pl.ds((2 * pair + part) * 8 + 2 * t + e, 1), :], (32, 128))
                    for part in range(2)
                ]
                cols = slice(128 * e, 128 * e + 128)
                real, imag = modes[rows, cols], modes[rows, 256 + 128 * e : 384 + 128 * e]
                grads_ref[t, pair, 0, :, cols] = real * g_real + imag * g_imag
                grads_ref[t, pair, 1, :, cols] = real * g_imag - imag * g_real
            return carry

        lax.fori_loop(0, pairs, body, 0, unroll=4)
        stores[t].start()
    for copy in stores:
        copy.wait()


def adjoint_kernel(
    slab,
    nx,
    lines,
    extra,
    grad_ref,
    weight_hbm,
    gx_hbm,
    inv_hbm,
    sums_ref,
    out_ref,
    weight_ref,
    gx_ref,
    inv_ref,
    rows_ref,
    soon,
    late,
    total,
    sems,
):
    pairs = weight_ref.shape[0]
    devices = nx // slab
    stride = slab * lines + extra
    tables, loads = weight_loads(weight_hbm, weight_ref, [(gx_hbm, gx_ref), (inv_hbm, inv_ref)], sems)
    tables[0].wait()
    bias = gradient_rows(grad_ref, gx_ref, nx, lines, pairs // 4, rows_ref)
    total[...] = jnp.zeros_like(total)
    late[...] = jnp.zeros_like(late)
    tables[1].wait()
    early = lax.broadcasted_iota(jnp.int32, (32, 128), 1) % 32 < 16
    count = pairs // 2

    def arrive(t, h):
        ends = (weight_part(weight_hbm, t, h), weight_part(weight_ref, t, h))
        pltpu.make_async_copy(*ends, sems.at[2 + 2 * t + h]).wait()

    def products(t, first, target):
        for k in range(count):
            pair = first + k
            for e in range(2):
                cols = pl.ds(pl.multiple_of(256 * t + 128 * e, 128), 128)
                g_real, g_imag = [
                    jnp.broadcast_to(rows_ref[pl.ds((2 * pair + part) * 8 + 2 * t + e, 1), :], (32, 128))
                    for part in range(2)
                ]
                w_real, w_imag = weight_ref[pair, 0, :, cols], weight_ref[pair, 1, :, cols]
                real = g_real * w_real + g_imag * w_imag
                imag = g_imag * w_real - g_real * w_imag
                folded = jnp.where(early, real + pltpu.roll(real, 112, 1), imag + pltpu.roll(imag, 16, 1))
                high, low = split(folded)
                target[32 * k : 32 * k + 32, 128 * e : 128 * e + 128] = high
                target[32 * k : 32 * k + 32, 256 + 128 * e : 384 + 128 * e] = low

    def gather(t, source, first):
        table = inv_ref[pl.ds(pl.multiple_of(256 * t, 256), 256), :]
        rows = slice(32 * first, 32 * (first + count))
        total[rows, :] += dot(source[:, :256], table) + dot(source[:, 256:], table)

    def body(t, carry):
        arrive(t, 0)
        gather(jnp.maximum(t - 1, 0), late, count)
        products(t, 0, soon)
        arrive(t, 1)
        gather(t, soon, 0)
        products(t, count, late)
        return carry

    lax.fori_loop(0, 4, body, 0)
    gather(3, late, count)
    lane = lax.broadcasted_iota(jnp.int32, (nx, 128), 1)
    carried = lax.axis_index("space") == 0
    for u in range(pairs // 4):
        both = total[128 * u : 128 * u + 128, :]
        planes = jnp.transpose(both[:, : 2 * nx] + both[:, 2 * nx :])
        real, imag = planes[:nx], planes[nx:]
        if u == 0:
            imag = jnp.where((lane < 32) & carried, jnp.broadcast_to(bias, (nx, 128)), imag)
        for part, values in ((0, real), (1, imag)):
            for p in range(slab):
                out_ref[pl.ds(p * lines + 2 * u + part, devices, stride=stride), :] = values[
                    p * devices : (p + 1) * devices
                ]
    for d in range(devices):
        out_ref[d * stride + slab * lines : d * stride + slab * lines + extra, :] = sums_ref[...]


def middle_kernel(
    stride,
    ky_own,
    in_ref,
    point_ref,
    cot_ref,
    tzi_ref,
    ty_ref,
    fy_ref,
    tzf_ref,
    output_hbm,
    gpre_hbm,
    spec_ref,
    output_ref,
    gpre_ref,
    scratch,
    sems,
):
    slab, channels = point_ref.shape[:2]
    rate = math.sqrt(2.0 / math.pi)

    def stores(p, g):
        part = pl.ds(8 * g, 8)
        pairs = ((output_ref, output_hbm), (gpre_ref, gpre_hbm))
        return [
            pltpu.make_async_copy(src.at[p, part], dst.at[p, part], sems.at[k, p, g])
            for k, (src, dst) in enumerate(pairs)
        ]

    def body(p, carry):
        row_of = rows_at(p, stride, ky_own)

        def emit(c, spectral):
            values = spectral + two(point_ref, p, c)
            square = values * values
            half = 0.5 + 0.5 * jnp.tanh(values * (rate + (0.044715 * rate) * square))
            result = values * half
            put_two(output_ref, p, c, result)
            slope = half + result * (1.0 - half) * (2.0 * rate + (6 * 0.044715 * rate) * square)
            put_two(gpre_ref, p, c, two(cot_ref, p, c) * slope)

        def after(h):
            for g in range(2):
                for copy in stores(p, 2 * h + g):
                    copy.start()

        inverse_plane(in_ref, row_of, tzi_ref, ty_ref, scratch, channels, emit, after)

        def pair(k, carry):
            forward_pair(2 * k, channels, two(gpre_ref, p, 2 * k), fy_ref, scratch)
            return carry

        lax.fori_loop(0, channels // 2, pair, 0, unroll=16)
        forward_finish(channels, tzf_ref, scratch, spec_ref, row_of)
        return carry

    lax.fori_loop(0, slab, body, 0)
    for p in range(slab):
        for g in range(channels // 8):
            for copy in stores(p, g):
                copy.wait()


def outer_kernel(
    field_hbm, gpre_hbm, weight_ref, sums_ref, back_hbm, field_ref, gpre_ref, kron, outer, field_sems, gpre_sems, out_sems
):
    channels = field_ref.shape[1]
    load, count = cell_copies(field_hbm, field_ref, field_sems)
    load_gpre, _ = cell_copies(gpre_hbm, gpre_ref, gpre_sems)
    store, _ = cell_copies(back_hbm, gpre_ref, out_sems, True)
    for n in range(count):
        load(n).start()
        load_gpre(n).start()
    outer[...] = jnp.zeros_like(outer)
    spread_weight(weight_ref[...], kron)
    cuts = field_ref.shape[2] // 32

    def body(n, carry):
        load(n).wait()
        load_gpre(n).wait()
        total = outer[...]
        for e in range(2):
            start = pl.multiple_of(32 * (n % cuts) + 16 * e, 16)
            high, low = split(cell_tile(field_ref, n // cuts, start))
            g_high, g_low = split(cell_tile(gpre_ref, n // cuts, start))
            both = dot(jnp.concatenate([high, low], axis=0), g_high, NT)
            total = total + (both[: 8 * channels] + both[8 * channels :] + dot(high, g_low, NT))
            put_tile(gpre_ref, n // cuts, start, mix_cells(kron, g_high, g_low))
        outer[...] = total
        store(n).start()
        return carry

    lax.fori_loop(0, count, body, 0)
    for n in range(count):
        store(n).wait()
    row = lax.broadcasted_iota(jnp.int32, outer.shape, 0) % 8
    column = lax.broadcasted_iota(jnp.int32, outer.shape, 1) % 8
    kept = jnp.where(row == column, outer[...], 0.0)
    kept = jnp.sum(kept.reshape(channels, 8, 8 * channels), axis=1)
    row = lax.broadcasted_iota(jnp.int32, (8 * channels, channels), 0) // 8
    column = lax.broadcasted_iota(jnp.int32, (8 * channels, channels), 1)
    pick = (row == column).astype(f32)
    small = lax.dot_general(
        kept, pick, (((1,), (0,)), ((), ())), precision=lax.Precision.HIGHEST, preferred_element_type=f32
    )
    sums_ref[...] = jnp.concatenate([small[8 * g : 8 * g + 8] for g in range(4)], axis=1)


def last_kernel(
    stride,
    ky_own,
    devices,
    sums_at,
    scales,
    in_ref,
    part_ref,
    back_hbm,
    tzi_hbm,
    ty_hbm,
    out_hbm,
    point_ref,
    bias_ref,
    scratch,
    cells_ref,
    tzi_ref,
    ty_ref,
    in_sems,
    out_sems,
    table_sems,
):
    slab, channels = cells_ref.shape[:2]
    groups = channels // 8
    places = [(p, c) for p in range(slab) for c in chunks(channels)]
    tables = transfers([(tzi_hbm, tzi_ref), (ty_hbm, ty_ref)], table_sems)
    loads = transfers([(back_hbm.at[at], cells_ref.at[at]) for at in places], in_sems)
    stores = transfers([(cells_ref.at[at], out_hbm.at[at]) for at in places], out_sems)

    def one(p, g, store):
        at = (p, pl.ds(8 * g, 8))
        if store:
            return pltpu.make_async_copy(cells_ref.at[at], out_hbm.at[at], out_sems.at[p * groups + g])
        return pltpu.make_async_copy(back_hbm.at[at], cells_ref.at[at], in_sems.at[p * groups + g])

    for copy in tables + loads:
        copy.start()
    step, first = sums_at
    total = part_ref[first : first + 8, :]
    for d in range(1, devices):
        total = total + part_ref[d * step + first : d * step + first + 8, :]
    for g in range(4):
        point_ref[8 * g : 8 * g + 8, :] = total[:, 32 * g : 32 * g + 32] * scales[0]
    bias_ref[...] = in_ref[1:2, 0:32] * scales[1]
    for copy in tables:
        copy.wait()

    def body(p, carry):
        def before(h):
            one(p, 2 * h, False).wait()
            one(p, 2 * h + 1, False).wait()

        def emit(c, values):
            put_two(cells_ref, p, c, two(cells_ref, p, c) + values)

        def after(h):
            one(p, 2 * h, True).start()
            one(p, 2 * h + 1, True).start()

        inverse_plane(
            in_ref, rows_at(p, stride, ky_own), tzi_ref, ty_ref, scratch, channels, emit, after, before
        )
        return carry

    lax.fori_loop(0, slab, body, 0)
    for copy in stores:
        copy.wait()


VM = pl.BlockSpec(memory_space=pltpu.VMEM)
HBM = pl.BlockSpec(memory_space=pltpu.HBM)


def params(megabytes):
    return pltpu.CompilerParams(vmem_limit_bytes=megabytes * MIB)


def cost(microseconds):
    return pl.CostEstimate(flops=0, bytes_accessed=int(microseconds * 3e6), transcendentals=0)


def keep(array):
    return pltpu.VMEM(array.shape, array.dtype)


def far(array):
    return pltpu.with_memory_space_constraint(array, pltpu.HBM)


def near(array):
    return pltpu.with_memory_space_constraint(array, pltpu.VMEM)


def per_device(flow_field, cotangent, spec_weight, point_weight, pointwise_bias):
    slab, channels, ny, nz = flow_field.shape
    devices = lax.axis_size("space")
    nx = slab * devices
    pair_local = spec_weight.shape[0]
    assert pair_local % MODES == 0 or slab == 1
    assert channels == 32 and ny == nz == 128 and pair_local % 4 == 0
    ky_own = max(1, pair_local // MODES)
    lines = pair_local // 2
    rows = nx * lines
    block = slab * lines
    stride = slab * ky_own * 8
    extra = 8
    wide = KX * channels
    fwd_scale = float(nx * ny * nz) ** (-0.5)
    inv_scale = float(4 * MODES**3) ** (-0.5)

    def twice(table):
        high, low = halves(table)
        return np.concatenate([np.tile(high, (1, 2)), np.tile(low, (1, 2))], axis=0)

    def forward_z(table):
        return jnp.asarray(np.concatenate([twice(table[:, :nz]), twice(table[:, nz:])], axis=0))

    def inverse_z(table):
        return jnp.asarray(np.concatenate([stack3(table[:, :nz], 0), stack3(table[:, nz:], 0)], axis=0))

    fy = jnp.asarray(twice(y_table(ny)))
    ty = jnp.asarray(stack3(y_table(ny)[: 2 * MODES].T, 1))
    tz_first = forward_z(z_table(nz, 1.0, 1.0))
    tz_grad = forward_z(z_table(nz, inv_scale, 2.0))
    tzi_out = inverse_z(z_table(nz, inv_scale, 2.0))
    tzi_grad = inverse_z(z_table(nz, fwd_scale, 1.0))
    fx = x_forward_table(nx, fwd_scale)
    fx_wide = jnp.asarray(np.repeat(stack3(fx, 0), channels, axis=1))
    gx = jnp.asarray(stack3(by_low(x_forward_table(nx, 1.0), 1).T, 1))
    inv = x_inverse_table(nx)
    inv_low = jnp.asarray(stack3(by_low(inv, 1), 1))
    by_plane = inv.reshape(2, devices, slab, 2 * KX).transpose(0, 2, 1, 3).reshape(2 * nx, 2 * KX)
    inv_wide = np.concatenate(halves(by_plane), axis=0).reshape(4 * nx, 2, KX).transpose(2, 1, 0)
    inv_wide = jnp.asarray(np.repeat(inv_wide.reshape(2 * KX, 4 * nx), channels // 2, axis=0))

    line_shape = jax.ShapeDtypeStruct((rows, 128), f32)
    field_shape = pltpu.HBM(flow_field.shape, f32)
    mode_scratch = pltpu.VMEM((SLOTS, nz), f32)
    kron_scratch = pltpu.VMEM((16 * channels, 8 * channels), bf16)
    chunk_count = slab * (channels // 8)
    chunk_sems = pltpu.SemaphoreType.DMA((chunk_count,))
    pair_sems = pltpu.SemaphoreType.DMA((2,))
    cell_sems = pltpu.SemaphoreType.DMA((slab * (ny // 32),))

    def exchange(lines_out):
        blocks = lines_out.reshape(devices, -1, 128)
        return lax.all_to_all(blocks, "space", split_axis=0, concat_axis=0, tiled=True)

    first = pl.pallas_call(
        functools.partial(first_kernel, stride, ky_own),
        in_specs=[HBM, HBM, HBM],
        out_specs=VM,
        out_shape=line_shape,
        scratch_shapes=[
            pltpu.VMEM(flow_field.shape, f32),
            keep(fy),
            keep(tz_first),
            mode_scratch,
            chunk_sems,
            pair_sems,
        ],
        compiler_params=params(16),
        cost_estimate=cost(4),
        name="field_forward",
    )(far(flow_field), far(fy), far(tz_first))
    spec_x = exchange(first).reshape(rows, 128)

    bias = pointwise_bias.reshape(1, channels)
    pointwise = pl.pallas_call(
        point_kernel,
        in_specs=[HBM, VM, VM],
        out_specs=HBM,
        out_shape=field_shape,
        scratch_shapes=[
            keep(flow_field),
            kron_scratch,
            pltpu.VMEM((8 * channels, 2 * nz), f32),
            cell_sems,
            cell_sems,
        ],
        compiler_params=params(16),
        cost_estimate=cost(6),
        name="pointwise",
    )(far(flow_field), point_weight, bias)

    spec_x, pointwise = lax.optimization_barrier((spec_x, pointwise))
    mixed = pl.pallas_call(
        functools.partial(mix_kernel, nx, lines),
        in_specs=[VM, HBM, HBM, HBM],
        out_specs=VM,
        out_shape=line_shape,
        scratch_shapes=[
            keep(spec_weight),
            keep(fx_wide),
            keep(inv_low),
            pltpu.VMEM((32 * pair_local, 6 * nx), bf16),
            pltpu.VMEM((32 * pair_local, 512), f32),
            pltpu.VMEM((128 * pair_local, 128), f32),
            pltpu.SemaphoreType.DMA((10,)),
        ],
        compiler_params=params(24),
        cost_estimate=cost(5),
        name="mode_mix",
    )(spec_x, far(spec_weight), far(fx_wide), far(inv_low))
    mixed = exchange(mixed).reshape(rows, 128)

    output, gpre, grad_lines = pl.pallas_call(
        functools.partial(middle_kernel, stride, ky_own),
        in_specs=[VM] * 7,
        out_specs=[HBM, HBM, VM],
        out_shape=[field_shape, field_shape, line_shape],
        scratch_shapes=[
            pltpu.VMEM(flow_field.shape, f32),
            pltpu.VMEM(flow_field.shape, f32),
            mode_scratch,
            pltpu.SemaphoreType.DMA((2, slab, channels // 8)),
        ],
        compiler_params=params(24),
        cost_estimate=cost(10),
        name="middle",
    )(mixed, near(pointwise), near(cotangent), near(tzi_out), near(ty), near(fy), near(tz_grad))
    grad_x = exchange(grad_lines).reshape(rows, 128)

    local_sums, back = pl.pallas_call(
        outer_kernel,
        in_specs=[HBM, HBM, VM],
        out_specs=[VM, HBM],
        out_shape=[jax.ShapeDtypeStruct((extra, 128), f32), field_shape],
        scratch_shapes=[
            keep(flow_field),
            keep(flow_field),
            kron_scratch,
            pltpu.VMEM((8 * channels, 8 * channels), f32),
            cell_sems,
            cell_sems,
            cell_sems,
        ],
        compiler_params=params(16),
        cost_estimate=cost(8),
        name="outer_and_back",
    )(far(flow_field), far(gpre), point_weight)

    sent = devices * (block + extra)
    grad_mixed = pl.pallas_call(
        functools.partial(adjoint_kernel, slab, nx, lines, extra),
        in_specs=[VM, HBM, HBM, HBM, VM],
        out_specs=VM,
        out_shape=jax.ShapeDtypeStruct((sent, 128), f32),
        scratch_shapes=[
            keep(spec_weight),
            keep(gx),
            keep(inv_wide),
            pltpu.VMEM((16 * pair_local, 128), f32),
            pltpu.VMEM((16 * pair_local, 512), bf16),
            pltpu.VMEM((16 * pair_local, 512), bf16),
            pltpu.VMEM((32 * pair_local, 4 * nx), f32),
            pltpu.SemaphoreType.DMA((10,)),
        ],
        compiler_params=params(24),
        cost_estimate=cost(6),
        name="mode_adjoint",
    )(grad_x, far(spec_weight), far(gx), far(inv_wide), local_sums)
    grad_spec = pl.pallas_call(
        functools.partial(weight_grad_kernel, nx, lines),
        in_specs=[VM, VM, HBM, HBM],
        out_specs=HBM,
        out_shape=pltpu.HBM(spec_weight.shape, f32),
        scratch_shapes=[
            keep(fx_wide),
            keep(gx),
            pltpu.VMEM((32 * pair_local, 6 * nx), bf16),
            pltpu.VMEM((32 * pair_local, 512), f32),
            pltpu.VMEM((16 * pair_local, 128), f32),
            pltpu.VMEM((4, pair_local, 2, channels, wide // 4), f32),
            pltpu.SemaphoreType.DMA((4,)),
            pair_sems,
        ],
        compiler_params=params(24),
        cost_estimate=cost(6),
        name="weight_grad",
    )(spec_x, grad_x, far(fx_wide), far(gx))

    received = exchange(grad_mixed)

    if pair_local >= MODES:
        lines_in = sums_in = received.reshape(sent, 128)
        stride_in, sums_at = stride + extra, (stride + extra, stride)
    else:
        lines_in = received[:, :block].reshape(rows, 128)
        sums_in = received[:, block:].reshape(devices * extra, 128)
        stride_in, sums_at = stride, (extra, 0)
    grad_field, grad_point, grad_bias = pl.pallas_call(
        functools.partial(
            last_kernel, stride_in, ky_own, devices, sums_at, (fwd_scale, fwd_scale / inv_scale)
        ),
        in_specs=[VM, VM, HBM, HBM, HBM],
        out_specs=[HBM, VM, VM],
        out_shape=[
            field_shape,
            jax.ShapeDtypeStruct((channels, channels), f32),
            jax.ShapeDtypeStruct((1, channels), f32),
        ],
        scratch_shapes=[
            mode_scratch,
            pltpu.VMEM(flow_field.shape, f32),
            keep(tzi_grad),
            keep(ty),
            chunk_sems,
            chunk_sems,
            pair_sems,
        ],
        compiler_params=params(16),
        cost_estimate=cost(8),
        name="field_inverse",
    )(lines_in, sums_in, far(back), far(tzi_grad), far(ty))

    return output, grad_field, grad_spec, grad_point, grad_bias.reshape(channels)


def solution(mesh):
    cells = P(("group", "space"), None, None, None)
    return jax.shard_map(
        per_device,
        mesh=mesh,
        in_specs=(cells, cells, P("space", None, None, None), P(), P()),
        out_specs=(cells, cells, cells, P("group", None), P("group")),
        check_vma=False,
    )
```
